256 devices in a mesh: ha: 32 (over x_lo, z, core), wa: 8 (over x_hi, y).
Axes of the slice: x: 4 (x_hi: 2, x_lo: 2; x = x_hi * 2 + x_lo), y: 4, z: 8, core: 2. Of those that a mesh axis runs over, the one named last changes fastest.
Arguments:
- features: bfloat16 [256, 262144], P('ha', 'wa'), may hold values from -6 to 6
- grad_out: bfloat16 [256, 262144], P('ha', 'wa'), may hold values from -6 to 6
- dw_weight: float32 [49, 256], replicated, may hold values from -0.875 to 0.875
- dw_bias: float32 [256], replicated, may hold values from -3 to 3
- ln_gain: float32 [256], replicated, may hold values from 0.5 to 1.5
- ln_bias: float32 [256], replicated, may hold values from -3 to 3
- w_in: bfloat16 [256, 1024], replicated, may hold values from -0.375 to 0.375
- b_in: float32 [1024], replicated, may hold values from -3 to 3
- w_out: bfloat16 [1024, 256], replicated, may hold values from -0.1875 to 0.1875
- b_out: float32 [256], replicated, may hold values from -3 to 3
- scale: float32 [256], replicated, may hold values from 0.3 to 1.5
Outputs:
- grad_features: bfloat16 [256, 262144], P('ha', 'wa')
- clip_dw_weight: float32 [49, 256], replicated
- clip_dw_bias: float32 [256], replicated
- clip_ln_gain: float32 [256], replicated
- clip_ln_bias: float32 [256], replicated
- clip_w_in: float32 [256, 1024], replicated
- clip_b_in: float32 [1024], replicated
- clip_w_out: float32 [1024, 256], replicated
- clip_b_out: float32 [256], replicated
- clip_scale: float32 [256], replicated
The draws below stay inside these ranges and needn't reach their ends.
All inputs are finite; a program needn't handle non-finite values.
Results may differ from the reference program's by a relative error of at most 0.0075.
Values may be sent and summed in bfloat16 or wider, within the bound.
No kernel may reach another device: no remote copies, remote signals or barrier semaphores. Data moves between devices by JAX's collectives and lax.ppermute only.
A program may use at most 64 MiB of HBM per device.

```python
import math
import jax
import jax.numpy as jnp
from jax import lax

C = 256
HID = 1024
K = 7
ROWS_DEV = 8
HEIGHT = 256
WIDTH = 1024


def block_levels(stream_key, shape, split, low, largest):
    factor_of = 1.0
    for axis_at, blocks in split:
        draws = jax.random.uniform(jax.random.fold_in(jax.random.fold_in(stream_key, 6), axis_at), (blocks,), jnp.float32, low / len(split), largest / len(split))
        factor_of = factor_of * jnp.repeat(jnp.exp(draws), shape[axis_at] // blocks).reshape((-1,) + (1,) * (len(shape) - 1 - axis_at))
    return factor_of


def gaussian(key, extent, scale, bound, cuts=(), kind=jnp.bfloat16):
    values = jax.random.normal(key, extent, jnp.float32) * scale
    if len(cuts) > 0:
        values = block_levels(key, extent, cuts, -0.22, 0.18) * values
    return jnp.clip(values, min=-bound, max=bound).astype(kind)


def setup_inputs(seed: int = 0) -> dict:
    key_list = jax.random.split(jax.random.key(seed), 12)
    features = gaussian(key_list[0], (HEIGHT, WIDTH * C), 1.0, 6.0, ((0, 32), (1, 8)))
    grad_out = gaussian(key_list[1], (HEIGHT, WIDTH * C), 1.0, 6.0, ((0, 32), (1, 8)))
    dw_weight = gaussian(key_list[2], (K * K, C), (K * K) ** -0.5, 0.875, (), jnp.float32)
    dw_bias = gaussian(key_list[3], (C,), 0.5, 3.0, (), jnp.float32)
    ln_gain = jnp.clip(1.0 + 0.1 * jax.random.normal(key_list[4], (C,), jnp.float32), 0.5, 1.5)
    ln_bias = gaussian(key_list[5], (C,), 0.5, 3.0, (), jnp.float32)
    w_in = gaussian(key_list[6], (C, HID), C ** -0.5, 0.375)
    b_in = gaussian(key_list[7], (HID,), 0.5, 3.0, (), jnp.float32)
    w_out = gaussian(key_list[8], (HID, C), HID ** -0.5, 0.1875)
    b_out = gaussian(key_list[9], (C,), 0.5, 3.0, (), jnp.float32)
    scale = jnp.clip(jnp.exp(jax.random.uniform(key_list[10], (C,), jnp.float32, math.log(0.3), math.log(1.5))), 0.3, 1.5)
    return {"features": features, "grad_out": grad_out, "dw_weight": dw_weight, "dw_bias": dw_bias, "ln_gain": ln_gain, "ln_bias": ln_bias, "w_in": w_in, "b_in": b_in, "w_out": w_out, "b_out": b_out, "scale": scale}


eps_norm = 1e-06
clip_bound = 500.0

def gelu_parts(pre):
    cdf = 0.5 * (1.0 + jax.scipy.special.erf(pre / math.sqrt(2.0)))
    pdf = jnp.exp(-0.5 * pre * pre) / math.sqrt(2.0 * math.pi)
    return (pre * cdf, cdf + pre * pdf)

def conv_rows(padded, weight, rows, cols, flip):
    total = jnp.zeros((rows, cols, padded.shape[2]), jnp.float32)
    for first in range(7):
        for second in range(7):
            if flip:
                window = padded[6 - first:6 - first + rows, 6 - second:6 - second + cols]
            else:
                window = padded[first:first + rows, second:second + cols]
            total = total + window.astype(jnp.float32) * weight[first * 7 + second]
    return total

def contract_rows(left, right):
    return lax.dot_general(left, right, (((0,), (0,)), ((), ())), preferred_element_type=jnp.float32)

def block_backward(padded, grad, dw_weight, dw_bias, ln_gain, ln_bias, w_in, b_in, w_out, b_out, scale):
    rows, cols, chans = grad.shape
    conv = conv_rows(padded, dw_weight, rows, cols, False) + dw_bias
    center = conv - lax.optimization_barrier(jnp.mean(conv, axis=-1, keepdims=True))
    inverse = lax.rsqrt(lax.optimization_barrier(jnp.mean(center * center, axis=-1, keepdims=True)) + eps_norm)
    normed = (center * inverse).reshape(rows * cols, chans)
    inverse = inverse.reshape(rows * cols, 1)
    lnout = (normed * ln_gain + ln_bias).astype(jnp.bfloat16)
    pre = jnp.dot(lnout, w_in, preferred_element_type=jnp.float32) + b_in
    act_full, slope = gelu_parts(pre)
    act = act_full.astype(jnp.bfloat16)
    branch = jnp.dot(act, w_out, preferred_element_type=jnp.float32) + b_out
    gflat = grad.reshape(rows * cols, chans).astype(jnp.float32)
    g_scale = lax.optimization_barrier(jnp.sum(gflat * branch, axis=0))
    dbranch = (gflat * scale).astype(jnp.bfloat16)
    g_wout = contract_rows(act, dbranch)
    g_bout = lax.optimization_barrier(jnp.sum(dbranch.astype(jnp.float32), axis=0))
    dact = lax.dot_general(dbranch, w_out, (((1,), (1,)), ((), ())), preferred_element_type=jnp.float32)
    dpre = (dact * slope).astype(jnp.bfloat16)
    g_win_t = contract_rows(dpre, lnout)
    g_bin = lax.optimization_barrier(jnp.sum(dpre.astype(jnp.float32), axis=0))
    dln = lax.dot_general(dpre, w_in, (((1,), (1,)), ((), ())), preferred_element_type=jnp.float32)
    g_gain = lax.optimization_barrier(jnp.sum(dln * normed, axis=0))
    g_lnb = lax.optimization_barrier(jnp.sum(dln, axis=0))
    dnorm = dln * ln_gain
    dconv_flat = (dnorm - lax.optimization_barrier(jnp.mean(dnorm, axis=-1, keepdims=True)) - normed * lax.optimization_barrier(jnp.mean(dnorm * normed, axis=-1, keepdims=True))) * inverse
    dconv = dconv_flat.astype(jnp.bfloat16).reshape(rows, cols, chans)
    dconv_wide = dconv.astype(jnp.float32)
    g_dwb = lax.optimization_barrier(jnp.sum(dconv_wide, axis=(0, 1)))
    kernel_terms = []
    for first in range(7):
        for second in range(7):
            window = padded[first:first + rows, second:second + cols].astype(jnp.float32)
            kernel_terms.append(lax.optimization_barrier(jnp.sum(dconv_wide * window, axis=(0, 1))))
    g_dw = jnp.stack(kernel_terms)
    return (dconv, (g_dw, g_dwb, g_gain, g_lnb, g_win_t, g_bin, g_wout, g_bout, g_scale))

def reference(features, grad_out, dw_weight, dw_bias, ln_gain, ln_bias, w_in, b_in, w_out, b_out, scale):
    height = features.shape[0]
    width = features.shape[1] // C
    image = features.reshape(height, width, C)
    grads3 = grad_out.reshape(height, width, C)
    padded = jnp.pad(image, ((3, 3), (3, 3), (0, 0)))
    zeros_init = (jnp.zeros((K * K, C), jnp.float32), jnp.zeros((C,), jnp.float32), jnp.zeros((C,), jnp.float32), jnp.zeros((C,), jnp.float32), jnp.zeros((HID, C), jnp.float32), jnp.zeros((HID,), jnp.float32), jnp.zeros((HID, C), jnp.float32), jnp.zeros((C,), jnp.float32), jnp.zeros((C,), jnp.float32))

    def first_pass(carry, index):
        start = (index * ROWS_DEV).astype(jnp.int32)
        block = lax.dynamic_slice_in_dim(padded, start, ROWS_DEV + 6, 0)
        grad = lax.dynamic_slice_in_dim(grads3, start, ROWS_DEV, 0)
        dconv, terms = block_backward(block, grad, dw_weight, dw_bias, ln_gain, ln_bias, w_in, b_in, w_out, b_out, scale)
        return (tuple((a + b for a, b in zip(carry, terms))), dconv)
    totals, dconvs = lax.scan(first_pass, zeros_init, jnp.arange(height // ROWS_DEV, dtype=jnp.int32))
    dconv_all = dconvs.reshape(height, width, C)
    dpad = jnp.pad(dconv_all, ((3, 3), (3, 3), (0, 0)))

    def second_pass(carry, index):
        start = (index * ROWS_DEV).astype(jnp.int32)
        block = lax.dynamic_slice_in_dim(dpad, start, ROWS_DEV + 6, 0)
        grad = lax.dynamic_slice_in_dim(grads3, start, ROWS_DEV, 0)
        out = conv_rows(block, dw_weight, ROWS_DEV, width, True) + grad.astype(jnp.float32)
        return (carry, out.astype(jnp.bfloat16))
    unused, blocks = lax.scan(second_pass, jnp.zeros((), jnp.float32), jnp.arange(height // ROWS_DEV, dtype=jnp.int32))
    grad_features = blocks.reshape(height, width * C)
    squares = sum((jnp.sum(t * t) for t in totals))
    factor = jnp.minimum(1.0, clip_bound / jnp.sqrt(squares))
    g_dw, g_dwb, g_gain, g_lnb, g_win_t, g_bin, g_wout, g_bout, g_scale = totals
    return (grad_features, factor * g_dw, factor * g_dwb, factor * g_gain, factor * g_lnb, factor * g_win_t.T, factor * g_bin, factor * g_wout, factor * g_bout, factor * g_scale)
```

```python
import math

import jax
import jax.numpy as jnp
from jax import lax
from jax.experimental import pallas as pl
from jax.experimental.pallas import tpu as pltpu
from jax.sharding import PartitionSpec as P

eps_norm = 1e-06
clip_bound = 500.0
F32, BF16 = jnp.float32, jnp.bfloat16
ROWS, COLS, C, HID = 8, 128, 256, 1024
PIX = ROWS * COLS
WIDE = COLS + 6
JB = 8
LIMIT = 60 * 1024 * 1024


def shift_rows(own, left, right, top, bottom, tall, shifted):
    def place(j, mid, at):
        tall[j, 8:16, :] = mid.astype(F32)
        tall[j, 5:8, :] = top[:, pl.ds(at, C)].astype(F32)
        tall[j, 16:19, :] = bottom[:, pl.ds(at, C)].astype(F32)
        for a in range(7):
            shifted[a, j] = tall[j, 5 + a : 13 + a, :]

    for k in range(3):
        place(k, left[:, k * C : (k + 1) * C], k * C)
        place(COLS + 3 + k, right[:, k * C : (k + 1) * C], (COLS + 3 + k) * C)

    def step(j, carry):
        mid = own[:, pl.ds(pl.multiple_of(j * C, C), C)]
        place(j + 3, mid, pl.multiple_of((j + 3) * C, C))
        return carry

    lax.fori_loop(0, COLS, step, 0, unroll=4)


def spread_weights(w_ref, spread):
    for k in range(49):
        spread[k] = jnp.broadcast_to(w_ref[k : k + 1, :], (8, C))


def conv_block(shifted, spread, first, lane):
    lanes = slice(lane * 128, lane * 128 + 128)
    acc = [None] * JB
    for a in range(7):
        taps = [spread[a * 7 + b, :, lanes] for b in range(7)]
        for t in range(JB + 6):
            x = shifted[a, first + t, :, lanes]
            for b in range(7):
                o = t - b
                if 0 <= o < JB:
                    term = x * taps[b]
                    acc[o] = term if acc[o] is None else acc[o] + term
    return acc


def fold(x):
    return jnp.sum(x.reshape(-1, 8, C), axis=0)


def main_kernel(
    own, left, right, top, bottom, grad, dww, dwb, gain, lnb, w_in, w_in_t, b_in, w_out_t, b_out, scale,
    dconv_out, pay,
    tall, shifted, spread, conv, normed, inv, lnout, lnout_t, grad_flat, grad_t, pre, dact, act, dpre, dcw, small,
    big,
):
    shift_rows(own, left, right, top, bottom, tall, shifted)
    spread_weights(dww, spread)

    def forward(n, carry):
        first = n * JB
        for lane in range(2):
            lanes = slice(lane * 128, lane * 128 + 128)
            for o, acc in enumerate(conv_block(shifted, spread, first, lane)):
                conv[first + o, :, lanes] = acc
        block = conv[pl.ds(first, JB)].reshape(JB * 8, C) + dwb[...]
        center = block - jnp.mean(block, axis=-1, keepdims=True)
        inverse = lax.rsqrt(jnp.mean(center * center, axis=-1, keepdims=True) + eps_norm)
        norm = center * inverse
        rows = pl.ds(pl.multiple_of(first * 8, 64), JB * 8)
        normed[rows, :] = norm
        inv[rows, :] = inverse
        lnout[rows, :] = (norm * gain[...] + lnb[...]).astype(BF16)
        for o in range(JB):
            at = pl.multiple_of((first + o) * C, C)
            g = grad[:, pl.ds(at, C)].astype(F32)
            grad_flat[pl.ds(pl.multiple_of((first + o) * 8, 8), 8), :] = g
        return carry

    lax.fori_loop(0, COLS // JB, forward, 0)

    CH = 256

    def mlp(n, carry):
        s_gain, s_lnb, s_g, s_dwb = carry
        rows = pl.ds(pl.multiple_of(n * CH, CH), CH)
        ln = lnout[rows, :]
        lnout_t[n, 0:C, :] = ln.astype(F32).T.astype(BF16)
        g = grad_flat[rows, :]
        grad_t[n] = g.T.astype(BF16)
        pre[...] = jnp.dot(ln, w_in[...], preferred_element_type=F32) + b_in[...]
        dbr = (g * scale[...]).astype(BF16)
        dact[...] = jnp.dot(dbr, w_out_t[...], preferred_element_type=F32)
        s_g = s_g + fold(g)

        def gelu(m, c):
            sub = pl.ds(pl.multiple_of(m * 16, 16), 16)
            out = pl.ds(pl.multiple_of(n * CH + m * 16, 16), 16)
            for q in range(4):
                lanes = slice(q * 256, q * 256 + 256)
                v = pre[sub, lanes]
                e = jnp.exp(v * v * -0.5)
                t = 1.0 / (1.0 + (0.3275911 / math.sqrt(2.0)) * jnp.abs(v))
                poly = 0.5 * 1.061405429 * t - 0.5 * 1.453152027
                poly = poly * t + 0.5 * 1.421413741
                poly = poly * t - 0.5 * 0.284496736
                poly = poly * t + 0.5 * 0.254829592
                tail = poly * t * e
                cdf = jnp.where(v < 0.0, tail, 1.0 - tail)
                act[out, lanes] = (v * cdf).astype(BF16)
                slope = cdf + v * (e * (1.0 / math.sqrt(2.0 * math.pi)))
                dpre[out, lanes] = (dact[sub, lanes] * slope).astype(BF16)
            return c

        lax.fori_loop(0, CH // 16, gelu, 0)
        dact[:, 0:C] = jnp.dot(dpre[rows, :], w_in_t[...], preferred_element_type=F32)

        def back(m, c):
            s_gain, s_lnb, s_dwb = c
            sub = pl.ds(pl.multiple_of(m * 64, 64), 64)
            out = pl.ds(pl.multiple_of(n * CH + m * 64, 64), 64)
            dln = dact[sub, 0:C]
            norm = normed[out, :]
            prod = dln * norm
            s_gain = s_gain + fold(prod)
            s_lnb = s_lnb + fold(dln)
            dn = dln * gain[...]
            m1 = jnp.mean(dn, axis=-1, keepdims=True)
            m2 = jnp.mean(dn * norm, axis=-1, keepdims=True)
            dc = ((dn - m1 - norm * m2) * inv[out, :]).astype(BF16)
            wide = dc.astype(F32)
            s_dwb = s_dwb + fold(wide)
            wide = wide.reshape(8, 8, C)
            j0 = n * (CH // 8) + m * 8
            dcw[pl.ds(j0, 8)] = wide
            for o in range(8):
                dconv_out[:, pl.ds(pl.multiple_of((j0 + o) * C, C), C)] = wide[o].astype(BF16)
            return s_gain, s_lnb, s_dwb

        s_gain, s_lnb, s_dwb = lax.fori_loop(0, CH // 64, back, (s_gain, s_lnb, s_dwb))
        return s_gain, s_lnb, s_g, s_dwb

    for n in range(PIX // CH):
        lnout_t[n, C:, :] = jnp.ones((16, CH), BF16)
    zero = jnp.zeros((8, C), F32)
    s_gain, s_lnb, s_g, s_dwb = lax.fori_loop(0, PIX // CH, mlp, (zero, zero, zero, zero))

    small[...] = jnp.zeros_like(small)
    down = lambda v: jnp.sum(v, axis=0, keepdims=True)
    sum_g = down(s_g)
    small[49:50, :] = down(s_dwb)
    small[50:51, :] = down(s_gain)
    small[51:52, :] = down(s_lnb)
    small[52:53, :] = sum_g * scale[...]

    pay[:, :, :, C:] = jnp.zeros((2, 128, 8, 128), BF16)
    s_scale = jnp.zeros((C, 1), F32)
    for q in range(4):
        lanes = slice(q * 256, q * 256 + 256)
        total = jnp.zeros((C + 16, 256), F32)
        for n in range(PIX // CH):
            part = slice(n * CH, (n + 1) * CH)
            total = total + jnp.dot(lnout_t[n], dpre[part, lanes], preferred_element_type=F32)
        small[54 + q : 55 + q, :] = total[C : C + 1]
        pay[0, q * 32 : q * 32 + 32, :, 0:C] = total[0:C].reshape(32, 8, C).astype(BF16)
    for q in range(4):
        lanes = slice(q * 256, q * 256 + 256)
        total = jnp.zeros((C, 256), F32)
        for n in range(PIX // CH):
            part = slice(n * CH, (n + 1) * CH)
            total = total + jnp.dot(grad_t[n], act[part, lanes], preferred_element_type=F32)
        big[...] = total
        s_scale = s_scale + jnp.sum(total * w_out_t[:, lanes].astype(F32), axis=1, keepdims=True)
        pay[1, q * 32 : q * 32 + 32, :, 0:C] = (
            (total.T * scale[...]).reshape(32, 8, C).astype(BF16)
        )
    wide_scale = jnp.broadcast_to(s_scale, (C, 128)).T
    small[53:54, :] = wide_scale[0:1, :] + b_out[...] * sum_g

    for lane in range(2):
        lanes = slice(lane * 128, lane * 128 + 128)
        for group in ((0, 1), (2, 3), (4, 5), (6,)):

            def taps(n, acc, group=group, lanes=lanes):
                first = n * JB
                d = [dcw[first + o, :, lanes] for o in range(JB)]
                acc = list(acc)
                for p, a in enumerate(group):
                    for t in range(JB + 6):
                        x = shifted[a, first + t, :, lanes]
                        for b in range(7):
                            o = t - b
                            if 0 <= o < JB:
                                acc[p * 7 + b] = acc[p * 7 + b] + d[o] * x
                return tuple(acc)

            none = jnp.zeros((8, 128), F32)
            acc = lax.fori_loop(0, COLS // JB, taps, (none,) * (7 * len(group)))
            for p, a in enumerate(group):
                for b in range(7):
                    k = a * 7 + b
                    small[k : k + 1, lanes] = down(acc[p * 7 + b])

    for k in range(8):
        for lane in range(2):
            part = small[k * 8 : k * 8 + 8, lane * 128 : lane * 128 + 128]
            pay[0, k * 2 + lane, :, C:] = part.astype(BF16)


def transposed_kernel(
    own, left, right, top, bottom, grad, dww, out, tall, shifted, spread
):
    shift_rows(own, left, right, top, bottom, tall, shifted)
    spread_weights(dww, spread)

    def step(n, carry):
        first = n * JB
        for lane in range(2):
            for o, acc in enumerate(conv_block(shifted, spread, first, lane)):
                at = pl.ds(pl.multiple_of((first + o) * C + lane * 128, 128), 128)
                out[:, at] = (acc + grad[:, at].astype(F32)).astype(BF16)
        return carry

    lax.fori_loop(0, COLS // JB, step, 0)


def finish_kernel(
    core, mine, other, o_dw, o_dwb, o_gain, o_lnb, o_win, o_bin, o_wout, o_bout, o_scale, small, win, wout
):
    even = core[0] == 0
    total = jnp.zeros((8, 256), F32)
    for q in range(4):
        for part in range(4):
            at = slice(q * 32 + part * 8, q * 32 + part * 8 + 8)
            a = mine[at, :, 0:C].astype(F32)
            b = other[at, :, 0:C].astype(F32)
            first = jnp.where(even, a, b)
            second = jnp.where(even, b, a)
            total = total + jnp.sum(first * first + second * second, axis=0)
            win[part * 64 : part * 64 + 64, q * 256 : q * 256 + 256] = first.reshape(64, C)
            row = q * 256 + part * 64
            wout[row : row + 64, :] = second.reshape(64, C)
    for k in range(8):
        for lane in range(2):
            a = mine[k * 2 + lane, :, C:].astype(F32)
            b = other[k * 2 + lane, :, C:].astype(F32)
            small[k * 8 : k * 8 + 8, lane * 128 : lane * 128 + 128] = jnp.where(even, a, b)
    rest = small[...]
    total = total + jnp.sum((rest * rest).reshape(8, 8, C), axis=0)
    squares = jnp.sum(jnp.sum(total, axis=1, keepdims=True), axis=0, keepdims=True)
    factor = jnp.minimum(1.0, clip_bound / jnp.sqrt(squares))
    o_win[...] = win[...] * factor
    o_wout[...] = wout[...] * factor
    o_dw[...] = small[0:49, :] * factor
    o_dwb[...] = small[49:50, :] * factor
    o_gain[...] = small[50:51, :] * factor
    o_lnb[...] = small[51:52, :] * factor
    o_bout[...] = small[52:53, :] * factor
    o_scale[...] = small[53:54, :] * factor
    for q in range(4):
        o_bin[:, q * 256 : q * 256 + 256] = small[54 + q : 55 + q, :] * factor


PARAMS = pltpu.CompilerParams(vmem_limit_bytes=LIMIT)
CONV_SCRATCH = (
    pltpu.VMEM((WIDE, 24, C), F32),
    pltpu.VMEM((7, WIDE, 8, C), F32),
    pltpu.VMEM((49, 8, C), F32),
)


def run_main(*operands):
    return pl.pallas_call(
        main_kernel,
        out_shape=(
            jax.ShapeDtypeStruct((ROWS, COLS * C), BF16),
            jax.ShapeDtypeStruct((2, 128, 8, 384), BF16),
        ),
        scratch_shapes=CONV_SCRATCH
        + (
            pltpu.VMEM((COLS, 8, C), F32),
            pltpu.VMEM((PIX, C), F32),
            pltpu.VMEM((PIX, 1), F32),
            pltpu.VMEM((PIX, C), BF16),
            pltpu.VMEM((4, C + 16, 256), BF16),
            pltpu.VMEM((PIX, C), F32),
            pltpu.VMEM((4, C, 256), BF16),
            pltpu.VMEM((256, HID), F32),
            pltpu.VMEM((256, HID), F32),
            pltpu.VMEM((PIX, HID), BF16),
            pltpu.VMEM((PIX, HID), BF16),
            pltpu.VMEM((COLS, 8, C), F32),
            pltpu.VMEM((64, C), F32),
            pltpu.VMEM((C, 256), F32),
        ),
        compiler_params=PARAMS,
        name="block_backward",
    )(*operands)


def run_transposed(*operands):
    return pl.pallas_call(
        transposed_kernel,
        out_shape=jax.ShapeDtypeStruct((ROWS, COLS * C), BF16),
        scratch_shapes=CONV_SCRATCH,
        compiler_params=PARAMS,
        name="transposed_conv",
    )(*operands)


def run_finish(core, mine, other):
    vec = jax.ShapeDtypeStruct((1, C), F32)
    vmem = pl.BlockSpec(memory_space=pltpu.VMEM)
    return pl.pallas_call(
        finish_kernel,
        in_specs=[pl.BlockSpec(memory_space=pltpu.SMEM), vmem, vmem],
        out_shape=(
            jax.ShapeDtypeStruct((49, C), F32), vec, vec, vec, jax.ShapeDtypeStruct((C, HID), F32),
            jax.ShapeDtypeStruct((1, HID), F32), jax.ShapeDtypeStruct((HID, C), F32), vec, vec,
        ),
        scratch_shapes=(
            pltpu.VMEM((64, C), F32), pltpu.VMEM((C, HID), F32), pltpu.VMEM((HID, C), F32),
        ),
        compiler_params=PARAMS,
        name="clip",
    )(core, mine, other)


def halo(x):
    up_w = [(i, i + 1) for i in range(lax.axis_size("wa") - 1)]
    up_h = [(i, i + 1) for i in range(lax.axis_size("ha") - 1)]
    left = lax.ppermute(x[:, -3 * C :], "wa", up_w)
    right = lax.ppermute(x[:, : 3 * C], "wa", [(j, i) for i, j in up_w])
    last = jnp.concatenate([left[5:], x[5:], right[5:]], axis=1)
    lead = jnp.concatenate([left[:3], x[:3], right[:3]], axis=1)
    top = lax.ppermute(last, "ha", up_h)
    bottom = lax.ppermute(lead, "ha", [(j, i) for i, j in up_h])
    return left, right, top, bottom


def sum_over_devices(pay):
    both = ("ha", "wa")
    pairs, wide = lax.axis_size("ha") // 2, lax.axis_size("wa")
    core = lax.rem(lax.axis_index("ha"), 2)
    swap = [(i, i ^ 1) for i in range(2 * pairs)]
    groups = [[(2 * i + c) * wide + w for i in range(pairs) for w in range(wide)] for c in range(2)]

    def exchange(x):
        return lax.all_to_all(x, both, 0, 0, axis_index_groups=groups, tiled=True)

    send = lax.dynamic_index_in_dim(pay, 1 - core, 0, keepdims=False)
    keep = lax.dynamic_index_in_dim(pay, core, 0, keepdims=False)
    half = (keep.astype(F32) + lax.ppermute(send, "ha", swap).astype(F32)).astype(BF16)
    total = jnp.sum(exchange(half).astype(F32), axis=0).astype(BF16)
    mine = exchange(jnp.broadcast_to(total[None], half.shape))
    return core, mine, lax.ppermute(mine, "ha", swap)


def on_device(
    features, grad_out, dw_weight, dw_bias, ln_gain, ln_bias, w_in, b_in, w_out, b_out, scale
):
    row = lambda v: v.reshape(1, -1)
    dconv, pay = run_main(
        features, *halo(features), grad_out, dw_weight, row(dw_bias), row(ln_gain), row(ln_bias),
        w_in, w_in.T, row(b_in), w_out.T, row(b_out), row(scale),
    )
    core, mine, other = sum_over_devices(pay)
    grad_features = run_transposed(dconv, *halo(dconv), grad_out, dw_weight[::-1])
    o_dw, o_dwb, o_gain, o_lnb, o_win, o_bin, o_wout, o_bout, o_scale = run_finish(
        core.reshape(1).astype(jnp.int32), mine, other
    )
    flat = lambda v: v.reshape(-1)
    return (
        grad_features, o_dw, flat(o_dwb), flat(o_gain), flat(o_lnb), o_win, flat(o_bin), o_wout,
        flat(o_bout), flat(o_scale),
    )


def solution(mesh):
    return jax.shard_map(
        on_device,
        mesh=mesh,
        in_specs=(P("ha", "wa"), P("ha", "wa"), P(), P(), P(), P(), P(), P(), P(), P(), P()),
        out_specs=(P("ha", "wa"), P(), P(), P(), P(), P(), P(), P(), P(), P()),
        check_vma=False,
    )
```

```python
import math

import jax
import jax.numpy as jnp
from jax import lax
from jax.experimental import pallas as pl
from jax.experimental.pallas import tpu as pltpu
from jax.sharding import PartitionSpec as P

eps_norm = 1e-06
clip_bound = 500.0
F32, BF16 = jnp.float32, jnp.bfloat16
ROWS, COLS, C, HID = 8, 128, 256, 1024
PIX = ROWS * COLS
WIDE = COLS + 6
JB = 8
LIMIT = 60 * 1024 * 1024


def shift_rows(own, left, right, top, bottom, tall, shifted):
    def place(j, mid, at):
        tall[j, 8:16, :] = mid.astype(F32)
        tall[j, 5:8, :] = top[:, pl.ds(at, C)].astype(F32)
        tall[j, 16:19, :] = bottom[:, pl.ds(at, C)].astype(F32)
        for a in range(7):
            shifted[a, j] = tall[j, 5 + a : 13 + a, :]

    for k in range(3):
        place(k, left[:, k * C : (k + 1) * C], k * C)
        place(COLS + 3 + k, right[:, k * C : (k + 1) * C], (COLS + 3 + k) * C)

    def step(j, carry):
        mid = own[:, pl.ds(pl.multiple_of(j * C, C), C)]
        place(j + 3, mid, pl.multiple_of((j + 3) * C, C))
        return carry

    lax.fori_loop(0, COLS, step, 0, unroll=4)


def spread_weights(w_ref, spread):
    for k in range(49):
        spread[k] = jnp.broadcast_to(w_ref[k : k + 1, :], (8, C))


def conv_block(shifted, spread, first, lane):
    lanes = slice(lane * 128, lane * 128 + 128)
    acc = [None] * JB
    for a in range(7):
        taps = [spread[a * 7 + b, :, lanes] for b in range(7)]
        for t in range(JB + 6):
            x = shifted[a, first + t, :, lanes]
            for b in range(7):
                o = t - b
                if 0 <= o < JB:
                    term = x * taps[b]
                    acc[o] = term if acc[o] is None else acc[o] + term
    return acc


def fold(x):
    return jnp.sum(x.reshape(-1, 8, C), axis=0)


def main_kernel(
    core, own, left, right, top, bottom, grad, dww, dwb, gain, lnb, w_in, w_in_t, b_in, w_out_t, b_out, scale,
    dconv_out, keep, send,
    tall, shifted, spread, conv, normed, inv, lnout, lnout_t, grad_flat, grad_t, pre, dact, act, dpre, dcw, small,
    pay,
):
    shift_rows(own, left, right, top, bottom, tall, shifted)
    spread_weights(dww, spread)

    def forward(n, carry):
        first = n * JB
        for lane in range(2):
            lanes = slice(lane * 128, lane * 128 + 128)
            for o, acc in enumerate(conv_block(shifted, spread, first, lane)):
                conv[first + o, :, lanes] = acc
        block = conv[pl.ds(first, JB)].reshape(JB * 8, C) + dwb[...]
        center = block - jnp.mean(block, axis=-1, keepdims=True)
        inverse = lax.rsqrt(jnp.mean(center * center, axis=-1, keepdims=True) + eps_norm)
        norm = center * inverse
        rows = pl.ds(pl.multiple_of(first * 8, 64), JB * 8)
        normed[rows, :] = norm
        inv[rows, :] = inverse
        lnout[rows, :] = (norm * gain[...] + lnb[...]).astype(BF16)
        for o in range(JB):
            at = pl.multiple_of((first + o) * C, C)
            g = grad[:, pl.ds(at, C)].astype(F32)
            grad_flat[pl.ds(pl.multiple_of((first + o) * 8, 8), 8), :] = g
        return carry

    lax.fori_loop(0, COLS // JB, forward, 0)

    CH = 256

    def mlp(n, carry):
        s_gain, s_lnb, s_g, s_dwb = carry
        rows = pl.ds(pl.multiple_of(n * CH, CH), CH)
        ln = lnout[rows, :]
        lnout_t[n, 0:C, :] = ln.astype(F32).T.astype(BF16)
        g = grad_flat[rows, :]
        grad_t[n] = g.T.astype(BF16)
        pre[...] = jnp.dot(ln, w_in[...], preferred_element_type=F32) + b_in[...]
        dbr = (g * scale[...]).astype(BF16)
        dact[...] = jnp.dot(dbr, w_out_t[...], preferred_element_type=F32)
        s_g = s_g + fold(g)

        def gelu(m, c):
            sub = pl.ds(pl.multiple_of(m * 16, 16), 16)
            out = pl.ds(pl.multiple_of(n * CH + m * 16, 16), 16)
            for q in range(4):
                lanes = slice(q * 256, q * 256 + 256)
                v = pre[sub, lanes]
                e = jnp.exp(v * v * -0.5)
                t = 1.0 / (1.0 + (0.3275911 / math.sqrt(2.0)) * jnp.abs(v))
                poly = 0.5 * 1.061405429 * t - 0.5 * 1.453152027
                poly = poly * t + 0.5 * 1.421413741
                poly = poly * t - 0.5 * 0.284496736
                poly = poly * t + 0.5 * 0.254829592
                tail = poly * t * e
                cdf = jnp.where(v < 0.0, tail, 1.0 - tail)
                act[out, lanes] = (v * cdf).astype(BF16)
                slope = cdf + v * (e * (1.0 / math.sqrt(2.0 * math.pi)))
                dpre[out, lanes] = (dact[sub, lanes] * slope).astype(BF16)
            return c

        lax.fori_loop(0, CH // 16, gelu, 0)
        dact[:, 0:C] = jnp.dot(dpre[rows, :], w_in_t[...], preferred_element_type=F32)

        def back(m, c):
            s_gain, s_lnb, s_dwb = c
            sub = pl.ds(pl.multiple_of(m * 64, 64), 64)
            out = pl.ds(pl.multiple_of(n * CH + m * 64, 64), 64)
            dln = dact[sub, 0:C]
            norm = normed[out, :]
            prod = dln * norm
            s_gain = s_gain + fold(prod)
            s_lnb = s_lnb + fold(dln)
            dn = dln * gain[...]
            m1 = jnp.mean(dn, axis=-1, keepdims=True)
            m2 = jnp.mean(dn * norm, axis=-1, keepdims=True)
            dc = ((dn - m1 - norm * m2) * inv[out, :]).astype(BF16)
            wide = dc.astype(F32)
            s_dwb = s_dwb + fold(wide)
            wide = wide.reshape(8, 8, C)
            j0 = n * (CH // 8) + m * 8
            dcw[pl.ds(j0, 8)] = wide
            for o in range(8):
                dconv_out[:, pl.ds(pl.multiple_of((j0 + o) * C, C), C)] = wide[o].astype(BF16)
            return s_gain, s_lnb, s_dwb

        s_gain, s_lnb, s_dwb = lax.fori_loop(0, CH // 64, back, (s_gain, s_lnb, s_dwb))
        return s_gain, s_lnb, s_g, s_dwb

    for n in range(PIX // CH):
        lnout_t[n, C:, :] = jnp.ones((16, CH), BF16)
    zero = jnp.zeros((8, C), F32)
    s_gain, s_lnb, s_g, s_dwb = lax.fori_loop(0, PIX // CH, mlp, (zero, zero, zero, zero))

    small[...] = jnp.zeros_like(small)
    down = lambda v: jnp.sum(v, axis=0, keepdims=True)
    sum_g = down(s_g)
    small[49:50, :] = down(s_dwb)
    small[50:51, :] = down(s_gain)
    small[51:52, :] = down(s_lnb)
    small[52:53, :] = sum_g * scale[...]

    pay[:, :, :, C:] = jnp.zeros((2, 128, 8, 128), BF16)
    s_scale = jnp.zeros((C, 1), F32)
    for q in range(4):
        lanes = slice(q * 256, q * 256 + 256)
        total = jnp.zeros((C + 16, 256), F32)
        for n in range(PIX // CH):
            part = slice(n * CH, (n + 1) * CH)
            total = total + jnp.dot(lnout_t[n], dpre[part, lanes], preferred_element_type=F32)
        small[54 + q : 55 + q, :] = total[C : C + 1]
        pay[0, q * 32 : q * 32 + 32, :, 0:C] = total[0:C].reshape(32, 8, C).astype(BF16)
    for q in range(4):
        lanes = slice(q * 256, q * 256 + 256)
        total = jnp.zeros((C, 256), F32)
        for n in range(PIX // CH):
            part = slice(n * CH, (n + 1) * CH)
            total = total + jnp.dot(grad_t[n], act[part, lanes], preferred_element_type=F32)
        s_scale = s_scale + jnp.sum(total * w_out_t[:, lanes].astype(F32), axis=1, keepdims=True)
        pay[1, q * 32 : q * 32 + 32, :, 0:C] = (
            (total.T * scale[...]).reshape(32, 8, C).astype(BF16)
        )
    wide_scale = jnp.broadcast_to(s_scale, (C, 128)).T
    small[53:54, :] = wide_scale[0:1, :] + b_out[...] * sum_g

    for lane in range(2):
        lanes = slice(lane * 128, lane * 128 + 128)
        for group in ((0, 1), (2, 3), (4, 5), (6,)):

            def taps(n, acc, group=group, lanes=lanes):
                first = n * JB
                d = [dcw[first + o, :, lanes] for o in range(JB)]
                acc = list(acc)
                for p, a in enumerate(group):
                    for t in range(JB + 6):
                        x = shifted[a, first + t, :, lanes]
                        for b in range(7):
                            o = t - b
                            if 0 <= o < JB:
                                acc[p * 7 + b] = acc[p * 7 + b] + d[o] * x
                return tuple(acc)

            none = jnp.zeros((8, 128), F32)
            acc = lax.fori_loop(0, COLS // JB, taps, (none,) * (7 * len(group)))
            for p, a in enumerate(group):
                for b in range(7):
                    k = a * 7 + b
                    small[k : k + 1, lanes] = down(acc[p * 7 + b])

    for k in range(8):
        for lane in range(2):
            part = small[k * 8 : k * 8 + 8, lane * 128 : lane * 128 + 128]
            pay[0, k * 2 + lane, :, C:] = part.astype(BF16)
    keep[...] = pay[core[0]]
    send[...] = pay[1 - core[0]]


def transposed_kernel(
    own, left, right, top, bottom, grad, dww, out, tall, shifted, spread
):
    shift_rows(own, left, right, top, bottom, tall, shifted)
    spread_weights(dww, spread)

    def step(n, carry):
        first = n * JB
        for lane in range(2):
            for o, acc in enumerate(conv_block(shifted, spread, first, lane)):
                at = pl.ds(pl.multiple_of((first + o) * C + lane * 128, 128), 128)
                out[:, at] = (acc + grad[:, at].astype(F32)).astype(BF16)
        return carry

    lax.fori_loop(0, COLS // JB, step, 0)


def finish_kernel(
    core, mine, other, o_dw, o_dwb, o_gain, o_lnb, o_win, o_bin, o_wout, o_bout, o_scale, small, win, wout
):
    even = core[0] == 0
    total = jnp.zeros((8, 256), F32)
    for q in range(4):
        for part in range(4):
            at = slice(q * 32 + part * 8, q * 32 + part * 8 + 8)
            a = mine[at, :, 0:C].astype(F32)
            b = other[at, :, 0:C].astype(F32)
            first = jnp.where(even, a, b)
            second = jnp.where(even, b, a)
            total = total + jnp.sum(first * first + second * second, axis=0)
            win[part * 64 : part * 64 + 64, q * 256 : q * 256 + 256] = first.reshape(64, C)
            row = q * 256 + part * 64
            wout[row : row + 64, :] = second.reshape(64, C)
    for k in range(8):
        for lane in range(2):
            a = mine[k * 2 + lane, :, C:].astype(F32)
            b = other[k * 2 + lane, :, C:].astype(F32)
            small[k * 8 : k * 8 + 8, lane * 128 : lane * 128 + 128] = jnp.where(even, a, b)
    rest = small[...]
    total = total + jnp.sum((rest * rest).reshape(8, 8, C), axis=0)
    squares = jnp.sum(jnp.sum(total, axis=1, keepdims=True), axis=0, keepdims=True)
    factor = jnp.minimum(1.0, clip_bound / jnp.sqrt(squares))
    o_win[...] = win[...] * factor
    o_wout[...] = wout[...] * factor
    o_dw[...] = small[0:49, :] * factor
    o_dwb[...] = small[49:50, :] * factor
    o_gain[...] = small[50:51, :] * factor
    o_lnb[...] = small[51:52, :] * factor
    o_bout[...] = small[52:53, :] * factor
    o_scale[...] = small[53:54, :] * factor
    for q in range(4):
        o_bin[:, q * 256 : q * 256 + 256] = small[54 + q : 55 + q, :] * factor


PARAMS = pltpu.CompilerParams(vmem_limit_bytes=LIMIT)
CONV_SCRATCH = (
    pltpu.VMEM((WIDE, 24, C), F32),
    pltpu.VMEM((7, WIDE, 8, C), F32),
    pltpu.VMEM((49, 8, C), F32),
)


def run_main(*operands):
    return pl.pallas_call(
        main_kernel,
        out_shape=(
            jax.ShapeDtypeStruct((ROWS, COLS * C), BF16),
            jax.ShapeDtypeStruct((128, 8, 384), BF16),
            jax.ShapeDtypeStruct((128, 8, 384), BF16),
        ),
        in_specs=[pl.BlockSpec(memory_space=pltpu.SMEM)]
        + [pl.BlockSpec(memory_space=pltpu.VMEM)] * (len(operands) - 1),
        scratch_shapes=CONV_SCRATCH
        + (
            pltpu.VMEM((COLS, 8, C), F32),
            pltpu.VMEM((PIX, C), F32),
            pltpu.VMEM((PIX, 1), F32),
            pltpu.VMEM((PIX, C), BF16),
            pltpu.VMEM((4, C + 16, 256), BF16),
            pltpu.VMEM((PIX, C), F32),
            pltpu.VMEM((4, C, 256), BF16),
            pltpu.VMEM((256, HID), F32),
            pltpu.VMEM((256, HID), F32),
            pltpu.VMEM((PIX, HID), BF16),
            pltpu.VMEM((PIX, HID), BF16),
            pltpu.VMEM((COLS, 8, C), F32),
            pltpu.VMEM((64, C), F32),
            pltpu.VMEM((2, 128, 8, 384), BF16),
        ),
        compiler_params=PARAMS,
        name="block_backward",
    )(*operands)


def run_transposed(*operands):
    return pl.pallas_call(
        transposed_kernel,
        out_shape=jax.ShapeDtypeStruct((ROWS, COLS * C), BF16),
        scratch_shapes=CONV_SCRATCH,
        compiler_params=PARAMS,
        name="transposed_conv",
    )(*operands)


def run_finish(core, mine, other):
    vec = jax.ShapeDtypeStruct((1, C), F32)
    vmem = pl.BlockSpec(memory_space=pltpu.VMEM)
    return pl.pallas_call(
        finish_kernel,
        in_specs=[pl.BlockSpec(memory_space=pltpu.SMEM), vmem, vmem],
        out_shape=(
            jax.ShapeDtypeStruct((49, C), F32), vec, vec, vec, jax.ShapeDtypeStruct((C, HID), F32),
            jax.ShapeDtypeStruct((1, HID), F32), jax.ShapeDtypeStruct((HID, C), F32), vec, vec,
        ),
        scratch_shapes=(
            pltpu.VMEM((64, C), F32), pltpu.VMEM((C, HID), F32), pltpu.VMEM((HID, C), F32),
        ),
        compiler_params=PARAMS,
        name="clip",
    )(core, mine, other)


def halo(x):
    up_w = [(i, i + 1) for i in range(lax.axis_size("wa") - 1)]
    up_h = [(i, i + 1) for i in range(lax.axis_size("ha") - 1)]
    left = lax.ppermute(x[:, -3 * C :], "wa", up_w)
    right = lax.ppermute(x[:, : 3 * C], "wa", [(j, i) for i, j in up_w])
    last = jnp.concatenate([left[5:], x[5:], right[5:]], axis=1)
    lead = jnp.concatenate([left[:3], x[:3], right[:3]], axis=1)
    top = lax.ppermute(last, "ha", up_h)
    bottom = lax.ppermute(lead, "ha", [(j, i) for i, j in up_h])
    return left, right, top, bottom


def on_device(
    features, grad_out, dw_weight, dw_bias, ln_gain, ln_bias, w_in, b_in, w_out, b_out, scale
):
    row = lambda v: v.reshape(1, -1)
    both = ("ha", "wa")
    pairs, wide = lax.axis_size("ha") // 2, lax.axis_size("wa")
    core = lax.rem(lax.axis_index("ha"), 2).reshape(1).astype(jnp.int32)
    swap = [(i, i ^ 1) for i in range(2 * pairs)]
    groups = [[(2 * i + c) * wide + w for i in range(pairs) for w in range(wide)] for c in range(2)]

    def exchange(x):
        return lax.all_to_all(x, both, 0, 0, axis_index_groups=groups, tiled=True)

    dconv, keep, send = run_main(
        core, features, *halo(features), grad_out, dw_weight, row(dw_bias), row(ln_gain),
        row(ln_bias), w_in, w_in.T, row(b_in), w_out.T, row(b_out), row(scale),
    )
    half = (keep.astype(F32) + lax.ppermute(send, "ha", swap).astype(F32)).astype(BF16)
    terms = exchange(half)
    grad_features = run_transposed(dconv, *halo(dconv), grad_out, dw_weight[::-1])
    terms, grad_features = lax.optimization_barrier((terms, grad_features))
    total = jnp.sum(terms.astype(F32), axis=0).astype(BF16)
    mine = exchange(jnp.broadcast_to(total[None], half.shape))
    other = lax.ppermute(mine, "ha", swap)
    o_dw, o_dwb, o_gain, o_lnb, o_win, o_bin, o_wout, o_bout, o_scale = run_finish(
        core, mine, other
    )
    flat = lambda v: v.reshape(-1)
    return (
        grad_features, o_dw, flat(o_dwb), flat(o_gain), flat(o_lnb), o_win, flat(o_bin), o_wout,
        flat(o_bout), flat(o_scale),
    )


def solution(mesh):
    return jax.shard_map(
        on_device,
        mesh=mesh,
        in_specs=(P("ha", "wa"), P("ha", "wa"), P(), P(), P(), P(), P(), P(), P(), P(), P()),
        out_specs=(P("ha", "wa"), P(), P(), P(), P(), P(), P(), P(), P(), P()),
        check_vma=False,
    )
```

```python
import math

import jax
import jax.numpy as jnp
from jax import lax
from jax.experimental import pallas as pl
from jax.experimental.pallas import tpu as pltpu
from jax.sharding import PartitionSpec as P

eps_norm = 1e-06
clip_bound = 500.0
F32, BF16 = jnp.float32, jnp.bfloat16
ROWS, COLS, C, HID = 8, 128, 256, 1024
PIX = ROWS * COLS
WIDE = COLS + 6
JB = 8
MIB = 1024 * 1024


def shift_rows(own, left, right, top, bottom, tall, shifted):
    def place(j, mid, at):
        tall[j, 8:16, :] = mid.astype(F32)
        tall[j, 5:8, :] = top[:, pl.ds(at, C)].astype(F32)
        tall[j, 16:19, :] = bottom[:, pl.ds(at, C)].astype(F32)
        for a in range(7):
            shifted[a, j] = tall[j, 5 + a : 13 + a, :]

    for k in range(3):
        place(k, left[:, k * C : (k + 1) * C], k * C)
        place(COLS + 3 + k, right[:, k * C : (k + 1) * C], (COLS + 3 + k) * C)

    def step(j, carry):
        mid = own[:, pl.ds(pl.multiple_of(j * C, C), C)]
        place(j + 3, mid, pl.multiple_of((j + 3) * C, C))
        return carry

    lax.fori_loop(0, COLS, step, 0, unroll=4)


def spread_weights(w_ref, spread):
    for k in range(49):
        spread[k] = jnp.broadcast_to(w_ref[k : k + 1, :], (8, C))


def conv_block(shifted, spread, first, lane):
    lanes = slice(lane * 128, lane * 128 + 128)
    acc = [None] * JB
    for a in range(7):
        taps = [spread[a * 7 + b, :, lanes] for b in range(7)]
        for t in range(JB + 6):
            x = shifted[a, first + t, :, lanes]
            for b in range(7):
                o = t - b
                if 0 <= o < JB:
                    term = x * taps[b]
                    acc[o] = term if acc[o] is None else acc[o] + term
    return acc


def fold(x):
    return jnp.sum(x.reshape(-1, 8, C), axis=0)


def main_kernel(
    core, own, left, right, top, bottom, grad, dww, dwb, gain, lnb, w_in, w_in_t, b_in, w_out_t, b_out, scale,
    dconv_out, keep, send,
    tall, shifted, spread, conv, normed, inv, lnout, lnout_t, grad_flat, grad_t, pre, dact, act, dpre, dcw, small,
    pay,
):
    shift_rows(own, left, right, top, bottom, tall, shifted)
    spread_weights(dww, spread)

    def forward(n, carry):
        first = n * JB
        for lane in range(2):
            lanes = slice(lane * 128, lane * 128 + 128)
            for o, acc in enumerate(conv_block(shifted, spread, first, lane)):
                conv[first + o, :, lanes] = acc
        block = conv[pl.ds(first, JB)].reshape(JB * 8, C) + dwb[...]
        center = block - jnp.mean(block, axis=-1, keepdims=True)
        inverse = lax.rsqrt(jnp.mean(center * center, axis=-1, keepdims=True) + eps_norm)
        norm = center * inverse
        rows = pl.ds(pl.multiple_of(first * 8, 64), JB * 8)
        normed[rows, :] = norm
        inv[rows, :] = inverse
        lnout[rows, :] = (norm * gain[...] + lnb[...]).astype(BF16)
        for o in range(JB):
            at = pl.multiple_of((first + o) * C, C)
            g = grad[:, pl.ds(at, C)].astype(F32)
            grad_flat[pl.ds(pl.multiple_of((first + o) * 8, 8), 8), :] = g
        return carry

    lax.fori_loop(0, COLS // JB, forward, 0)

    CH = 256

    def mlp(n, carry):
        s_gain, s_lnb, s_g, s_dwb = carry
        rows = pl.ds(pl.multiple_of(n * CH, CH), CH)
        ln = lnout[rows, :]
        lnout_t[n, 0:C, :] = ln.astype(F32).T.astype(BF16)
        g = grad_flat[rows, :]
        grad_t[n] = g.T.astype(BF16)
        pre[...] = jnp.dot(ln, w_in[...], preferred_element_type=F32) + b_in[...]
        dbr = (g * scale[...]).astype(BF16)
        dact[...] = jnp.dot(dbr, w_out_t[...], preferred_element_type=F32)
        s_g = s_g + fold(g)

        def gelu(m, c):
            sub = pl.ds(pl.multiple_of(m * 16, 16), 16)
            out = pl.ds(pl.multiple_of(n * CH + m * 16, 16), 16)
            for q in range(4):
                lanes = slice(q * 256, q * 256 + 256)
                v = pre[sub, lanes]
                e = jnp.exp(v * v * -0.5)
                t = 1.0 / (1.0 + (0.3275911 / math.sqrt(2.0)) * jnp.abs(v))
                poly = 0.5 * 1.061405429 * t - 0.5 * 1.453152027
                poly = poly * t + 0.5 * 1.421413741
                poly = poly * t - 0.5 * 0.284496736
                poly = poly * t + 0.5 * 0.254829592
                tail = poly * t * e
                cdf = jnp.where(v < 0.0, tail, 1.0 - tail)
                act[out, lanes] = (v * cdf).astype(BF16)
                slope = cdf + v * (e * (1.0 / math.sqrt(2.0 * math.pi)))
                dpre[out, lanes] = (dact[sub, lanes] * slope).astype(BF16)
            return c

        lax.fori_loop(0, CH // 16, gelu, 0)
        dact[:, 0:C] = jnp.dot(dpre[rows, :], w_in_t[...], preferred_element_type=F32)

        def back(m, c):
            s_gain, s_lnb, s_dwb = c
            sub = pl.ds(pl.multiple_of(m * 64, 64), 64)
            out = pl.ds(pl.multiple_of(n * CH + m * 64, 64), 64)
            dln = dact[sub, 0:C]
            norm = normed[out, :]
            prod = dln * norm
            s_gain = s_gain + fold(prod)
            s_lnb = s_lnb + fold(dln)
            dn = dln * gain[...]
            m1 = jnp.mean(dn, axis=-1, keepdims=True)
            m2 = jnp.mean(dn * norm, axis=-1, keepdims=True)
            dc = ((dn - m1 - norm * m2) * inv[out, :]).astype(BF16)
            wide = dc.astype(F32)
            s_dwb = s_dwb + fold(wide)
            wide = wide.reshape(8, 8, C)
            j0 = n * (CH // 8) + m * 8
            dcw[pl.ds(j0, 8)] = wide
            for o in range(8):
                dconv_out[:, pl.ds(pl.multiple_of((j0 + o) * C, C), C)] = wide[o].astype(BF16)
            return s_gain, s_lnb, s_dwb

        s_gain, s_lnb, s_dwb = lax.fori_loop(0, CH // 64, back, (s_gain, s_lnb, s_dwb))
        return s_gain, s_lnb, s_g, s_dwb

    for n in range(PIX // CH):
        lnout_t[n, C:, :] = jnp.ones((16, CH), BF16)
    zero = jnp.zeros((8, C), F32)
    s_gain, s_lnb, s_g, s_dwb = lax.fori_loop(0, PIX // CH, mlp, (zero, zero, zero, zero))

    small[...] = jnp.zeros_like(small)
    down = lambda v: jnp.sum(v, axis=0, keepdims=True)
    sum_g = down(s_g)
    small[49:50, :] = down(s_dwb)
    small[50:51, :] = down(s_gain)
    small[51:52, :] = down(s_lnb)
    small[52:53, :] = sum_g * scale[...]

    pay[:, :, :, C:] = jnp.zeros((2, 128, 8, 128), BF16)
    s_scale = jnp.zeros((C, 1), F32)
    for q in range(4):
        lanes = slice(q * 256, q * 256 + 256)
        total = jnp.zeros((C + 16, 256), F32)
        for n in range(PIX // CH):
            part = slice(n * CH, (n + 1) * CH)
            total = total + jnp.dot(lnout_t[n], dpre[part, lanes], preferred_element_type=F32)
        small[54 + q : 55 + q, :] = total[C : C + 1]
        pay[0, q * 32 : q * 32 + 32, :, 0:C] = total[0:C].reshape(32, 8, C).astype(BF16)
    for q in range(4):
        lanes = slice(q * 256, q * 256 + 256)
        total = jnp.zeros((C, 256), F32)
        for n in range(PIX // CH):
            part = slice(n * CH, (n + 1) * CH)
            total = total + jnp.dot(grad_t[n], act[part, lanes], preferred_element_type=F32)
        s_scale = s_scale + jnp.sum(total * w_out_t[:, lanes].astype(F32), axis=1, keepdims=True)
        pay[1, q * 32 : q * 32 + 32, :, 0:C] = (
            (total.T * scale[...]).reshape(32, 8, C).astype(BF16)
        )
    wide_scale = jnp.broadcast_to(s_scale, (C, 128)).T
    small[53:54, :] = wide_scale[0:1, :] + b_out[...] * sum_g

    for lane in range(2):
        lanes = slice(lane * 128, lane * 128 + 128)
        for group in ((0, 1), (2, 3), (4, 5), (6,)):

            def taps(n, acc, group=group, lanes=lanes):
                first = n * JB
                d = [dcw[first + o, :, lanes] for o in range(JB)]
                acc = list(acc)
                for p, a in enumerate(group):
                    for t in range(JB + 6):
                        x = shifted[a, first + t, :, lanes]
                        for b in range(7):
                            o = t - b
                            if 0 <= o < JB:
                                acc[p * 7 + b] = acc[p * 7 + b] + d[o] * x
                return tuple(acc)

            none = jnp.zeros((8, 128), F32)
            acc = lax.fori_loop(0, COLS // JB, taps, (none,) * (7 * len(group)))
            for p, a in enumerate(group):
                for b in range(7):
                    k = a * 7 + b
                    small[k : k + 1, lanes] = down(acc[p * 7 + b])

    for k in range(8):
        for lane in range(2):
            part = small[k * 8 : k * 8 + 8, lane * 128 : lane * 128 + 128]
            pay[0, k * 2 + lane, :, C:] = part.astype(BF16)
    keep[...] = pay[core[0]]
    send[...] = pay[1 - core[0]]


def transposed_kernel(
    own, left, right, top, bottom, grad, dww, out, tall, shifted, spread
):
    shift_rows(own, left, right, top, bottom, tall, shifted)
    spread_weights(dww, spread)

    def step(n, carry):
        first = n * JB
        for lane in range(2):
            for o, acc in enumerate(conv_block(shifted, spread, first, lane)):
                at = pl.ds(pl.multiple_of((first + o) * C + lane * 128, 128), 128)
                out[:, at] = (acc + grad[:, at].astype(F32)).astype(BF16)
        return carry

    lax.fori_loop(0, COLS // JB, step, 0)


def finish_kernel(
    core, mine, other, o_dw, o_dwb, o_gain, o_lnb, o_win, o_bin, o_wout, o_bout, o_scale, small, win, wout
):
    even = core[0] == 0
    total = jnp.zeros((8, 256), F32)
    for q in range(4):
        for part in range(4):
            at = slice(q * 32 + part * 8, q * 32 + part * 8 + 8)
            a = mine[at, :, 0:C].astype(F32)
            b = other[at, :, 0:C].astype(F32)
            first = jnp.where(even, a, b)
            second = jnp.where(even, b, a)
            total = total + jnp.sum(first * first + second * second, axis=0)
            win[part * 64 : part * 64 + 64, q * 256 : q * 256 + 256] = first.reshape(64, C)
            row = q * 256 + part * 64
            wout[row : row + 64, :] = second.reshape(64, C)
    for k in range(8):
        for lane in range(2):
            a = mine[k * 2 + lane, :, C:].astype(F32)
            b = other[k * 2 + lane, :, C:].astype(F32)
            small[k * 8 : k * 8 + 8, lane * 128 : lane * 128 + 128] = jnp.where(even, a, b)
    rest = small[...]
    total = total + jnp.sum((rest * rest).reshape(8, 8, C), axis=0)
    squares = jnp.sum(jnp.sum(total, axis=1, keepdims=True), axis=0, keepdims=True)
    factor = jnp.minimum(1.0, clip_bound / jnp.sqrt(squares))
    o_win[...] = win[...] * factor
    o_wout[...] = wout[...] * factor
    o_dw[...] = small[0:49, :] * factor
    o_dwb[...] = small[49:50, :] * factor
    o_gain[...] = small[50:51, :] * factor
    o_lnb[...] = small[51:52, :] * factor
    o_bout[...] = small[52:53, :] * factor
    o_scale[...] = small[53:54, :] * factor
    for q in range(4):
        o_bin[:, q * 256 : q * 256 + 256] = small[54 + q : 55 + q, :] * factor


CONV_SCRATCH = (
    pltpu.VMEM((WIDE, 24, C), F32),
    pltpu.VMEM((7, WIDE, 8, C), F32),
    pltpu.VMEM((49, 8, C), F32),
)


def run_main(*operands):
    return pl.pallas_call(
        main_kernel,
        out_shape=(
            jax.ShapeDtypeStruct((ROWS, COLS * C), BF16),
            jax.ShapeDtypeStruct((128, 8, 384), BF16),
            jax.ShapeDtypeStruct((128, 8, 384), BF16),
        ),
        in_specs=[pl.BlockSpec(memory_space=pltpu.SMEM)]
        + [pl.BlockSpec(memory_space=pltpu.VMEM)] * (len(operands) - 1),
        scratch_shapes=CONV_SCRATCH
        + (
            pltpu.VMEM((COLS, 8, C), F32),
            pltpu.VMEM((PIX, C), F32),
            pltpu.VMEM((PIX, 1), F32),
            pltpu.VMEM((PIX, C), BF16),
            pltpu.VMEM((4, C + 16, 256), BF16),
            pltpu.VMEM((PIX, C), F32),
            pltpu.VMEM((4, C, 256), BF16),
            pltpu.VMEM((256, HID), F32),
            pltpu.VMEM((256, HID), F32),
            pltpu.VMEM((PIX, HID), BF16),
            pltpu.VMEM((PIX, HID), BF16),
            pltpu.VMEM((COLS, 8, C), F32),
            pltpu.VMEM((64, C), F32),
            pltpu.VMEM((2, 128, 8, 384), BF16),
        ),
        compiler_params=pltpu.CompilerParams(vmem_limit_bytes=40 * MIB),
        name="block_backward",
    )(*operands)


def run_transposed(*operands):
    return pl.pallas_call(
        transposed_kernel,
        out_shape=jax.ShapeDtypeStruct((ROWS, COLS * C), BF16),
        scratch_shapes=CONV_SCRATCH,
        compiler_params=pltpu.CompilerParams(vmem_limit_bytes=20 * MIB),
        cost_estimate=pl.CostEstimate(flops=200_000_000, bytes_accessed=40 * MIB, transcendentals=0),
        name="transposed_conv",
    )(*operands)


def run_finish(core, mine, other):
    vec = jax.ShapeDtypeStruct((1, C), F32)
    vmem = pl.BlockSpec(memory_space=pltpu.VMEM)
    return pl.pallas_call(
        finish_kernel,
        in_specs=[pl.BlockSpec(memory_space=pltpu.SMEM), vmem, vmem],
        out_shape=(
            jax.ShapeDtypeStruct((49, C), F32), vec, vec, vec, jax.ShapeDtypeStruct((C, HID), F32),
            jax.ShapeDtypeStruct((1, HID), F32), jax.ShapeDtypeStruct((HID, C), F32), vec, vec,
        ),
        scratch_shapes=(
            pltpu.VMEM((64, C), F32), pltpu.VMEM((C, HID), F32), pltpu.VMEM((HID, C), F32),
        ),
        compiler_params=pltpu.CompilerParams(vmem_limit_bytes=16 * MIB),
        name="clip",
    )(core, mine, other)


def halo(x):
    up_w = [(i, i + 1) for i in range(lax.axis_size("wa") - 1)]
    up_h = [(i, i + 1) for i in range(lax.axis_size("ha") - 1)]
    left = lax.ppermute(x[:, -3 * C :], "wa", up_w)
    right = lax.ppermute(x[:, : 3 * C], "wa", [(j, i) for i, j in up_w])
    last = jnp.concatenate([left[5:], x[5:], right[5:]], axis=1)
    lead = jnp.concatenate([left[:3], x[:3], right[:3]], axis=1)
    top = lax.ppermute(last, "ha", up_h)
    bottom = lax.ppermute(lead, "ha", [(j, i) for i, j in up_h])
    return left, right, top, bottom


def on_device(
    features, grad_out, dw_weight, dw_bias, ln_gain, ln_bias, w_in, b_in, w_out, b_out, scale
):
    row = lambda v: v.reshape(1, -1)
    both = ("ha", "wa")
    pairs, wide = lax.axis_size("ha") // 2, lax.axis_size("wa")
    core = lax.rem(lax.axis_index("ha"), 2).reshape(1).astype(jnp.int32)
    swap = [(i, i ^ 1) for i in range(2 * pairs)]
    groups = [[(2 * i + c) * wide + w for i in range(pairs) for w in range(wide)] for c in range(2)]

    def exchange(x):
        return lax.all_to_all(x, both, 0, 0, axis_index_groups=groups, tiled=True)

    dconv, keep, send = run_main(
        core, features, *halo(features), grad_out, dw_weight, row(dw_bias), row(ln_gain),
        row(ln_bias), w_in, w_in.T, row(b_in), w_out.T, row(b_out), row(scale),
    )
    half = (keep.astype(F32) + lax.ppermute(send, "ha", swap).astype(F32)).astype(BF16)
    terms = exchange(half)
    edges = halo(dconv)
    total = jnp.sum(terms.astype(F32), axis=0).astype(BF16)
    total, edges = lax.optimization_barrier((total, edges))
    mine = exchange(jnp.broadcast_to(total[None], half.shape))
    grad_features = run_transposed(dconv, *edges, grad_out, dw_weight[::-1])
    mine, grad_features = lax.optimization_barrier((mine, grad_features))
    other = lax.ppermute(mine, "ha", swap)
    o_dw, o_dwb, o_gain, o_lnb, o_win, o_bin, o_wout, o_bout, o_scale = run_finish(
        core, mine, other
    )
    flat = lambda v: v.reshape(-1)
    return (
        grad_features, o_dw, flat(o_dwb), flat(o_gain), flat(o_lnb), o_win, flat(o_bin), o_wout,
        flat(o_bout), flat(o_scale),
    )


def solution(mesh):
    return jax.shard_map(
        on_device,
        mesh=mesh,
        in_specs=(P("ha", "wa"), P("ha", "wa"), P(), P(), P(), P(), P(), P(), P(), P(), P()),
        out_specs=(P("ha", "wa"), P(), P(), P(), P(), P(), P(), P(), P(), P()),
        check_vma=False,
    )
```

```python
import math

import jax
import jax.numpy as jnp
from jax import lax
from jax.experimental import pallas as pl
from jax.experimental.pallas import tpu as pltpu
from jax.sharding import PartitionSpec as P

eps_norm = 1e-06
clip_bound = 500.0
F32, BF16 = jnp.float32, jnp.bfloat16
ROWS, COLS, C, HID = 8, 128, 256, 1024
PIX = ROWS * COLS
WIDE = COLS + 6
JB = 8
MIB = 1024 * 1024


def shift_rows(core, own, left, right, swapped, crossed, tall, shifted):
    even = core[0] == 0

    def place(j, mid, at):
        inner = swapped[:, pl.ds(at, C)].astype(F32)
        outer = crossed[:, pl.ds(at, C)].astype(F32)
        tall[j, 8:16, :] = mid.astype(F32)
        tall[j, 5:8, :] = jnp.where(even, outer, inner)
        tall[j, 16:19, :] = jnp.where(even, inner, outer)
        for a in range(7):
            shifted[a, j] = tall[j, 5 + a : 13 + a, :]

    for k in range(3):
        place(k, left[:, k * C : (k + 1) * C], k * C)
        place(COLS + 3 + k, right[:, k * C : (k + 1) * C], (COLS + 3 + k) * C)

    def step(j, carry):
        mid = own[:, pl.ds(pl.multiple_of(j * C, C), C)]
        place(j + 3, mid, pl.multiple_of((j + 3) * C, C))
        return carry

    lax.fori_loop(0, COLS, step, 0, unroll=4)


def spread_weights(w_ref, spread):
    for k in range(49):
        spread[k] = jnp.broadcast_to(w_ref[k : k + 1, :], (8, C))


def conv_block(shifted, spread, first, lane):
    lanes = slice(lane * 128, lane * 128 + 128)
    acc = [None] * JB
    for a in range(7):
        taps = [spread[a * 7 + b, :, lanes] for b in range(7)]
        for t in range(JB + 6):
            x = shifted[a, first + t, :, lanes]
            for b in range(7):
                o = t - b
                if 0 <= o < JB:
                    term = x * taps[b]
                    acc[o] = term if acc[o] is None else acc[o] + term
    return acc


def fold(x):
    return jnp.sum(x.reshape(-1, 8, C), axis=0)


def main_kernel(
    core, own, left, right, swapped, crossed, grad, dww, dwb, gain, lnb, w_in, w_in_t, b_in, w_out_t, b_out, scale,
    dconv_out, keep, send,
    tall, shifted, spread, conv, normed, inv, lnout, lnout_t, grad_flat, grad_t, pre, dact, act, dpre, dcw, small,
    pay,
):
    shift_rows(core, own, left, right, swapped, crossed, tall, shifted)
    spread_weights(dww, spread)

    def forward(n, carry):
        first = n * JB
        for lane in range(2):
            lanes = slice(lane * 128, lane * 128 + 128)
            for o, acc in enumerate(conv_block(shifted, spread, first, lane)):
                conv[first + o, :, lanes] = acc
        block = conv[pl.ds(first, JB)].reshape(JB * 8, C) + dwb[...]
        center = block - jnp.mean(block, axis=-1, keepdims=True)
        inverse = lax.rsqrt(jnp.mean(center * center, axis=-1, keepdims=True) + eps_norm)
        norm = center * inverse
        rows = pl.ds(pl.multiple_of(first * 8, 64), JB * 8)
        normed[rows, :] = norm
        inv[rows, :] = inverse
        lnout[rows, :] = (norm * gain[...] + lnb[...]).astype(BF16)
        for o in range(JB):
            at = pl.multiple_of((first + o) * C, C)
            g = grad[:, pl.ds(at, C)].astype(F32)
            grad_flat[pl.ds(pl.multiple_of((first + o) * 8, 8), 8), :] = g
        return carry

    lax.fori_loop(0, COLS // JB, forward, 0)

    CH = 256

    def mlp(n, carry):
        s_gain, s_lnb, s_g, s_dwb = carry
        rows = pl.ds(pl.multiple_of(n * CH, CH), CH)
        ln = lnout[rows, :]
        lnout_t[n, 0:C, :] = ln.astype(F32).T.astype(BF16)
        g = grad_flat[rows, :]
        grad_t[n] = g.T.astype(BF16)
        pre[...] = jnp.dot(ln, w_in[...], preferred_element_type=F32) + b_in[...]
        dbr = (g * scale[...]).astype(BF16)
        dact[...] = jnp.dot(dbr, w_out_t[...], preferred_element_type=F32)
        s_g = s_g + fold(g)

        def gelu(m, c):
            sub = pl.ds(pl.multiple_of(m * 16, 16), 16)
            out = pl.ds(pl.multiple_of(n * CH + m * 16, 16), 16)
            for q in range(4):
                lanes = slice(q * 256, q * 256 + 256)
                v = pre[sub, lanes]
                e = jnp.exp(v * v * -0.5)
                t = 1.0 / (1.0 + (0.3275911 / math.sqrt(2.0)) * jnp.abs(v))
                poly = 0.5 * 1.061405429 * t - 0.5 * 1.453152027
                poly = poly * t + 0.5 * 1.421413741
                poly = poly * t - 0.5 * 0.284496736
                poly = poly * t + 0.5 * 0.254829592
                tail = poly * t * e
                cdf = jnp.where(v < 0.0, tail, 1.0 - tail)
                act[out, lanes] = (v * cdf).astype(BF16)
                slope = cdf + v * (e * (1.0 / math.sqrt(2.0 * math.pi)))
                dpre[out, lanes] = (dact[sub, lanes] * slope).astype(BF16)
            return c

        lax.fori_loop(0, CH // 16, gelu, 0)
        dact[:, 0:C] = jnp.dot(dpre[rows, :], w_in_t[...], preferred_element_type=F32)

        def back(m, c):
            s_gain, s_lnb, s_dwb = c
            sub = pl.ds(pl.multiple_of(m * 64, 64), 64)
            out = pl.ds(pl.multiple_of(n * CH + m * 64, 64), 64)
            dln = dact[sub, 0:C]
            norm = normed[out, :]
            prod = dln * norm
            s_gain = s_gain + fold(prod)
            s_lnb = s_lnb + fold(dln)
            dn = dln * gain[...]
            m1 = jnp.mean(dn, axis=-1, keepdims=True)
            m2 = jnp.mean(dn * norm, axis=-1, keepdims=True)
            dc = ((dn - m1 - norm * m2) * inv[out, :]).astype(BF16)
            wide = dc.astype(F32)
            s_dwb = s_dwb + fold(wide)
            wide = wide.reshape(8, 8, C)
            j0 = n * (CH // 8) + m * 8
            dcw[pl.ds(j0, 8)] = wide
            for o in range(8):
                dconv_out[:, pl.ds(pl.multiple_of((j0 + o) * C, C), C)] = wide[o].astype(BF16)
            return s_gain, s_lnb, s_dwb

        s_gain, s_lnb, s_dwb = lax.fori_loop(0, CH // 64, back, (s_gain, s_lnb, s_dwb))
        return s_gain, s_lnb, s_g, s_dwb

    for n in range(PIX // CH):
        lnout_t[n, C:, :] = jnp.ones((16, CH), BF16)
    zero = jnp.zeros((8, C), F32)
    s_gain, s_lnb, s_g, s_dwb = lax.fori_loop(0, PIX // CH, mlp, (zero, zero, zero, zero))

    small[...] = jnp.zeros_like(small)
    down = lambda v: jnp.sum(v, axis=0, keepdims=True)
    sum_g = down(s_g)
    small[49:50, :] = down(s_dwb)
    small[50:51, :] = down(s_gain)
    small[51:52, :] = down(s_lnb)
    small[52:53, :] = sum_g * scale[...]

    pay[:, :, :, C:] = jnp.zeros((2, 128, 8, 128), BF16)
    s_scale = jnp.zeros((C, 1), F32)
    for q in range(4):
        lanes = slice(q * 256, q * 256 + 256)
        total = jnp.zeros((C + 16, 256), F32)
        for n in range(PIX // CH):
            part = slice(n * CH, (n + 1) * CH)
            total = total + jnp.dot(lnout_t[n], dpre[part, lanes], preferred_element_type=F32)
        small[54 + q : 55 + q, :] = total[C : C + 1]
        pay[0, q * 32 : q * 32 + 32, :, 0:C] = total[0:C].reshape(32, 8, C).astype(BF16)
    for q in range(4):
        lanes = slice(q * 256, q * 256 + 256)
        total = jnp.zeros((C, 256), F32)
        for n in range(PIX // CH):
            part = slice(n * CH, (n + 1) * CH)
            total = total + jnp.dot(grad_t[n], act[part, lanes], preferred_element_type=F32)
        s_scale = s_scale + jnp.sum(total * w_out_t[:, lanes].astype(F32), axis=1, keepdims=True)
        pay[1, q * 32 : q * 32 + 32, :, 0:C] = (
            (total.T * scale[...]).reshape(32, 8, C).astype(BF16)
        )
    wide_scale = jnp.broadcast_to(s_scale, (C, 128)).T
    small[53:54, :] = wide_scale[0:1, :] + b_out[...] * sum_g

    for lane in range(2):
        lanes = slice(lane * 128, lane * 128 + 128)
        for group in ((0, 1), (2, 3), (4, 5), (6,)):

            def taps(n, acc, group=group, lanes=lanes):
                first = n * JB
                d = [dcw[first + o, :, lanes] for o in range(JB)]
                acc = list(acc)
                for p, a in enumerate(group):
                    for t in range(JB + 6):
                        x = shifted[a, first + t, :, lanes]
                        for b in range(7):
                            o = t - b
                            if 0 <= o < JB:
                                acc[p * 7 + b] = acc[p * 7 + b] + d[o] * x
                return tuple(acc)

            none = jnp.zeros((8, 128), F32)
            acc = lax.fori_loop(0, COLS // JB, taps, (none,) * (7 * len(group)))
            for p, a in enumerate(group):
                for b in range(7):
                    k = a * 7 + b
                    small[k : k + 1, lanes] = down(acc[p * 7 + b])

    for k in range(8):
        for lane in range(2):
            part = small[k * 8 : k * 8 + 8, lane * 128 : lane * 128 + 128]
            pay[0, k * 2 + lane, :, C:] = part.astype(BF16)
    keep[...] = pay[core[0]]
    send[...] = pay[1 - core[0]]


def transposed_kernel(
    core, own, left, right, swapped, crossed, grad, dww, out, tall, shifted, spread
):
    shift_rows(core, own, left, right, swapped, crossed, tall, shifted)
    spread_weights(dww, spread)

    def step(n, carry):
        first = n * JB
        for lane in range(2):
            for o, acc in enumerate(conv_block(shifted, spread, first, lane)):
                at = pl.ds(pl.multiple_of((first + o) * C + lane * 128, 128), 128)
                out[:, at] = (acc + grad[:, at].astype(F32)).astype(BF16)
        return carry

    lax.fori_loop(0, COLS // JB, step, 0)


def finish_kernel(
    core, mine, other, o_dw, o_dwb, o_gain, o_lnb, o_win, o_bin, o_wout, o_bout, o_scale, small, win, wout
):
    even = core[0] == 0
    total = jnp.zeros((8, 256), F32)
    for q in range(4):
        for part in range(4):
            at = slice(q * 32 + part * 8, q * 32 + part * 8 + 8)
            a = mine[at, :, 0:C].astype(F32)
            b = other[at, :, 0:C].astype(F32)
            first = jnp.where(even, a, b)
            second = jnp.where(even, b, a)
            total = total + jnp.sum(first * first + second * second, axis=0)
            win[part * 64 : part * 64 + 64, q * 256 : q * 256 + 256] = first.reshape(64, C)
            row = q * 256 + part * 64
            wout[row : row + 64, :] = second.reshape(64, C)
    for k in range(8):
        for lane in range(2):
            a = mine[k * 2 + lane, :, C:].astype(F32)
            b = other[k * 2 + lane, :, C:].astype(F32)
            small[k * 8 : k * 8 + 8, lane * 128 : lane * 128 + 128] = jnp.where(even, a, b)
    rest = small[...]
    total = total + jnp.sum((rest * rest).reshape(8, 8, C), axis=0)
    squares = jnp.sum(jnp.sum(total, axis=1, keepdims=True), axis=0, keepdims=True)
    factor = jnp.minimum(1.0, clip_bound / jnp.sqrt(squares))
    o_win[...] = win[...] * factor
    o_wout[...] = wout[...] * factor
    o_dw[...] = small[0:49, :] * factor
    o_dwb[...] = small[49:50, :] * factor
    o_gain[...] = small[50:51, :] * factor
    o_lnb[...] = small[51:52, :] * factor
    o_bout[...] = small[52:53, :] * factor
    o_scale[...] = small[53:54, :] * factor
    for q in range(4):
        o_bin[:, q * 256 : q * 256 + 256] = small[54 + q : 55 + q, :] * factor


CONV_SCRATCH = (
    pltpu.VMEM((WIDE, 24, C), F32),
    pltpu.VMEM((7, WIDE, 8, C), F32),
    pltpu.VMEM((49, 8, C), F32),
)


def run_main(*operands):
    return pl.pallas_call(
        main_kernel,
        out_shape=(
            jax.ShapeDtypeStruct((ROWS, COLS * C), BF16),
            jax.ShapeDtypeStruct((128, 8, 384), BF16),
            jax.ShapeDtypeStruct((128, 8, 384), BF16),
        ),
        in_specs=[pl.BlockSpec(memory_space=pltpu.SMEM)]
        + [pl.BlockSpec(memory_space=pltpu.VMEM)] * (len(operands) - 1),
        scratch_shapes=CONV_SCRATCH
        + (
            pltpu.VMEM((COLS, 8, C), F32),
            pltpu.VMEM((PIX, C), F32),
            pltpu.VMEM((PIX, 1), F32),
            pltpu.VMEM((PIX, C), BF16),
            pltpu.VMEM((4, C + 16, 256), BF16),
            pltpu.VMEM((PIX, C), F32),
            pltpu.VMEM((4, C, 256), BF16),
            pltpu.VMEM((256, HID), F32),
            pltpu.VMEM((256, HID), F32),
            pltpu.VMEM((PIX, HID), BF16),
            pltpu.VMEM((PIX, HID), BF16),
            pltpu.VMEM((COLS, 8, C), F32),
            pltpu.VMEM((64, C), F32),
            pltpu.VMEM((2, 128, 8, 384), BF16),
        ),
        compiler_params=pltpu.CompilerParams(vmem_limit_bytes=40 * MIB),
        name="block_backward",
    )(*operands)


def run_transposed(*operands):
    return pl.pallas_call(
        transposed_kernel,
        out_shape=jax.ShapeDtypeStruct((ROWS, COLS * C), BF16),
        in_specs=[pl.BlockSpec(memory_space=pltpu.SMEM)]
        + [pl.BlockSpec(memory_space=pltpu.VMEM)] * (len(operands) - 1),
        scratch_shapes=CONV_SCRATCH,
        compiler_params=pltpu.CompilerParams(vmem_limit_bytes=20 * MIB),
        cost_estimate=pl.CostEstimate(flops=200_000_000, bytes_accessed=40 * MIB, transcendentals=0),
        name="transposed_conv",
    )(*operands)


def run_finish(core, mine, other):
    vec = jax.ShapeDtypeStruct((1, C), F32)
    vmem = pl.BlockSpec(memory_space=pltpu.VMEM)
    return pl.pallas_call(
        finish_kernel,
        in_specs=[pl.BlockSpec(memory_space=pltpu.SMEM), vmem, vmem],
        out_shape=(
            jax.ShapeDtypeStruct((49, C), F32), vec, vec, vec, jax.ShapeDtypeStruct((C, HID), F32),
            jax.ShapeDtypeStruct((1, HID), F32), jax.ShapeDtypeStruct((HID, C), F32), vec, vec,
        ),
        scratch_shapes=(
            pltpu.VMEM((64, C), F32), pltpu.VMEM((C, HID), F32), pltpu.VMEM((HID, C), F32),
        ),
        compiler_params=pltpu.CompilerParams(vmem_limit_bytes=16 * MIB),
        name="clip",
    )(core, mine, other)


def pair_swaps(n):
    inner = [(i, i ^ 1) for i in range(n)]
    outer = [(i, i + 1 if i % 2 else i - 1) for i in range(1, n - 1)]
    return inner, outer


def halo(x, core):
    inner, outer = pair_swaps(lax.axis_size("wa"))
    even = lax.rem(lax.axis_index("wa"), 2) == 0
    first, last = x[:, : 3 * C], x[:, -3 * C :]
    near = lax.ppermute(jnp.where(even, last, first), "wa", inner)
    far = lax.ppermute(jnp.where(even, first, last), "wa", outer)
    left, right = jnp.where(even, far, near), jnp.where(even, near, far)
    inner, outer = pair_swaps(lax.axis_size("ha"))
    even = core[0] == 0
    last = jnp.concatenate([left[5:], x[5:], right[5:]], axis=1)
    lead = jnp.concatenate([left[:3], x[:3], right[:3]], axis=1)
    crossed = lax.ppermute(jnp.where(even, lead, last), "ha", outer)
    swapped = lax.ppermute(jnp.where(even, last, lead), "ha", inner)
    return left, right, swapped, crossed


def plane_and_line():
    wide, pairs = lax.axis_size("wa"), lax.axis_size("ha") // 2
    depth = pairs // 2
    at = lambda x, z, c, w: ((x * depth + z) * 2 + c) * wide + w
    plane = [
        [at(x, z, c, w) for x in range(2) for w in range(wide)]
        for z in range(depth)
        for c in range(2)
    ]
    line = [
        [at(x, z, c, w) for z in range(depth)]
        for x in range(2)
        for w in range(wide)
        for c in range(2)
    ]
    return plane, line


def on_device(
    features, grad_out, dw_weight, dw_bias, ln_gain, ln_bias, w_in, b_in, w_out, b_out, scale
):
    row = lambda v: v.reshape(1, -1)
    core = lax.rem(lax.axis_index("ha"), 2).reshape(1).astype(jnp.int32)
    swap, _ = pair_swaps(lax.axis_size("ha"))
    plane, line = plane_and_line()

    def exchange(x, groups):
        return lax.all_to_all(x, ("ha", "wa"), 0, 0, axis_index_groups=groups, tiled=True)

    dconv, keep, send = run_main(
        core, features, *halo(features, core), grad_out, dw_weight, row(dw_bias), row(ln_gain),
        row(ln_bias), w_in, w_in.T, row(b_in), w_out.T, row(b_out), row(scale),
    )
    half = (keep.astype(F32) + lax.ppermute(send, "ha", swap).astype(F32)).astype(BF16)
    terms = exchange(half, plane)
    edges = halo(dconv, core)
    sums = jnp.sum(terms.reshape(len(plane[0]), -1, 8, 384).astype(F32), axis=0)
    total = jnp.sum(exchange(sums, line), axis=0).astype(BF16)
    total, edges = lax.optimization_barrier((total, edges))
    mine = exchange(jnp.broadcast_to(total[None], sums.shape), line)
    mine = jnp.broadcast_to(mine[None], (len(plane[0]),) + mine.shape).reshape(half.shape)
    mine = exchange(mine, plane)
    grad_features = run_transposed(core, dconv, *edges, grad_out, dw_weight[::-1])
    mine, grad_features = lax.optimization_barrier((mine, grad_features))
    other = lax.ppermute(mine, "ha", swap)
    o_dw, o_dwb, o_gain, o_lnb, o_win, o_bin, o_wout, o_bout, o_scale = run_finish(
        core, mine, other
    )
    flat = lambda v: v.reshape(-1)
    return (
        grad_features, o_dw, flat(o_dwb), flat(o_gain), flat(o_lnb), o_win, flat(o_bin), o_wout,
        flat(o_bout), flat(o_scale),
    )


def solution(mesh):
    return jax.shard_map(
        on_device,
        mesh=mesh,
        in_specs=(P("ha", "wa"), P("ha", "wa"), P(), P(), P(), P(), P(), P(), P(), P(), P()),
        out_specs=(P("ha", "wa"), P(), P(), P(), P(), P(), P(), P(), P(), P()),
        check_vma=False,
    )
```

```python
import math

import jax
import jax.numpy as jnp
from jax import lax
from jax.experimental import pallas as pl
from jax.experimental.pallas import tpu as pltpu
from jax.sharding import PartitionSpec as P

eps_norm = 1e-06
clip_bound = 500.0
F32, BF16 = jnp.float32, jnp.bfloat16
ROWS, COLS, C, HID = 8, 128, 256, 1024
PIX = ROWS * COLS
WIDE = COLS + 6
JB = 8
MIB = 1024 * 1024


def shift_rows(own, left, right, rows, tall, shifted):
    def place(j, mid, at):
        edge = rows[:, pl.ds(at, C)].astype(F32)
        tall[j, 8:16, :] = mid.astype(F32)
        tall[j, 5:8, :] = edge[0:3]
        tall[j, 16:19, :] = edge[3:6]
        for a in range(7):
            shifted[a, j] = tall[j, 5 + a : 13 + a, :]

    for k in range(3):
        place(k, left[:, k * C : (k + 1) * C], k * C)
        place(COLS + 3 + k, right[:, k * C : (k + 1) * C], (COLS + 3 + k) * C)

    def step(j, carry):
        mid = own[:, pl.ds(pl.multiple_of(j * C, C), C)]
        place(j + 3, mid, pl.multiple_of((j + 3) * C, C))
        return carry

    lax.fori_loop(0, COLS, step, 0, unroll=4)


def spread_weights(w_ref, spread):
    for k in range(49):
        spread[k] = jnp.broadcast_to(w_ref[k : k + 1, :], (8, C))


def conv_block(shifted, spread, first, lane):
    lanes = slice(lane * 128, lane * 128 + 128)
    acc = [None] * JB
    for a in range(7):
        taps = [spread[a * 7 + b, :, lanes] for b in range(7)]
        for t in range(JB + 6):
            x = shifted[a, first + t, :, lanes]
            for b in range(7):
                o = t - b
                if 0 <= o < JB:
                    term = x * taps[b]
                    acc[o] = term if acc[o] is None else acc[o] + term
    return acc


def fold(x):
    return jnp.sum(x.reshape(-1, 8, C), axis=0)


def main_kernel(
    core, own, left, right, rows, grad, dww, dwb, gain, lnb, w_in, w_in_t, b_in, w_out_t, b_out, scale,
    dconv_out, keep, send,
    tall, shifted, spread, conv, normed, inv, lnout, lnout_t, grad_flat, grad_t, pre, dact, act, dpre, dcw, small,
    pay,
):
    shift_rows(own, left, right, rows, tall, shifted)
    spread_weights(dww, spread)

    def forward(n, carry):
        first = n * JB
        for lane in range(2):
            lanes = slice(lane * 128, lane * 128 + 128)
            for o, acc in enumerate(conv_block(shifted, spread, first, lane)):
                conv[first + o, :, lanes] = acc
        block = conv[pl.ds(first, JB)].reshape(JB * 8, C) + dwb[...]
        center = block - jnp.mean(block, axis=-1, keepdims=True)
        inverse = lax.rsqrt(jnp.mean(center * center, axis=-1, keepdims=True) + eps_norm)
        norm = center * inverse
        rows = pl.ds(pl.multiple_of(first * 8, 64), JB * 8)
        normed[rows, :] = norm
        inv[rows, :] = inverse
        lnout[rows, :] = (norm * gain[...] + lnb[...]).astype(BF16)
        for o in range(JB):
            at = pl.multiple_of((first + o) * C, C)
            g = grad[:, pl.ds(at, C)].astype(F32)
            grad_flat[pl.ds(pl.multiple_of((first + o) * 8, 8), 8), :] = g
        return carry

    lax.fori_loop(0, COLS // JB, forward, 0)

    CH = 256

    def mlp(n, carry):
        s_gain, s_lnb, s_g, s_dwb = carry
        rows = pl.ds(pl.multiple_of(n * CH, CH), CH)
        ln = lnout[rows, :]
        lnout_t[n, 0:C, :] = ln.astype(F32).T.astype(BF16)
        g = grad_flat[rows, :]
        grad_t[n] = g.T.astype(BF16)
        pre[...] = jnp.dot(ln, w_in[...], preferred_element_type=F32) + b_in[...]
        dbr = (g * scale[...]).astype(BF16)
        dact[...] = jnp.dot(dbr, w_out_t[...], preferred_element_type=F32)
        s_g = s_g + fold(g)

        def gelu(m, c):
            sub = pl.ds(pl.multiple_of(m * 16, 16), 16)
            out = pl.ds(pl.multiple_of(n * CH + m * 16, 16), 16)
            for q in range(4):
                lanes = slice(q * 256, q * 256 + 256)
                v = pre[sub, lanes]
                e = jnp.exp2(v * v * (-0.5 / math.log(2.0)))
                d = 1.0 + (0.3275911 / math.sqrt(2.0)) * jnp.abs(v)
                t = pl.reciprocal(d, approx=True)
                t = t * (2.0 - d * t)
                poly = 0.5 * 1.061405429 * t - 0.5 * 1.453152027
                poly = poly * t + 0.5 * 1.421413741
                poly = poly * t - 0.5 * 0.284496736
                poly = poly * t + 0.5 * 0.254829592
                tail = poly * t * e
                cdf = jnp.where(v < 0.0, tail, 1.0 - tail)
                act[out, lanes] = (v * cdf).astype(BF16)
                slope = cdf + v * (e * (1.0 / math.sqrt(2.0 * math.pi)))
                dpre[out, lanes] = (dact[sub, lanes] * slope).astype(BF16)
            return c

        lax.fori_loop(0, CH // 16, gelu, 0)
        dact[:, 0:C] = jnp.dot(dpre[rows, :], w_in_t[...], preferred_element_type=F32)

        def back(m, c):
            s_gain, s_lnb, s_dwb = c
            sub = pl.ds(pl.multiple_of(m * 64, 64), 64)
            out = pl.ds(pl.multiple_of(n * CH + m * 64, 64), 64)
            dln = dact[sub, 0:C]
            norm = normed[out, :]
            prod = dln * norm
            s_gain = s_gain + fold(prod)
            s_lnb = s_lnb + fold(dln)
            dn = dln * gain[...]
            m1 = jnp.mean(dn, axis=-1, keepdims=True)
            m2 = jnp.mean(dn * norm, axis=-1, keepdims=True)
            dc = ((dn - m1 - norm * m2) * inv[out, :]).astype(BF16)
            wide = dc.astype(F32)
            s_dwb = s_dwb + fold(wide)
            wide = wide.reshape(8, 8, C)
            j0 = n * (CH // 8) + m * 8
            dcw[pl.ds(j0, 8)] = wide
            for o in range(8):
                dconv_out[:, pl.ds(pl.multiple_of((j0 + o) * C, C), C)] = wide[o].astype(BF16)
            return s_gain, s_lnb, s_dwb

        s_gain, s_lnb, s_dwb = lax.fori_loop(0, CH // 64, back, (s_gain, s_lnb, s_dwb))
        return s_gain, s_lnb, s_g, s_dwb

    for n in range(PIX // CH):
        lnout_t[n, C:, :] = jnp.ones((16, CH), BF16)
    zero = jnp.zeros((8, C), F32)
    s_gain, s_lnb, s_g, s_dwb = lax.fori_loop(0, PIX // CH, mlp, (zero, zero, zero, zero))

    small[...] = jnp.zeros_like(small)
    down = lambda v: jnp.sum(v, axis=0, keepdims=True)
    sum_g = down(s_g)
    small[49:50, :] = down(s_dwb)
    small[50:51, :] = down(s_gain)
    small[51:52, :] = down(s_lnb)
    small[52:53, :] = sum_g * scale[...]

    pay[:, :, :, C:] = jnp.zeros((2, 128, 8, 128), BF16)
    s_scale = jnp.zeros((C, 1), F32)
    for q in range(4):
        lanes = slice(q * 256, q * 256 + 256)
        total = jnp.zeros((C + 16, 256), F32)
        for n in range(PIX // CH):
            part = slice(n * CH, (n + 1) * CH)
            total = total + jnp.dot(lnout_t[n], dpre[part, lanes], preferred_element_type=F32)
        small[54 + q : 55 + q, :] = total[C : C + 1]
        pay[0, q * 32 : q * 32 + 32, :, 0:C] = total[0:C].reshape(32, 8, C).astype(BF16)
    for q in range(4):
        lanes = slice(q * 256, q * 256 + 256)
        total = jnp.zeros((C, 256), F32)
        for n in range(PIX // CH):
            part = slice(n * CH, (n + 1) * CH)
            total = total + jnp.dot(grad_t[n], act[part, lanes], preferred_element_type=F32)
        s_scale = s_scale + jnp.sum(total * w_out_t[:, lanes].astype(F32), axis=1, keepdims=True)
        pay[1, q * 32 : q * 32 + 32, :, 0:C] = (
            (total.T * scale[...]).reshape(32, 8, C).astype(BF16)
        )
    wide_scale = jnp.broadcast_to(s_scale, (C, 128)).T
    small[53:54, :] = wide_scale[0:1, :] + b_out[...] * sum_g

    for lane in range(2):
        lanes = slice(lane * 128, lane * 128 + 128)
        for group in ((0, 1), (2, 3), (4, 5), (6,)):

            def taps(n, acc, group=group, lanes=lanes):
                first = n * JB
                d = [dcw[first + o, :, lanes] for o in range(JB)]
                acc = list(acc)
                for p, a in enumerate(group):
                    for t in range(JB + 6):
                        x = shifted[a, first + t, :, lanes]
                        for b in range(7):
                            o = t - b
                            if 0 <= o < JB:
                                acc[p * 7 + b] = acc[p * 7 + b] + d[o] * x
                return tuple(acc)

            none = jnp.zeros((8, 128), F32)
            acc = lax.fori_loop(0, COLS // JB, taps, (none,) * (7 * len(group)))
            for p, a in enumerate(group):
                for b in range(7):
                    k = a * 7 + b
                    small[k : k + 1, lanes] = down(acc[p * 7 + b])

    for k in range(8):
        for lane in range(2):
            part = small[k * 8 : k * 8 + 8, lane * 128 : lane * 128 + 128]
            pay[0, k * 2 + lane, :, C:] = part.astype(BF16)
    keep[...] = pay[core[0]]
    send[...] = pay[1 - core[0]]


def transposed_kernel(
    own, left, right, rows, grad, dww, out, tall, shifted, spread
):
    shift_rows(own, left, right, rows, tall, shifted)
    spread_weights(dww, spread)

    def step(n, carry):
        first = n * JB
        for lane in range(2):
            for o, acc in enumerate(conv_block(shifted, spread, first, lane)):
                at = pl.ds(pl.multiple_of((first + o) * C + lane * 128, 128), 128)
                out[:, at] = (acc + grad[:, at].astype(F32)).astype(BF16)
        return carry

    lax.fori_loop(0, COLS // JB, step, 0)


def finish_kernel(
    core, mine, other, o_dw, o_dwb, o_gain, o_lnb, o_win, o_bin, o_wout, o_bout, o_scale, small, win, wout
):
    even = core[0] == 0
    total = jnp.zeros((8, 256), F32)
    for q in range(4):
        for part in range(4):
            at = slice(q * 32 + part * 8, q * 32 + part * 8 + 8)
            a = mine[at, :, 0:C].astype(F32)
            b = other[at, :, 0:C].astype(F32)
            first = jnp.where(even, a, b)
            second = jnp.where(even, b, a)
            total = total + jnp.sum(first * first + second * second, axis=0)
            win[part * 64 : part * 64 + 64, q * 256 : q * 256 + 256] = first.reshape(64, C)
            row = q * 256 + part * 64
            wout[row : row + 64, :] = second.reshape(64, C)
    for k in range(8):
        for lane in range(2):
            a = mine[k * 2 + lane, :, C:].astype(F32)
            b = other[k * 2 + lane, :, C:].astype(F32)
            small[k * 8 : k * 8 + 8, lane * 128 : lane * 128 + 128] = jnp.where(even, a, b)
    rest = small[...]
    total = total + jnp.sum((rest * rest).reshape(8, 8, C), axis=0)
    squares = jnp.sum(jnp.sum(total, axis=1, keepdims=True), axis=0, keepdims=True)
    factor = jnp.minimum(1.0, clip_bound / jnp.sqrt(squares))
    o_win[...] = win[...] * factor
    o_wout[...] = wout[...] * factor
    o_dw[...] = small[0:49, :] * factor
    o_dwb[...] = small[49:50, :] * factor
    o_gain[...] = small[50:51, :] * factor
    o_lnb[...] = small[51:52, :] * factor
    o_bout[...] = small[52:53, :] * factor
    o_scale[...] = small[53:54, :] * factor
    for q in range(4):
        o_bin[:, q * 256 : q * 256 + 256] = small[54 + q : 55 + q, :] * factor


CONV_SCRATCH = (
    pltpu.VMEM((WIDE, 24, C), F32),
    pltpu.VMEM((7, WIDE, 8, C), F32),
    pltpu.VMEM((49, 8, C), F32),
)


def run_main(*operands):
    return pl.pallas_call(
        main_kernel,
        out_shape=(
            jax.ShapeDtypeStruct((ROWS, COLS * C), BF16),
            jax.ShapeDtypeStruct((128, 8, 384), BF16),
            jax.ShapeDtypeStruct((128, 8, 384), BF16),
        ),
        in_specs=[pl.BlockSpec(memory_space=pltpu.SMEM)]
        + [pl.BlockSpec(memory_space=pltpu.VMEM)] * (len(operands) - 1),
        scratch_shapes=CONV_SCRATCH
        + (
            pltpu.VMEM((COLS, 8, C), F32),
            pltpu.VMEM((PIX, C), F32),
            pltpu.VMEM((PIX, 1), F32),
            pltpu.VMEM((PIX, C), BF16),
            pltpu.VMEM((4, C + 16, 256), BF16),
            pltpu.VMEM((PIX, C), F32),
            pltpu.VMEM((4, C, 256), BF16),
            pltpu.VMEM((256, HID), F32),
            pltpu.VMEM((256, HID), F32),
            pltpu.VMEM((PIX, HID), BF16),
            pltpu.VMEM((PIX, HID), BF16),
            pltpu.VMEM((COLS, 8, C), F32),
            pltpu.VMEM((64, C), F32),
            pltpu.VMEM((2, 128, 8, 384), BF16),
        ),
        compiler_params=pltpu.CompilerParams(vmem_limit_bytes=40 * MIB),
        name="block_backward",
    )(*operands)


def run_transposed(*operands):
    return pl.pallas_call(
        transposed_kernel,
        out_shape=jax.ShapeDtypeStruct((ROWS, COLS * C), BF16),
        scratch_shapes=CONV_SCRATCH,
        compiler_params=pltpu.CompilerParams(vmem_limit_bytes=20 * MIB),
        cost_estimate=pl.CostEstimate(flops=200_000_000, bytes_accessed=40 * MIB, transcendentals=0),
        name="transposed_conv",
    )(*operands)


def run_finish(core, mine, other):
    vec = jax.ShapeDtypeStruct((1, C), F32)
    vmem = pl.BlockSpec(memory_space=pltpu.VMEM)
    return pl.pallas_call(
        finish_kernel,
        in_specs=[pl.BlockSpec(memory_space=pltpu.SMEM), vmem, vmem],
        out_shape=(
            jax.ShapeDtypeStruct((49, C), F32), vec, vec, vec, jax.ShapeDtypeStruct((C, HID), F32),
            jax.ShapeDtypeStruct((1, HID), F32), jax.ShapeDtypeStruct((HID, C), F32), vec, vec,
        ),
        scratch_shapes=(
            pltpu.VMEM((64, C), F32), pltpu.VMEM((C, HID), F32), pltpu.VMEM((HID, C), F32),
        ),
        compiler_params=pltpu.CompilerParams(vmem_limit_bytes=16 * MIB),
        name="clip",
    )(core, mine, other)


def pair_swaps(n):
    inner = [(i, i ^ 1) for i in range(n)]
    outer = [(i, i + 1 if i % 2 else i - 1) for i in range(1, n - 1)]
    return inner, outer


def halo(x, core, after=None):
    inner, outer = pair_swaps(lax.axis_size("wa"))
    even = lax.rem(lax.axis_index("wa"), 2) == 0
    first, last = x[:, : 3 * C], x[:, -3 * C :]
    near = lax.ppermute(jnp.where(even, last, first), "wa", inner)
    far = lax.ppermute(jnp.where(even, first, last), "wa", outer)
    left, right = jnp.where(even, far, near), jnp.where(even, near, far)
    inner, outer = pair_swaps(lax.axis_size("ha"))
    even = core[0] == 0
    last = jnp.concatenate([left[5:], x[5:], right[5:]], axis=1)
    lead = jnp.concatenate([left[:3], x[:3], right[:3]], axis=1)
    if after is not None:
        lead, last, after = lax.optimization_barrier((lead, last, after))
    crossed = lax.ppermute(jnp.where(even, lead, last), "ha", outer)
    swapped = lax.ppermute(jnp.where(even, last, lead), "ha", inner)
    top, bottom = jnp.where(even, crossed, swapped), jnp.where(even, swapped, crossed)
    return left, right, jnp.concatenate([top, bottom], axis=0)


def plane_and_line():
    wide, pairs = lax.axis_size("wa"), lax.axis_size("ha") // 2
    depth = pairs // 2
    at = lambda x, z, c, w: ((x * depth + z) * 2 + c) * wide + w
    plane = [
        [at(x, z, c, w) for x in range(2) for w in range(wide)]
        for z in range(depth)
        for c in range(2)
    ]
    line = [
        [at(x, z, c, w) for z in range(depth)]
        for x in range(2)
        for w in range(wide)
        for c in range(2)
    ]
    return plane, line


def on_device(
    features, grad_out, dw_weight, dw_bias, ln_gain, ln_bias, w_in, b_in, w_out, b_out, scale
):
    row = lambda v: v.reshape(1, -1)
    core = lax.rem(lax.axis_index("ha"), 2).reshape(1).astype(jnp.int32)
    swap, _ = pair_swaps(lax.axis_size("ha"))
    plane, line = plane_and_line()

    def exchange(x, groups):
        return lax.all_to_all(x, ("ha", "wa"), 0, 0, axis_index_groups=groups, tiled=True)

    dconv, keep, send = run_main(
        core, features, *halo(features, core), grad_out, dw_weight, row(dw_bias), row(ln_gain),
        row(ln_bias), w_in, w_in.T, row(b_in), w_out.T, row(b_out), row(scale),
    )
    half = (keep.astype(F32) + lax.ppermute(send, "ha", swap).astype(F32)).astype(BF16)
    half, dconv = lax.optimization_barrier((half, dconv))
    terms = exchange(half, plane)
    edges = halo(dconv, core, terms)
    fold_first = lambda v, n: jnp.sum(v.reshape((n, -1) + v.shape[1:]).astype(F32), axis=0).astype(BF16)
    sums = fold_first(terms, len(plane[0]))
    every = jnp.broadcast_to(sums[None], (len(line[0]),) + sums.shape)
    total = fold_first(exchange(every.reshape((-1,) + sums.shape[1:]), line), len(line[0]))
    total, edges = lax.optimization_barrier((total, edges))
    mine = jnp.broadcast_to(total[None], (len(plane[0]),) + total.shape).reshape(half.shape)
    mine = exchange(mine, plane)
    grad_features = run_transposed(dconv, *edges, grad_out, dw_weight[::-1])
    mine, grad_features = lax.optimization_barrier((mine, grad_features))
    other = lax.ppermute(mine, "ha", swap)
    o_dw, o_dwb, o_gain, o_lnb, o_win, o_bin, o_wout, o_bout, o_scale = run_finish(
        core, mine, other
    )
    flat = lambda v: v.reshape(-1)
    return (
        grad_features, o_dw, flat(o_dwb), flat(o_gain), flat(o_lnb), o_win, flat(o_bin), o_wout,
        flat(o_bout), flat(o_scale),
    )


def solution(mesh):
    return jax.shard_map(
        on_device,
        mesh=mesh,
        in_specs=(P("ha", "wa"), P("ha", "wa"), P(), P(), P(), P(), P(), P(), P(), P(), P()),
        out_specs=(P("ha", "wa"), P(), P(), P(), P(), P(), P(), P(), P(), P()),
        check_vma=False,
    )
```

```python
import math

import jax
import jax.numpy as jnp
from jax import lax
from jax.experimental import pallas as pl
from jax.experimental.pallas import tpu as pltpu
from jax.sharding import PartitionSpec as P

eps_norm = 1e-06
clip_bound = 500.0
F32, BF16 = jnp.float32, jnp.bfloat16
ROWS, COLS, C, HID = 8, 128, 256, 1024
PIX = ROWS * COLS
WIDE = COLS + 6
JB = 8
MIB = 1024 * 1024


def shift_rows(own, left, right, rows, tall, shifted):
    def place(j, mid, at):
        edge = rows[:, pl.ds(at, C)].astype(F32)
        tall[j, 8:16, :] = mid.astype(F32)
        tall[j, 5:8, :] = edge[0:3]
        tall[j, 16:19, :] = edge[3:6]
        for a in range(7):
            shifted[a, j] = tall[j, 5 + a : 13 + a, :]

    for k in range(3):
        place(k, left[:, k * C : (k + 1) * C], k * C)
        place(COLS + 3 + k, right[:, k * C : (k + 1) * C], (COLS + 3 + k) * C)

    def step(j, carry):
        mid = own[:, pl.ds(pl.multiple_of(j * C, C), C)]
        place(j + 3, mid, pl.multiple_of((j + 3) * C, C))
        return carry

    lax.fori_loop(0, COLS, step, 0, unroll=4)


def spread_weights(w_ref, spread):
    for k in range(49):
        spread[k] = jnp.broadcast_to(w_ref[k : k + 1, :], (8, C))


def conv_block(shifted, spread, first, lane):
    lanes = slice(lane * 128, lane * 128 + 128)
    acc = [None] * JB
    for a in range(7):
        taps = [spread[a * 7 + b, :, lanes] for b in range(7)]
        for t in range(JB + 6):
            x = shifted[a, first + t, :, lanes]
            for b in range(7):
                o = t - b
                if 0 <= o < JB:
                    term = x * taps[b]
                    acc[o] = term if acc[o] is None else acc[o] + term
    return acc


def fold(x):
    return jnp.sum(x.reshape(-1, 8, C), axis=0)


def main_kernel(
    core, own, left, right, rows, grad, dww, dwb, gain, lnb, w_in, w_in_t, b_in, w_out_t, b_out, scale,
    dconv_out, keep, send,
    tall, shifted, spread, conv, normed, inv, lnout, lnout_t, grad_flat, grad_t, pre, dact, act, dpre, dcw, small,
    pay,
):
    shift_rows(own, left, right, rows, tall, shifted)
    spread_weights(dww, spread)

    def normalize(n):
        first = n * JB
        block = conv[pl.ds(first, JB)].reshape(JB * 8, C) + dwb[...]
        center = block - jnp.mean(block, axis=-1, keepdims=True)
        inverse = lax.rsqrt(jnp.mean(center * center, axis=-1, keepdims=True) + eps_norm)
        norm = center * inverse
        at = pl.ds(pl.multiple_of(first * 8, 64), JB * 8)
        normed[at, :] = norm
        inv[at, :] = inverse
        lnout[at, :] = (norm * gain[...] + lnb[...]).astype(BF16)

    def convolve(n):
        first = n * JB
        for lane in range(2):
            lanes = slice(lane * 128, lane * 128 + 128)
            for o, acc in enumerate(conv_block(shifted, spread, first, lane)):
                conv[first + o, :, lanes] = acc
        for o in range(JB):
            at = pl.multiple_of((first + o) * C, C)
            g = grad[:, pl.ds(at, C)].astype(F32)
            grad_flat[pl.ds(pl.multiple_of((first + o) * 8, 8), 8), :] = g

    def forward(n, carry):
        normalize(n - 1)
        convolve(n)
        return carry

    convolve(0)
    lax.fori_loop(1, COLS // JB, forward, 0)
    normalize(COLS // JB - 1)

    CH = 256

    def mlp(n, carry):
        s_gain, s_lnb, s_g, s_dwb = carry
        rows = pl.ds(pl.multiple_of(n * CH, CH), CH)
        ln = lnout[rows, :]
        lnout_t[n, 0:C, :] = ln.astype(F32).T.astype(BF16)
        g = grad_flat[rows, :]
        grad_t[n] = g.T.astype(BF16)
        pre[...] = jnp.dot(ln, w_in[...], preferred_element_type=F32) + b_in[...]
        dbr = (g * scale[...]).astype(BF16)
        dact[...] = jnp.dot(dbr, w_out_t[...], preferred_element_type=F32)
        s_g = s_g + fold(g)

        def gelu(m, c):
            sub = pl.ds(pl.multiple_of(m * 16, 16), 16)
            out = pl.ds(pl.multiple_of(n * CH + m * 16, 16), 16)
            for q in range(4):
                lanes = slice(q * 256, q * 256 + 256)
                v = pre[sub, lanes]
                e = jnp.exp2(v * v * (-0.5 / math.log(2.0)))
                d = 1.0 + (0.3275911 / math.sqrt(2.0)) * jnp.abs(v)
                t = pl.reciprocal(d, approx=True)
                t = t * (2.0 - d * t)
                poly = 0.5 * 1.061405429 * t - 0.5 * 1.453152027
                poly = poly * t + 0.5 * 1.421413741
                poly = poly * t - 0.5 * 0.284496736
                poly = poly * t + 0.5 * 0.254829592
                tail = poly * t * e
                cdf = jnp.where(v < 0.0, tail, 1.0 - tail)
                act[out, lanes] = (v * cdf).astype(BF16)
                slope = cdf + v * (e * (1.0 / math.sqrt(2.0 * math.pi)))
                dpre[out, lanes] = (dact[sub, lanes] * slope).astype(BF16)
            return c

        lax.fori_loop(0, CH // 16, gelu, 0, unroll=4)
        dact[:, 0:C] = jnp.dot(dpre[rows, :], w_in_t[...], preferred_element_type=F32)

        def back(m, c):
            s_gain, s_lnb, s_dwb = c
            sub = pl.ds(pl.multiple_of(m * 64, 64), 64)
            out = pl.ds(pl.multiple_of(n * CH + m * 64, 64), 64)
            dln = dact[sub, 0:C]
            norm = normed[out, :]
            prod = dln * norm
            s_gain = s_gain + fold(prod)
            s_lnb = s_lnb + fold(dln)
            dn = dln * gain[...]
            m1 = jnp.mean(dn, axis=-1, keepdims=True)
            m2 = jnp.mean(dn * norm, axis=-1, keepdims=True)
            dc = ((dn - m1 - norm * m2) * inv[out, :]).astype(BF16)
            wide = dc.astype(F32)
            s_dwb = s_dwb + fold(wide)
            wide = wide.reshape(8, 8, C)
            j0 = n * (CH // 8) + m * 8
            dcw[pl.ds(j0, 8)] = wide
            for o in range(8):
                dconv_out[:, pl.ds(pl.multiple_of((j0 + o) * C, C), C)] = wide[o].astype(BF16)
            return s_gain, s_lnb, s_dwb

        s_gain, s_lnb, s_dwb = lax.fori_loop(0, CH // 64, back, (s_gain, s_lnb, s_dwb), unroll=2)
        return s_gain, s_lnb, s_g, s_dwb

    for n in range(PIX // CH):
        lnout_t[n, C:, :] = jnp.ones((16, CH), BF16)
    zero = jnp.zeros((8, C), F32)
    s_gain, s_lnb, s_g, s_dwb = lax.fori_loop(0, PIX // CH, mlp, (zero, zero, zero, zero))

    small[...] = jnp.zeros_like(small)
    down = lambda v: jnp.sum(v, axis=0, keepdims=True)
    sum_g = down(s_g)
    small[49:50, :] = down(s_dwb)
    small[50:51, :] = down(s_gain)
    small[51:52, :] = down(s_lnb)
    small[52:53, :] = sum_g * scale[...]

    pay[:, :, :, C:] = jnp.zeros((2, 128, 8, 128), BF16)
    s_scale = jnp.zeros((C, 1), F32)
    for q in range(4):
        lanes = slice(q * 256, q * 256 + 256)
        total = jnp.zeros((C + 16, 256), F32)
        for n in range(PIX // CH):
            part = slice(n * CH, (n + 1) * CH)
            total = total + jnp.dot(lnout_t[n], dpre[part, lanes], preferred_element_type=F32)
        small[54 + q : 55 + q, :] = total[C : C + 1]
        pay[0, q * 32 : q * 32 + 32, :, 0:C] = total[0:C].reshape(32, 8, C).astype(BF16)
    for q in range(4):
        lanes = slice(q * 256, q * 256 + 256)
        total = jnp.zeros((C, 256), F32)
        for n in range(PIX // CH):
            part = slice(n * CH, (n + 1) * CH)
            total = total + jnp.dot(grad_t[n], act[part, lanes], preferred_element_type=F32)
        s_scale = s_scale + jnp.sum(total * w_out_t[:, lanes].astype(F32), axis=1, keepdims=True)
        pay[1, q * 32 : q * 32 + 32, :, 0:C] = (
            (total.T * scale[...]).reshape(32, 8, C).astype(BF16)
        )
    wide_scale = jnp.broadcast_to(s_scale, (C, 128)).T
    small[53:54, :] = wide_scale[0:1, :] + b_out[...] * sum_g

    for lane in range(2):
        lanes = slice(lane * 128, lane * 128 + 128)
        for group in ((0, 1), (2, 3), (4, 5), (6,)):

            def taps(n, acc, group=group, lanes=lanes):
                first = n * JB
                d = [dcw[first + o, :, lanes] for o in range(JB)]
                acc = list(acc)
                for p, a in enumerate(group):
                    for t in range(JB + 6):
                        x = shifted[a, first + t, :, lanes]
                        for b in range(7):
                            o = t - b
                            if 0 <= o < JB:
                                acc[p * 7 + b] = acc[p * 7 + b] + d[o] * x
                return tuple(acc)

            none = jnp.zeros((8, 128), F32)
            acc = lax.fori_loop(0, COLS // JB, taps, (none,) * (7 * len(group)))
            for p, a in enumerate(group):
                for b in range(7):
                    k = a * 7 + b
                    small[k : k + 1, lanes] = down(acc[p * 7 + b])

    for k in range(8):
        for lane in range(2):
            part = small[k * 8 : k * 8 + 8, lane * 128 : lane * 128 + 128]
            pay[0, k * 2 + lane, :, C:] = part.astype(BF16)
    keep[...] = pay[core[0]]
    send[...] = pay[1 - core[0]]


def transposed_kernel(
    own, left, right, rows, grad, dww, out, tall, shifted, spread
):
    shift_rows(own, left, right, rows, tall, shifted)
    spread_weights(dww, spread)

    def step(n, carry):
        first = n * JB
        for lane in range(2):
            for o, acc in enumerate(conv_block(shifted, spread, first, lane)):
                at = pl.ds(pl.multiple_of((first + o) * C + lane * 128, 128), 128)
                out[:, at] = (acc + grad[:, at].astype(F32)).astype(BF16)
        return carry

    lax.fori_loop(0, COLS // JB, step, 0)


def finish_kernel(
    core, mine, other, o_dw, o_dwb, o_gain, o_lnb, o_win, o_bin, o_wout, o_bout, o_scale, small, win, wout
):
    even = core[0] == 0
    total = jnp.zeros((8, 256), F32)
    for q in range(4):
        for part in range(4):
            at = slice(q * 32 + part * 8, q * 32 + part * 8 + 8)
            a = mine[at, :, 0:C].astype(F32)
            b = other[at, :, 0:C].astype(F32)
            first = jnp.where(even, a, b)
            second = jnp.where(even, b, a)
            total = total + jnp.sum(first * first + second * second, axis=0)
            win[part * 64 : part * 64 + 64, q * 256 : q * 256 + 256] = first.reshape(64, C)
            row = q * 256 + part * 64
            wout[row : row + 64, :] = second.reshape(64, C)
    for k in range(8):
        for lane in range(2):
            a = mine[k * 2 + lane, :, C:].astype(F32)
            b = other[k * 2 + lane, :, C:].astype(F32)
            small[k * 8 : k * 8 + 8, lane * 128 : lane * 128 + 128] = jnp.where(even, a, b)
    rest = small[...]
    total = total + jnp.sum((rest * rest).reshape(8, 8, C), axis=0)
    squares = jnp.sum(jnp.sum(total, axis=1, keepdims=True), axis=0, keepdims=True)
    factor = jnp.minimum(1.0, clip_bound / jnp.sqrt(squares))
    o_win[...] = win[...] * factor
    o_wout[...] = wout[...] * factor
    o_dw[...] = small[0:49, :] * factor
    o_dwb[...] = small[49:50, :] * factor
    o_gain[...] = small[50:51, :] * factor
    o_lnb[...] = small[51:52, :] * factor
    o_bout[...] = small[52:53, :] * factor
    o_scale[...] = small[53:54, :] * factor
    for q in range(4):
        o_bin[:, q * 256 : q * 256 + 256] = small[54 + q : 55 + q, :] * factor


CONV_SCRATCH = (
    pltpu.VMEM((WIDE, 24, C), F32),
    pltpu.VMEM((7, WIDE, 8, C), F32),
    pltpu.VMEM((49, 8, C), F32),
)


def run_main(*operands):
    return pl.pallas_call(
        main_kernel,
        out_shape=(
            jax.ShapeDtypeStruct((ROWS, COLS * C), BF16),
            jax.ShapeDtypeStruct((128, 8, 384), BF16),
            jax.ShapeDtypeStruct((128, 8, 384), BF16),
        ),
        in_specs=[pl.BlockSpec(memory_space=pltpu.SMEM)]
        + [pl.BlockSpec(memory_space=pltpu.VMEM)] * (len(operands) - 1),
        scratch_shapes=CONV_SCRATCH
        + (
            pltpu.VMEM((COLS, 8, C), F32),
            pltpu.VMEM((PIX, C), F32),
            pltpu.VMEM((PIX, 1), F32),
            pltpu.VMEM((PIX, C), BF16),
            pltpu.VMEM((4, C + 16, 256), BF16),
            pltpu.VMEM((PIX, C), F32),
            pltpu.VMEM((4, C, 256), BF16),
            pltpu.VMEM((256, HID), F32),
            pltpu.VMEM((256, HID), F32),
            pltpu.VMEM((PIX, HID), BF16),
            pltpu.VMEM((PIX, HID), BF16),
            pltpu.VMEM((COLS, 8, C), F32),
            pltpu.VMEM((64, C), F32),
            pltpu.VMEM((2, 128, 8, 384), BF16),
        ),
        compiler_params=pltpu.CompilerParams(vmem_limit_bytes=40 * MIB),
        name="block_backward",
    )(*operands)


def run_transposed(*operands):
    return pl.pallas_call(
        transposed_kernel,
        out_shape=jax.ShapeDtypeStruct((ROWS, COLS * C), BF16),
        scratch_shapes=CONV_SCRATCH,
        compiler_params=pltpu.CompilerParams(vmem_limit_bytes=20 * MIB),
        cost_estimate=pl.CostEstimate(flops=200_000_000, bytes_accessed=40 * MIB, transcendentals=0),
        name="transposed_conv",
    )(*operands)


def run_finish(core, mine, other):
    vec = jax.ShapeDtypeStruct((1, C), F32)
    vmem = pl.BlockSpec(memory_space=pltpu.VMEM)
    return pl.pallas_call(
        finish_kernel,
        in_specs=[pl.BlockSpec(memory_space=pltpu.SMEM), vmem, vmem],
        out_shape=(
            jax.ShapeDtypeStruct((49, C), F32), vec, vec, vec, jax.ShapeDtypeStruct((C, HID), F32),
            jax.ShapeDtypeStruct((1, HID), F32), jax.ShapeDtypeStruct((HID, C), F32), vec, vec,
        ),
        scratch_shapes=(
            pltpu.VMEM((64, C), F32), pltpu.VMEM((C, HID), F32), pltpu.VMEM((HID, C), F32),
        ),
        compiler_params=pltpu.CompilerParams(vmem_limit_bytes=16 * MIB),
        name="clip",
    )(core, mine, other)


def pair_swaps(n):
    inner = [(i, i ^ 1) for i in range(n)]
    outer = [(i, i + 1 if i % 2 else i - 1) for i in range(1, n - 1)]
    return inner, outer


def halo(x, core, after=None):
    inner, outer = pair_swaps(lax.axis_size("wa"))
    even = lax.rem(lax.axis_index("wa"), 2) == 0
    first, last = x[:, : 3 * C], x[:, -3 * C :]
    near = lax.ppermute(jnp.where(even, last, first), "wa", inner)
    far = lax.ppermute(jnp.where(even, first, last), "wa", outer)
    if after is not None:
        near, far, after = lax.optimization_barrier((near, far, after))
    left, right = jnp.where(even, far, near), jnp.where(even, near, far)
    inner, outer = pair_swaps(lax.axis_size("ha"))
    even = core[0] == 0
    last = jnp.concatenate([left[5:], x[5:], right[5:]], axis=1)
    lead = jnp.concatenate([left[:3], x[:3], right[:3]], axis=1)
    crossed = lax.ppermute(jnp.where(even, lead, last), "ha", outer)
    swapped = lax.ppermute(jnp.where(even, last, lead), "ha", inner)
    top, bottom = jnp.where(even, crossed, swapped), jnp.where(even, swapped, crossed)
    return left, right, jnp.concatenate([top, bottom], axis=0)


def plane_and_line():
    wide, pairs = lax.axis_size("wa"), lax.axis_size("ha") // 2
    depth = pairs // 2
    at = lambda x, z, c, w: ((x * depth + z) * 2 + c) * wide + w
    plane = [
        [at(x, z, c, w) for x in range(2) for w in range(wide)]
        for z in range(depth)
        for c in range(2)
    ]
    line = [
        [at(x, z, c, w) for z in range(depth)]
        for x in range(2)
        for w in range(wide)
        for c in range(2)
    ]
    return plane, line


def on_device(
    features, grad_out, dw_weight, dw_bias, ln_gain, ln_bias, w_in, b_in, w_out, b_out, scale
):
    row = lambda v: v.reshape(1, -1)
    core = lax.rem(lax.axis_index("ha"), 2).reshape(1).astype(jnp.int32)
    swap, _ = pair_swaps(lax.axis_size("ha"))
    plane, line = plane_and_line()

    def exchange(x, groups):
        return lax.all_to_all(x, ("ha", "wa"), 0, 0, axis_index_groups=groups, tiled=True)

    dconv, keep, send = run_main(
        core, features, *halo(features, core), grad_out, dw_weight, row(dw_bias), row(ln_gain),
        row(ln_bias), w_in, w_in.T, row(b_in), w_out.T, row(b_out), row(scale),
    )
    half = (keep.astype(F32) + lax.ppermute(send, "ha", swap).astype(F32)).astype(BF16)
    half, dconv = lax.optimization_barrier((half, dconv))
    terms = exchange(half, plane)
    edges = halo(dconv, core, terms)
    fold_first = lambda v, n: jnp.sum(v.reshape((n, -1) + v.shape[1:]).astype(F32), axis=0).astype(BF16)
    sums = fold_first(terms, len(plane[0]))
    every = jnp.broadcast_to(sums[None], (len(line[0]),) + sums.shape)
    total = fold_first(exchange(every.reshape((-1,) + sums.shape[1:]), line), len(line[0]))
    total, edges = lax.optimization_barrier((total, edges))
    mine = jnp.broadcast_to(total[None], (len(plane[0]),) + total.shape).reshape(half.shape)
    mine = exchange(mine, plane)
    grad_features = run_transposed(dconv, *edges, grad_out, dw_weight[::-1])
    mine, grad_features = lax.optimization_barrier((mine, grad_features))
    other = lax.ppermute(mine, "ha", swap)
    o_dw, o_dwb, o_gain, o_lnb, o_win, o_bin, o_wout, o_bout, o_scale = run_finish(
        core, mine, other
    )
    flat = lambda v: v.reshape(-1)
    return (
        grad_features, o_dw, flat(o_dwb), flat(o_gain), flat(o_lnb), o_win, flat(o_bin), o_wout,
        flat(o_bout), flat(o_scale),
    )


def solution(mesh):
    return jax.shard_map(
        on_device,
        mesh=mesh,
        in_specs=(P("ha", "wa"), P("ha", "wa"), P(), P(), P(), P(), P(), P(), P(), P(), P()),
        out_specs=(P("ha", "wa"), P(), P(), P(), P(), P(), P(), P(), P(), P()),
        check_vma=False,
    )
```

```python
import math

import jax
import jax.numpy as jnp
from jax import lax
from jax.experimental import pallas as pl
from jax.experimental.pallas import tpu as pltpu
from jax.sharding import PartitionSpec as P

eps_norm = 1e-06
clip_bound = 500.0
F32, BF16 = jnp.float32, jnp.bfloat16
ROWS, COLS, C, HID = 8, 128, 256, 1024
PIX = ROWS * COLS
WIDE = COLS + 6
JB = 8
MIB = 1024 * 1024


def shift_rows(own, left, right, rows, tall, shifted):
    def place(j, mid, at):
        edge = rows[:, pl.ds(at, C)].astype(F32)
        tall[j, 8:16, :] = mid.astype(F32)
        tall[j, 5:8, :] = edge[0:3]
        tall[j, 16:19, :] = edge[3:6]
        for a in range(7):
            shifted[a, j] = tall[j, 5 + a : 13 + a, :]

    for k in range(3):
        place(k, left[:, k * C : (k + 1) * C], k * C)
        place(COLS + 3 + k, right[:, k * C : (k + 1) * C], (COLS + 3 + k) * C)

    def step(j, carry):
        mid = own[:, pl.ds(pl.multiple_of(j * C, C), C)]
        place(j + 3, mid, pl.multiple_of((j + 3) * C, C))
        return carry

    lax.fori_loop(0, COLS, step, 0, unroll=4)


def spread_weights(w_ref, spread):
    for k in range(49):
        spread[k] = jnp.broadcast_to(w_ref[k : k + 1, :], (8, C))


def conv_block(shifted, spread, first, lane):
    lanes = slice(lane * 128, lane * 128 + 128)
    acc = [None] * JB
    for a in range(7):
        taps = [spread[a * 7 + b, :, lanes] for b in range(7)]
        for t in range(JB + 6):
            x = shifted[a, first + t, :, lanes]
            for b in range(7):
                o = t - b
                if 0 <= o < JB:
                    term = x * taps[b]
                    acc[o] = term if acc[o] is None else acc[o] + term
    return acc


def fold(x):
    return jnp.sum(x.reshape(-1, 8, C), axis=0)


def main_kernel(
    core, own, left, right, rows, grad, dww, dwb, gain, lnb, w_in, w_in_t, b_in, w_out_t, b_out, scale,
    dconv_out, keep, send,
    tall, shifted, spread, conv, normed, inv, lnout, lnout_t, grad_flat, grad_t, pre, dact, act, dpre, dcw, small,
    pay,
):
    shift_rows(own, left, right, rows, tall, shifted)
    spread_weights(dww, spread)

    def normalize(n):
        first = n * JB
        block = conv[pl.ds(first, JB)].reshape(JB * 8, C) + dwb[...]
        center = block - jnp.mean(block, axis=-1, keepdims=True)
        inverse = lax.rsqrt(jnp.mean(center * center, axis=-1, keepdims=True) + eps_norm)
        norm = center * inverse
        at = pl.ds(pl.multiple_of(first * 8, 64), JB * 8)
        normed[at, :] = norm
        inv[at, :] = inverse
        lnout[at, :] = (norm * gain[...] + lnb[...]).astype(BF16)

    def convolve(n):
        first = n * JB
        for lane in range(2):
            lanes = slice(lane * 128, lane * 128 + 128)
            for o, acc in enumerate(conv_block(shifted, spread, first, lane)):
                conv[first + o, :, lanes] = acc
        for o in range(JB):
            at = pl.multiple_of((first + o) * C, C)
            g = grad[:, pl.ds(at, C)].astype(F32)
            grad_flat[pl.ds(pl.multiple_of((first + o) * 8, 8), 8), :] = g

    def forward(n, carry):
        normalize(n - 1)
        convolve(n)
        return carry

    convolve(0)
    lax.fori_loop(1, COLS // JB, forward, 0)
    normalize(COLS // JB - 1)

    CH = 256

    def mlp(n, carry):
        s_gain, s_lnb, s_g, s_dwb = carry
        rows = pl.ds(pl.multiple_of(n * CH, CH), CH)
        ln = lnout[rows, :]
        lnout_t[n, 0:C, :] = ln.astype(F32).T.astype(BF16)
        g = grad_flat[rows, :]
        grad_t[n] = g.T.astype(BF16)
        pre[...] = jnp.dot(ln, w_in[...], preferred_element_type=F32) + b_in[...]
        dbr = (g * scale[...]).astype(BF16)
        dact[...] = jnp.dot(dbr, w_out_t[...], preferred_element_type=F32)
        s_g = s_g + fold(g)

        def gelu(m, c):
            sub = pl.ds(pl.multiple_of(m * 16, 16), 16)
            out = pl.ds(pl.multiple_of(n * CH + m * 16, 16), 16)
            for q in range(4):
                lanes = slice(q * 256, q * 256 + 256)
                v = pre[sub, lanes]
                e = jnp.exp2(v * v * (-0.5 / math.log(2.0)))
                d = 1.0 + (0.3275911 / math.sqrt(2.0)) * jnp.abs(v)
                t = pl.reciprocal(d, approx=True)
                t = t * (2.0 - d * t)
                poly = 0.5 * 1.061405429 * t - 0.5 * 1.453152027
                poly = poly * t + 0.5 * 1.421413741
                poly = poly * t - 0.5 * 0.284496736
                poly = poly * t + 0.5 * 0.254829592
                tail = poly * t * e
                cdf = jnp.where(v < 0.0, tail, 1.0 - tail)
                act[out, lanes] = (v * cdf).astype(BF16)
                slope = cdf + v * (e * (1.0 / math.sqrt(2.0 * math.pi)))
                dpre[out, lanes] = (dact[sub, lanes] * slope).astype(BF16)
            return c

        lax.fori_loop(0, CH // 16, gelu, 0, unroll=4)
        dact[:, 0:C] = jnp.dot(dpre[rows, :], w_in_t[...], preferred_element_type=F32)

        def back(m, c):
            s_gain, s_lnb, s_dwb = c
            sub = pl.ds(pl.multiple_of(m * 64, 64), 64)
            out = pl.ds(pl.multiple_of(n * CH + m * 64, 64), 64)
            dln = dact[sub, 0:C]
            norm = normed[out, :]
            prod = dln * norm
            s_gain = s_gain + fold(prod)
            s_lnb = s_lnb + fold(dln)
            dn = dln * gain[...]
            m1 = jnp.mean(dn, axis=-1, keepdims=True)
            m2 = jnp.mean(dn * norm, axis=-1, keepdims=True)
            dc = ((dn - m1 - norm * m2) * inv[out, :]).astype(BF16)
            wide = dc.astype(F32)
            s_dwb = s_dwb + fold(wide)
            wide = wide.reshape(8, 8, C)
            j0 = n * (CH // 8) + m * 8
            dcw[pl.ds(j0, 8)] = wide
            for o in range(8):
                dconv_out[:, pl.ds(pl.multiple_of((j0 + o) * C, C), C)] = wide[o].astype(BF16)
            return s_gain, s_lnb, s_dwb

        s_gain, s_lnb, s_dwb = lax.fori_loop(0, CH // 64, back, (s_gain, s_lnb, s_dwb), unroll=2)
        return s_gain, s_lnb, s_g, s_dwb

    for n in range(PIX // CH):
        lnout_t[n, C:, :] = jnp.ones((16, CH), BF16)
    zero = jnp.zeros((8, C), F32)
    s_gain, s_lnb, s_g, s_dwb = lax.fori_loop(0, PIX // CH, mlp, (zero, zero, zero, zero))

    small[...] = jnp.zeros_like(small)
    down = lambda v: jnp.sum(v, axis=0, keepdims=True)
    sum_g = down(s_g)
    small[49:50, :] = down(s_dwb)
    small[50:51, :] = down(s_gain)
    small[51:52, :] = down(s_lnb)
    small[52:53, :] = sum_g * scale[...]

    s_scale = jnp.zeros((C, 1), F32)
    for q in range(4):
        lanes = slice(q * 256, q * 256 + 256)
        total = jnp.zeros((C + 16, 256), F32)
        for n in range(PIX // CH):
            part = slice(n * CH, (n + 1) * CH)
            total = total + jnp.dot(lnout_t[n], dpre[part, lanes], preferred_element_type=F32)
        small[54 + q : 55 + q, :] = total[C : C + 1]
        pay[0, q * 4 : q * 4 + 4] = total[0:C].reshape(4, 64, C)
    for q in range(4):
        lanes = slice(q * 256, q * 256 + 256)
        total = jnp.zeros((C, 256), F32)
        for n in range(PIX // CH):
            part = slice(n * CH, (n + 1) * CH)
            total = total + jnp.dot(grad_t[n], act[part, lanes], preferred_element_type=F32)
        s_scale = s_scale + jnp.sum(total * w_out_t[:, lanes].astype(F32), axis=1, keepdims=True)
        pay[1, q * 4 : q * 4 + 4] = (total.T * scale[...]).reshape(4, 64, C)
    wide_scale = jnp.broadcast_to(s_scale, (C, 128)).T
    small[53:54, :] = wide_scale[0:1, :] + b_out[...] * sum_g

    for lane in range(2):
        lanes = slice(lane * 128, lane * 128 + 128)
        for group in ((0, 1), (2, 3), (4, 5), (6,)):

            def taps(n, acc, group=group, lanes=lanes):
                first = n * JB
                d = [dcw[first + o, :, lanes] for o in range(JB)]
                acc = list(acc)
                for p, a in enumerate(group):
                    for t in range(JB + 6):
                        x = shifted[a, first + t, :, lanes]
                        for b in range(7):
                            o = t - b
                            if 0 <= o < JB:
                                acc[p * 7 + b] = acc[p * 7 + b] + d[o] * x
                return tuple(acc)

            none = jnp.zeros((8, 128), F32)
            acc = lax.fori_loop(0, COLS // JB, taps, (none,) * (7 * len(group)))
            for p, a in enumerate(group):
                for b in range(7):
                    k = a * 7 + b
                    small[k : k + 1, lanes] = down(acc[p * 7 + b])

    even = core[0] == 0
    for k in range(16):
        rest = small[k * 8 : k * 8 + 8, :] if k < 8 else jnp.zeros((8, C), F32)
        none = jnp.zeros((8, C), F32)
        for out, half, first in ((keep, core[0], even), (send, 1 - core[0], jnp.logical_not(even))):
            extra = jnp.where(first, rest, none)
            out[k] = jnp.concatenate([pay[half, k], extra], axis=0).astype(BF16)


def transposed_kernel(
    own, left, right, rows, grad, dww, out, tall, shifted, spread
):
    shift_rows(own, left, right, rows, tall, shifted)
    spread_weights(dww, spread)

    def step(n, carry):
        first = n * JB
        for lane in range(2):
            for o, acc in enumerate(conv_block(shifted, spread, first, lane)):
                at = pl.ds(pl.multiple_of((first + o) * C + lane * 128, 128), 128)
                out[:, at] = (acc + grad[:, at].astype(F32)).astype(BF16)
        return carry

    lax.fori_loop(0, COLS // JB, step, 0)


def finish_kernel(
    core, mine, other, o_dw, o_dwb, o_gain, o_lnb, o_win, o_bin, o_wout, o_bout, o_scale, small, win, wout
):
    even = core[0] == 0
    total = jnp.zeros((8, 256), F32)
    for k in range(16):
        a, b = mine[k].astype(F32), other[k].astype(F32)
        first, second = jnp.where(even, a, b), jnp.where(even, b, a)
        squares = first[0:64] * first[0:64] + second[0:64] * second[0:64]
        total = total + jnp.sum(squares.reshape(8, 8, C), axis=0)
        q, part = k // 4, k % 4
        win[part * 64 : part * 64 + 64, q * 256 : q * 256 + 256] = first[0:64]
        wout[k * 64 : k * 64 + 64, :] = second[0:64]
        if k < 8:
            small[k * 8 : k * 8 + 8, :] = first[64:72]
    rest = small[...]
    total = total + jnp.sum((rest * rest).reshape(8, 8, C), axis=0)
    squares = jnp.sum(jnp.sum(total, axis=1, keepdims=True), axis=0, keepdims=True)
    factor = jnp.minimum(1.0, clip_bound / jnp.sqrt(squares))
    o_win[...] = win[...] * factor
    o_wout[...] = wout[...] * factor
    o_dw[...] = small[0:49, :] * factor
    o_dwb[...] = small[49:50, :] * factor
    o_gain[...] = small[50:51, :] * factor
    o_lnb[...] = small[51:52, :] * factor
    o_bout[...] = small[52:53, :] * factor
    o_scale[...] = small[53:54, :] * factor
    for q in range(4):
        o_bin[:, q * 256 : q * 256 + 256] = small[54 + q : 55 + q, :] * factor


CONV_SCRATCH = (
    pltpu.VMEM((WIDE, 24, C), F32),
    pltpu.VMEM((7, WIDE, 8, C), F32),
    pltpu.VMEM((49, 8, C), F32),
)


def run_main(*operands):
    return pl.pallas_call(
        main_kernel,
        out_shape=(
            jax.ShapeDtypeStruct((ROWS, COLS * C), BF16),
            jax.ShapeDtypeStruct((16, 72, C), BF16),
            jax.ShapeDtypeStruct((16, 72, C), BF16),
        ),
        in_specs=[pl.BlockSpec(memory_space=pltpu.SMEM)]
        + [pl.BlockSpec(memory_space=pltpu.VMEM)] * (len(operands) - 1),
        scratch_shapes=CONV_SCRATCH
        + (
            pltpu.VMEM((COLS, 8, C), F32),
            pltpu.VMEM((PIX, C), F32),
            pltpu.VMEM((PIX, 1), F32),
            pltpu.VMEM((PIX, C), BF16),
            pltpu.VMEM((4, C + 16, 256), BF16),
            pltpu.VMEM((PIX, C), F32),
            pltpu.VMEM((4, C, 256), BF16),
            pltpu.VMEM((256, HID), F32),
            pltpu.VMEM((256, HID), F32),
            pltpu.VMEM((PIX, HID), BF16),
            pltpu.VMEM((PIX, HID), BF16),
            pltpu.VMEM((COLS, 8, C), F32),
            pltpu.VMEM((64, C), F32),
            pltpu.VMEM((2, 16, 64, C), F32),
        ),
        compiler_params=pltpu.CompilerParams(vmem_limit_bytes=40 * MIB),
        name="block_backward",
    )(*operands)


def run_transposed(*operands):
    return pl.pallas_call(
        transposed_kernel,
        out_shape=jax.ShapeDtypeStruct((ROWS, COLS * C), BF16),
        scratch_shapes=CONV_SCRATCH,
        compiler_params=pltpu.CompilerParams(vmem_limit_bytes=20 * MIB),
        cost_estimate=pl.CostEstimate(flops=200_000_000, bytes_accessed=40 * MIB, transcendentals=0),
        name="transposed_conv",
    )(*operands)


def run_finish(core, mine, other):
    vec = jax.ShapeDtypeStruct((1, C), F32)
    vmem = pl.BlockSpec(memory_space=pltpu.VMEM)
    return pl.pallas_call(
        finish_kernel,
        in_specs=[pl.BlockSpec(memory_space=pltpu.SMEM), vmem, vmem],
        out_shape=(
            jax.ShapeDtypeStruct((49, C), F32), vec, vec, vec, jax.ShapeDtypeStruct((C, HID), F32),
            jax.ShapeDtypeStruct((1, HID), F32), jax.ShapeDtypeStruct((HID, C), F32), vec, vec,
        ),
        scratch_shapes=(
            pltpu.VMEM((64, C), F32), pltpu.VMEM((C, HID), F32), pltpu.VMEM((HID, C), F32),
        ),
        compiler_params=pltpu.CompilerParams(vmem_limit_bytes=16 * MIB),
        name="clip",
    )(core, mine, other)


def pair_swaps(n):
    inner = [(i, i ^ 1) for i in range(n)]
    outer = [(i, i + 1 if i % 2 else i - 1) for i in range(1, n - 1)]
    return inner, outer


def halo(x, core, beside_columns=None, beside_rows=None):
    inner, outer = pair_swaps(lax.axis_size("wa"))
    even = lax.rem(lax.axis_index("wa"), 2) == 0
    first, last = x[:, : 3 * C], x[:, -3 * C :]
    near = lax.ppermute(jnp.where(even, last, first), "wa", inner)
    far = lax.ppermute(jnp.where(even, first, last), "wa", outer)
    if beside_columns is not None:
        near, far, _ = lax.optimization_barrier((near, far, beside_columns))
    left, right = jnp.where(even, far, near), jnp.where(even, near, far)
    inner, outer = pair_swaps(lax.axis_size("ha"))
    even = core[0] == 0
    last = jnp.concatenate([left[5:], x[5:], right[5:]], axis=1)
    lead = jnp.concatenate([left[:3], x[:3], right[:3]], axis=1)
    crossed = lax.ppermute(jnp.where(even, lead, last), "ha", outer)
    swapped = lax.ppermute(jnp.where(even, last, lead), "ha", inner)
    if beside_rows is not None:
        crossed, swapped, _ = lax.optimization_barrier((crossed, swapped, beside_rows))
    top, bottom = jnp.where(even, crossed, swapped), jnp.where(even, swapped, crossed)
    return left, right, jnp.concatenate([top, bottom], axis=0)


def plane_and_line():
    wide, pairs = lax.axis_size("wa"), lax.axis_size("ha") // 2
    depth = pairs // 2
    at = lambda x, z, c, w: ((x * depth + z) * 2 + c) * wide + w
    plane = [
        [at(x, z, c, w) for x in range(2) for w in range(wide)]
        for z in range(depth)
        for c in range(2)
    ]
    line = [
        [at(x, z, c, w) for z in range(depth)]
        for x in range(2)
        for w in range(wide)
        for c in range(2)
    ]
    return plane, line


def on_device(
    features, grad_out, dw_weight, dw_bias, ln_gain, ln_bias, w_in, b_in, w_out, b_out, scale
):
    row = lambda v: v.reshape(1, -1)
    core = lax.rem(lax.axis_index("ha"), 2).reshape(1).astype(jnp.int32)
    swap, _ = pair_swaps(lax.axis_size("ha"))
    plane, line = plane_and_line()

    def exchange(x, groups):
        return lax.all_to_all(x, ("ha", "wa"), 0, 0, axis_index_groups=groups, tiled=True)

    dconv, keep, send = run_main(
        core, features, *halo(features, core), grad_out, dw_weight, row(dw_bias), row(ln_gain),
        row(ln_bias), w_in, w_in.T, row(b_in), w_out.T, row(b_out), row(scale),
    )
    half = (keep.astype(F32) + lax.ppermute(send, "ha", swap).astype(F32)).astype(BF16)
    half, dconv = lax.optimization_barrier((half, dconv))
    add_up = lambda v: jnp.sum(v.astype(F32), axis=0).astype(BF16)
    repeat = lambda v, n: jnp.broadcast_to(v[None], (n,) + v.shape)
    terms = exchange(half, plane)
    sums = exchange(repeat(add_up(terms), len(line[0])), line)
    edges = halo(dconv, core, terms, sums)
    total = add_up(sums)
    total, edges = lax.optimization_barrier((total, edges))
    mine = exchange(repeat(total, len(plane[0])), plane)
    grad_features = run_transposed(dconv, *edges, grad_out, dw_weight[::-1])
    mine, grad_features = lax.optimization_barrier((mine, grad_features))
    other = lax.ppermute(mine, "ha", swap)
    o_dw, o_dwb, o_gain, o_lnb, o_win, o_bin, o_wout, o_bout, o_scale = run_finish(
        core, mine, other
    )
    flat = lambda v: v.reshape(-1)
    return (
        grad_features, o_dw, flat(o_dwb), flat(o_gain), flat(o_lnb), o_win, flat(o_bin), o_wout,
        flat(o_bout), flat(o_scale),
    )


def solution(mesh):
    return jax.shard_map(
        on_device,
        mesh=mesh,
        in_specs=(P("ha", "wa"), P("ha", "wa"), P(), P(), P(), P(), P(), P(), P(), P(), P()),
        out_specs=(P("ha", "wa"), P(), P(), P(), P(), P(), P(), P(), P(), P()),
        check_vma=False,
    )
```

```python
import math

import jax
import jax.numpy as jnp
from jax import lax
from jax.experimental import pallas as pl
from jax.experimental.pallas import tpu as pltpu
from jax.sharding import PartitionSpec as P

eps_norm = 1e-06
clip_bound = 500.0
F32, BF16 = jnp.float32, jnp.bfloat16
ROWS, COLS, C, HID = 8, 128, 256, 1024
PIX = ROWS * COLS
WIDE = COLS + 6
JB = 8
MIB = 1024 * 1024


def shift_rows(core, own, left, right, rows, tall, shifted):
    even = core[0] == 0

    def place(j, mid, at):
        edge = rows[:, pl.ds(at, C)].astype(F32)
        crossed, swapped = edge[0:3], edge[3:6]
        tall[j, 8:16, :] = mid.astype(F32)
        tall[j, 5:8, :] = jnp.where(even, crossed, swapped)
        tall[j, 16:19, :] = jnp.where(even, swapped, crossed)
        for a in range(7):
            shifted[a, j] = tall[j, 5 + a : 13 + a, :]

    for k in range(3):
        place(k, left[:, k * C : (k + 1) * C], k * C)
        place(COLS + 3 + k, right[:, k * C : (k + 1) * C], (COLS + 3 + k) * C)

    def step(j, carry):
        mid = own[:, pl.ds(pl.multiple_of(j * C, C), C)]
        place(j + 3, mid, pl.multiple_of((j + 3) * C, C))
        return carry

    lax.fori_loop(0, COLS, step, 0, unroll=4)


def spread_weights(w_ref, spread):
    for k in range(49):
        spread[k] = jnp.broadcast_to(w_ref[k : k + 1, :], (8, C))


def conv_block(shifted, spread, first, lane):
    lanes = slice(lane * 128, lane * 128 + 128)
    acc = [None] * JB
    for a in range(7):
        taps = [spread[a * 7 + b, :, lanes] for b in range(7)]
        for t in range(JB + 6):
            x = shifted[a, first + t, :, lanes]
            for b in range(7):
                o = t - b
                if 0 <= o < JB:
                    term = x * taps[b]
                    acc[o] = term if acc[o] is None else acc[o] + term
    return acc


def fold(x):
    return jnp.sum(x.reshape(-1, 8, C), axis=0)


def main_kernel(
    core, own, left, right, rows, grad, dww, dwb, gain, lnb, w_in, w_in_t, b_in, w_out_t, b_out, scale,
    dconv_out, keep, send,
    tall, shifted, spread, conv, normed, inv, lnout, lnout_t, grad_flat, grad_t, pre, dact, act, dpre, dcw, small,
    pay,
):
    shift_rows(core, own, left, right, rows, tall, shifted)
    spread_weights(dww, spread)

    def normalize(n):
        first = n * JB
        block = conv[pl.ds(first, JB)].reshape(JB * 8, C) + dwb[...]
        center = block - jnp.mean(block, axis=-1, keepdims=True)
        inverse = lax.rsqrt(jnp.mean(center * center, axis=-1, keepdims=True) + eps_norm)
        norm = center * inverse
        at = pl.ds(pl.multiple_of(first * 8, 64), JB * 8)
        normed[at, :] = norm
        inv[at, :] = inverse
        lnout[at, :] = (norm * gain[...] + lnb[...]).astype(BF16)

    def convolve(n):
        first = n * JB
        for lane in range(2):
            lanes = slice(lane * 128, lane * 128 + 128)
            for o, acc in enumerate(conv_block(shifted, spread, first, lane)):
                conv[first + o, :, lanes] = acc
        for o in range(JB):
            at = pl.multiple_of((first + o) * C, C)
            g = grad[:, pl.ds(at, C)].astype(F32)
            grad_flat[pl.ds(pl.multiple_of((first + o) * 8, 8), 8), :] = g

    def forward(n, carry):
        normalize(n - 1)
        convolve(n)
        return carry

    convolve(0)
    lax.fori_loop(1, COLS // JB, forward, 0, unroll=3)
    normalize(COLS // JB - 1)

    CH = 256

    def mlp(n, carry):
        s_gain, s_lnb, s_g, s_dwb = carry
        rows = pl.ds(pl.multiple_of(n * CH, CH), CH)
        ln = lnout[rows, :]
        lnout_t[n, 0:C, :] = ln.astype(F32).T.astype(BF16)
        g = grad_flat[rows, :]
        grad_t[n] = g.T.astype(BF16)
        pre[...] = jnp.dot(ln, w_in[...], preferred_element_type=F32) + b_in[...]
        dbr = (g * scale[...]).astype(BF16)
        dact[...] = jnp.dot(dbr, w_out_t[...], preferred_element_type=F32)
        s_g = s_g + fold(g)

        def gelu(m, c):
            sub = pl.ds(pl.multiple_of(m * 16, 16), 16)
            out = pl.ds(pl.multiple_of(n * CH + m * 16, 16), 16)
            for q in range(4):
                lanes = slice(q * 256, q * 256 + 256)
                v = pre[sub, lanes]
                e = jnp.exp2(v * v * (-0.5 / math.log(2.0)))
                d = 1.0 + (0.3275911 / math.sqrt(2.0)) * jnp.abs(v)
                t = pl.reciprocal(d, approx=True)
                t = t * (2.0 - d * t)
                poly = 0.5 * 1.061405429 * t - 0.5 * 1.453152027
                poly = poly * t + 0.5 * 1.421413741
                poly = poly * t - 0.5 * 0.284496736
                poly = poly * t + 0.5 * 0.254829592
                tail = poly * t * e
                cdf = jnp.where(v < 0.0, tail, 1.0 - tail)
                act[out, lanes] = (v * cdf).astype(BF16)
                slope = cdf + v * (e * (1.0 / math.sqrt(2.0 * math.pi)))
                dpre[out, lanes] = (dact[sub, lanes] * slope).astype(BF16)
            return c

        lax.fori_loop(0, CH // 16, gelu, 0, unroll=4)
        dact[:, 0:C] = jnp.dot(dpre[rows, :], w_in_t[...], preferred_element_type=F32)

        def back(m, c):
            s_gain, s_lnb, s_dwb = c
            sub = pl.ds(pl.multiple_of(m * 64, 64), 64)
            out = pl.ds(pl.multiple_of(n * CH + m * 64, 64), 64)
            dln = dact[sub, 0:C]
            norm = normed[out, :]
            prod = dln * norm
            s_gain = s_gain + fold(prod)
            s_lnb = s_lnb + fold(dln)
            dn = dln * gain[...]
            m1 = jnp.mean(dn, axis=-1, keepdims=True)
            m2 = jnp.mean(dn * norm, axis=-1, keepdims=True)
            dc = ((dn - m1 - norm * m2) * inv[out, :]).astype(BF16)
            wide = dc.astype(F32)
            s_dwb = s_dwb + fold(wide)
            wide = wide.reshape(8, 8, C)
            j0 = n * (CH // 8) + m * 8
            dcw[pl.ds(j0, 8)] = wide
            for o in range(8):
                dconv_out[:, pl.ds(pl.multiple_of((j0 + o) * C, C), C)] = wide[o].astype(BF16)
            return s_gain, s_lnb, s_dwb

        s_gain, s_lnb, s_dwb = lax.fori_loop(0, CH // 64, back, (s_gain, s_lnb, s_dwb), unroll=4)
        return s_gain, s_lnb, s_g, s_dwb

    for n in range(PIX // CH):
        lnout_t[n, C:, :] = jnp.ones((16, CH), BF16)
    zero = jnp.zeros((8, C), F32)
    s_gain, s_lnb, s_g, s_dwb = lax.fori_loop(0, PIX // CH, mlp, (zero, zero, zero, zero))

    small[...] = jnp.zeros_like(small)
    down = lambda v: jnp.sum(v, axis=0, keepdims=True)
    sum_g = down(s_g)
    small[49:50, :] = down(s_dwb)
    small[50:51, :] = down(s_gain)
    small[51:52, :] = down(s_lnb)
    small[52:53, :] = sum_g * scale[...]

    s_scale = jnp.zeros((C, 1), F32)
    for q in range(4):
        lanes = slice(q * 256, q * 256 + 256)
        total = jnp.zeros((C + 16, 256), F32)
        for n in range(PIX // CH):
            part = slice(n * CH, (n + 1) * CH)
            total = total + jnp.dot(lnout_t[n], dpre[part, lanes], preferred_element_type=F32)
        small[54 + q : 55 + q, :] = total[C : C + 1]
        pay[0, q * 4 : q * 4 + 4] = total[0:C].reshape(4, 64, C)
    for q in range(4):
        lanes = slice(q * 256, q * 256 + 256)
        total = jnp.zeros((C, 256), F32)
        for n in range(PIX // CH):
            part = slice(n * CH, (n + 1) * CH)
            total = total + jnp.dot(grad_t[n], act[part, lanes], preferred_element_type=F32)
        s_scale = s_scale + jnp.sum(total * w_out_t[:, lanes].astype(F32), axis=1, keepdims=True)
        pay[1, q * 4 : q * 4 + 4] = (total.T * scale[...]).reshape(4, 64, C)
    wide_scale = jnp.broadcast_to(s_scale, (C, 128)).T
    small[53:54, :] = wide_scale[0:1, :] + b_out[...] * sum_g

    for lane in range(2):
        lanes = slice(lane * 128, lane * 128 + 128)
        for group in ((0, 1, 2), (3, 4), (5, 6)):

            def taps(n, acc, group=group, lanes=lanes):
                first = n * JB
                d = [dcw[first + o, :, lanes] for o in range(JB)]
                acc = list(acc)
                for p, a in enumerate(group):
                    for t in range(JB + 6):
                        x = shifted[a, first + t, :, lanes]
                        for b in range(7):
                            o = t - b
                            if 0 <= o < JB:
                                acc[p * 7 + b] = acc[p * 7 + b] + d[o] * x
                return tuple(acc)

            none = jnp.zeros((8, 128), F32)
            acc = lax.fori_loop(0, COLS // JB, taps, (none,) * (7 * len(group)))
            for p, a in enumerate(group):
                for b in range(7):
                    k = a * 7 + b
                    small[k : k + 1, lanes] = down(acc[p * 7 + b])

    even = core[0] == 0
    for k in range(16):
        rest = small[k * 8 : k * 8 + 8, :] if k < 8 else jnp.zeros((8, C), F32)
        none = jnp.zeros((8, C), F32)
        for out, half, first in ((keep, core[0], even), (send, 1 - core[0], jnp.logical_not(even))):
            extra = jnp.where(first, rest, none)
            out[k] = jnp.concatenate([pay[half, k], extra], axis=0).astype(BF16)


def transposed_kernel(
    core, own, left, right, rows, grad, dww, out, tall, shifted, spread
):
    shift_rows(core, own, left, right, rows, tall, shifted)
    spread_weights(dww, spread)

    def step(n, carry):
        first = n * JB
        for lane in range(2):
            for o, acc in enumerate(conv_block(shifted, spread, first, lane)):
                at = pl.ds(pl.multiple_of((first + o) * C + lane * 128, 128), 128)
                out[:, at] = (acc + grad[:, at].astype(F32)).astype(BF16)
        return carry

    lax.fori_loop(0, COLS // JB, step, 0)


def finish_kernel(
    core, mine, other, o_dw, o_dwb, o_gain, o_lnb, o_win, o_bin, o_wout, o_bout, o_scale, small, win, wout
):
    even = core[0] == 0
    total = jnp.zeros((8, 256), F32)
    for k in range(16):
        a, b = mine[k].astype(F32), other[k].astype(F32)
        first, second = jnp.where(even, a, b), jnp.where(even, b, a)
        squares = first[0:64] * first[0:64] + second[0:64] * second[0:64]
        total = total + jnp.sum(squares.reshape(8, 8, C), axis=0)
        q, part = k // 4, k % 4
        win[part * 64 : part * 64 + 64, q * 256 : q * 256 + 256] = first[0:64]
        wout[k * 64 : k * 64 + 64, :] = second[0:64]
        if k < 8:
            small[k * 8 : k * 8 + 8, :] = first[64:72]
    rest = small[...]
    total = total + jnp.sum((rest * rest).reshape(8, 8, C), axis=0)
    squares = jnp.sum(jnp.sum(total, axis=1, keepdims=True), axis=0, keepdims=True)
    factor = jnp.minimum(1.0, clip_bound / jnp.sqrt(squares))
    o_win[...] = win[...] * factor
    o_wout[...] = wout[...] * factor
    o_dw[...] = small[0:49, :] * factor
    o_dwb[...] = small[49:50, :] * factor
    o_gain[...] = small[50:51, :] * factor
    o_lnb[...] = small[51:52, :] * factor
    o_bout[...] = small[52:53, :] * factor
    o_scale[...] = small[53:54, :] * factor
    for q in range(4):
        o_bin[:, q * 256 : q * 256 + 256] = small[54 + q : 55 + q, :] * factor


CONV_SCRATCH = (
    pltpu.VMEM((WIDE, 24, C), F32),
    pltpu.VMEM((7, WIDE, 8, C), F32),
    pltpu.VMEM((49, 8, C), F32),
)


def run_main(*operands):
    return pl.pallas_call(
        main_kernel,
        out_shape=(
            jax.ShapeDtypeStruct((ROWS, COLS * C), BF16),
            jax.ShapeDtypeStruct((16, 72, C), BF16),
            jax.ShapeDtypeStruct((16, 72, C), BF16),
        ),
        in_specs=[pl.BlockSpec(memory_space=pltpu.SMEM)]
        + [pl.BlockSpec(memory_space=pltpu.VMEM)] * (len(operands) - 1),
        scratch_shapes=CONV_SCRATCH
        + (
            pltpu.VMEM((COLS, 8, C), F32),
            pltpu.VMEM((PIX, C), F32),
            pltpu.VMEM((PIX, 1), F32),
            pltpu.VMEM((PIX, C), BF16),
            pltpu.VMEM((4, C + 16, 256), BF16),
            pltpu.VMEM((PIX, C), F32),
            pltpu.VMEM((4, C, 256), BF16),
            pltpu.VMEM((256, HID), F32),
            pltpu.VMEM((256, HID), F32),
            pltpu.VMEM((PIX, HID), BF16),
            pltpu.VMEM((PIX, HID), BF16),
            pltpu.VMEM((COLS, 8, C), F32),
            pltpu.VMEM((64, C), F32),
            pltpu.VMEM((2, 16, 64, C), F32),
        ),
        compiler_params=pltpu.CompilerParams(vmem_limit_bytes=40 * MIB),
        name="block_backward",
    )(*operands)


def run_transposed(*operands):
    return pl.pallas_call(
        transposed_kernel,
        out_shape=jax.ShapeDtypeStruct((ROWS, COLS * C), BF16),
        in_specs=[pl.BlockSpec(memory_space=pltpu.SMEM)]
        + [pl.BlockSpec(memory_space=pltpu.VMEM)] * (len(operands) - 1),
        scratch_shapes=CONV_SCRATCH,
        compiler_params=pltpu.CompilerParams(vmem_limit_bytes=20 * MIB),
        cost_estimate=pl.CostEstimate(flops=200_000_000, bytes_accessed=40 * MIB, transcendentals=0),
        name="transposed_conv",
    )(*operands)


def run_finish(core, mine, other):
    vec = jax.ShapeDtypeStruct((1, C), F32)
    vmem = pl.BlockSpec(memory_space=pltpu.VMEM)
    return pl.pallas_call(
        finish_kernel,
        in_specs=[pl.BlockSpec(memory_space=pltpu.SMEM), vmem, vmem],
        out_shape=(
            jax.ShapeDtypeStruct((49, C), F32), vec, vec, vec, jax.ShapeDtypeStruct((C, HID), F32),
            jax.ShapeDtypeStruct((1, HID), F32), jax.ShapeDtypeStruct((HID, C), F32), vec, vec,
        ),
        scratch_shapes=(
            pltpu.VMEM((64, C), F32), pltpu.VMEM((C, HID), F32), pltpu.VMEM((HID, C), F32),
        ),
        compiler_params=pltpu.CompilerParams(vmem_limit_bytes=16 * MIB),
        name="clip",
    )(core, mine, other)


def pair_swaps(n):
    inner = [(i, i ^ 1) for i in range(n)]
    outer = [(i, i + 1 if i % 2 else i - 1) for i in range(1, n - 1)]
    return inner, outer


def halo(x, core, beside_columns=None, beside_rows=None):
    inner, outer = pair_swaps(lax.axis_size("wa"))
    even = lax.rem(lax.axis_index("wa"), 2) == 0
    first, last = x[:, : 3 * C], x[:, -3 * C :]
    near = lax.ppermute(jnp.where(even, last, first), "wa", inner)
    far = lax.ppermute(jnp.where(even, first, last), "wa", outer)
    if beside_columns is not None:
        near, far, _ = lax.optimization_barrier((near, far, beside_columns))
    left, right = jnp.where(even, far, near), jnp.where(even, near, far)
    inner, outer = pair_swaps(lax.axis_size("ha"))
    even = core[0] == 0
    last = jnp.concatenate([left[5:], x[5:], right[5:]], axis=1)
    lead = jnp.concatenate([left[:3], x[:3], right[:3]], axis=1)
    crossed = lax.ppermute(jnp.where(even, lead, last), "ha", outer)
    swapped = lax.ppermute(jnp.where(even, last, lead), "ha", inner)
    if beside_rows is not None:
        crossed, swapped, _ = lax.optimization_barrier((crossed, swapped, beside_rows))
    return left, right, jnp.concatenate([crossed, swapped], axis=0)


def plane_and_line():
    wide, pairs = lax.axis_size("wa"), lax.axis_size("ha") // 2
    depth = pairs // 2
    at = lambda x, z, c, w: ((x * depth + z) * 2 + c) * wide + w
    plane = [
        [at(x, z, c, w) for x in range(2) for w in range(wide)]
        for z in range(depth)
        for c in range(2)
    ]
    line = [
        [at(x, z, c, w) for z in range(depth)]
        for x in range(2)
        for w in range(wide)
        for c in range(2)
    ]
    return plane, line


def on_device(
    features, grad_out, dw_weight, dw_bias, ln_gain, ln_bias, w_in, b_in, w_out, b_out, scale
):
    row = lambda v: v.reshape(1, -1)
    core = lax.rem(lax.axis_index("ha"), 2).reshape(1).astype(jnp.int32)
    swap, _ = pair_swaps(lax.axis_size("ha"))
    plane, line = plane_and_line()

    def exchange(x, groups):
        return lax.all_to_all(x, ("ha", "wa"), 0, 0, axis_index_groups=groups, tiled=True)

    dconv, keep, send = run_main(
        core, features, *halo(features, core), grad_out, dw_weight, row(dw_bias), row(ln_gain),
        row(ln_bias), w_in, w_in.T, row(b_in), w_out.T, row(b_out), row(scale),
    )
    half = (keep.astype(F32) + lax.ppermute(send, "ha", swap).astype(F32)).astype(BF16)
    half, dconv = lax.optimization_barrier((half, dconv))
    add_up = lambda v: jnp.sum(v.astype(F32), axis=0).astype(BF16)
    repeat = lambda v, n: jnp.broadcast_to(v[None], (n,) + v.shape)
    terms = exchange(half, plane)
    sums = exchange(repeat(add_up(terms), len(line[0])), line)
    edges = halo(dconv, core, terms, sums)
    total = add_up(sums)
    total, edges = lax.optimization_barrier((total, edges))
    mine = exchange(repeat(total, len(plane[0])), plane)
    grad_features = run_transposed(core, dconv, *edges, grad_out, dw_weight[::-1])
    mine, grad_features = lax.optimization_barrier((mine, grad_features))
    other = lax.ppermute(mine, "ha", swap)
    o_dw, o_dwb, o_gain, o_lnb, o_win, o_bin, o_wout, o_bout, o_scale = run_finish(
        core, mine, other
    )
    flat = lambda v: v.reshape(-1)
    return (
        grad_features, o_dw, flat(o_dwb), flat(o_gain), flat(o_lnb), o_win, flat(o_bin), o_wout,
        flat(o_bout), flat(o_scale),
    )


def solution(mesh):
    return jax.shard_map(
        on_device,
        mesh=mesh,
        in_specs=(P("ha", "wa"), P("ha", "wa"), P(), P(), P(), P(), P(), P(), P(), P(), P()),
        out_specs=(P("ha", "wa"), P(), P(), P(), P(), P(), P(), P(), P(), P()),
        check_vma=False,
    )
```

```python
import math

import jax
import jax.numpy as jnp
from jax import lax
from jax.experimental import pallas as pl
from jax.experimental.pallas import tpu as pltpu
from jax.sharding import PartitionSpec as P

eps_norm = 1e-06
clip_bound = 500.0
F32, BF16 = jnp.float32, jnp.bfloat16
ROWS, COLS, C, HID = 8, 128, 256, 1024
PIX = ROWS * COLS
WIDE = COLS + 6
JB = 8
MIB = 1024 * 1024


def shift_rows(core, own, left, right, rows, tall, shifted):
    even = core[0] == 0

    def place(j, mid, at):
        edge = rows[:, pl.ds(at, C)].astype(F32)
        crossed, swapped = edge[0:3], edge[3:6]
        tall[j, 8:16, :] = mid.astype(F32)
        tall[j, 5:8, :] = jnp.where(even, crossed, swapped)
        tall[j, 16:19, :] = jnp.where(even, swapped, crossed)
        for a in range(7):
            shifted[a, j] = tall[j, 5 + a : 13 + a, :]

    for k in range(3):
        place(k, left[:, k * C : (k + 1) * C], k * C)
        place(COLS + 3 + k, right[:, k * C : (k + 1) * C], (COLS + 3 + k) * C)

    def step(j, carry):
        mid = own[:, pl.ds(pl.multiple_of(j * C, C), C)]
        place(j + 3, mid, pl.multiple_of((j + 3) * C, C))
        return carry

    lax.fori_loop(0, COLS, step, 0, unroll=4)


def spread_weights(w_ref, spread):
    for k in range(49):
        spread[k] = jnp.broadcast_to(w_ref[k : k + 1, :], (8, C))


def conv_block(shifted, spread, first, lane):
    lanes = slice(lane * 128, lane * 128 + 128)
    acc = [None] * JB
    for a in range(7):
        taps = [spread[a * 7 + b, :, lanes] for b in range(7)]
        for t in range(JB + 6):
            x = shifted[a, first + t, :, lanes]
            for b in range(7):
                o = t - b
                if 0 <= o < JB:
                    term = x * taps[b]
                    acc[o] = term if acc[o] is None else acc[o] + term
    return acc


def fold(x):
    return jnp.sum(x.reshape(-1, 8, C), axis=0)


def main_kernel(
    core, own, left, right, rows, grad_t, dact, sum_g8, dww, dwb, gain, lnb, w_in, w_in_t, b_in, w_out_t, b_out, scale,
    dconv_out, keep, send,
    tall, shifted, spread, conv, normed, inv, lnout, lnout_t, pre, back_in, act, dpre, dcw, small,
    pay,
):
    shift_rows(core, own, left, right, rows, tall, shifted)
    spread_weights(dww, spread)

    def normalize(n):
        first = n * JB
        block = conv[pl.ds(first, JB)].reshape(JB * 8, C) + dwb[...]
        center = block - jnp.mean(block, axis=-1, keepdims=True)
        inverse = lax.rsqrt(jnp.mean(center * center, axis=-1, keepdims=True) + eps_norm)
        norm = center * inverse
        at = pl.ds(pl.multiple_of(first * 8, 64), JB * 8)
        normed[at, :] = norm
        inv[at, :] = inverse
        lnout[at, :] = (norm * gain[...] + lnb[...]).astype(BF16)

    def convolve(n):
        first = n * JB
        for lane in range(2):
            lanes = slice(lane * 128, lane * 128 + 128)
            for o, acc in enumerate(conv_block(shifted, spread, first, lane)):
                conv[first + o, :, lanes] = acc

    def forward(n, carry):
        normalize(n - 1)
        convolve(n)
        return carry

    convolve(0)
    lax.fori_loop(1, COLS // JB, forward, 0, unroll=3)
    normalize(COLS // JB - 1)

    CH = 256

    def mlp(n, carry):
        s_gain, s_lnb, s_dwb = carry
        rows = pl.ds(pl.multiple_of(n * CH, CH), CH)
        ln = lnout[rows, :]
        lnout_t[n, 0:C, :] = ln.astype(F32).T.astype(BF16)
        pre[...] = jnp.dot(ln, w_in[...], preferred_element_type=F32) + b_in[...]

        def gelu(m, c):
            sub = pl.ds(pl.multiple_of(m * 16, 16), 16)
            out = pl.ds(pl.multiple_of(n * CH + m * 16, 16), 16)
            for q in range(4):
                lanes = slice(q * 256, q * 256 + 256)
                v = pre[sub, lanes]
                e = jnp.exp2(v * v * (-0.5 / math.log(2.0)))
                d = 1.0 + (0.3275911 / math.sqrt(2.0)) * jnp.abs(v)
                t = pl.reciprocal(d, approx=True)
                t = t * (2.0 - d * t)
                poly = 0.5 * 1.061405429 * t - 0.5 * 1.453152027
                poly = poly * t + 0.5 * 1.421413741
                poly = poly * t - 0.5 * 0.284496736
                poly = poly * t + 0.5 * 0.254829592
                tail = poly * t * e
                cdf = jnp.where(v < 0.0, tail, 1.0 - tail)
                act[out, lanes] = (v * cdf).astype(BF16)
                slope = cdf + v * (e * (1.0 / math.sqrt(2.0 * math.pi)))
                dpre[out, lanes] = (dact[out, lanes] * slope).astype(BF16)
            return c

        lax.fori_loop(0, CH // 16, gelu, 0, unroll=4)
        back_in[...] = jnp.dot(dpre[rows, :], w_in_t[...], preferred_element_type=F32)

        def back(m, c):
            s_gain, s_lnb, s_dwb = c
            sub = pl.ds(pl.multiple_of(m * 64, 64), 64)
            out = pl.ds(pl.multiple_of(n * CH + m * 64, 64), 64)
            dln = back_in[sub, :]
            norm = normed[out, :]
            prod = dln * norm
            s_gain = s_gain + fold(prod)
            s_lnb = s_lnb + fold(dln)
            dn = dln * gain[...]
            m1 = jnp.mean(dn, axis=-1, keepdims=True)
            m2 = jnp.mean(dn * norm, axis=-1, keepdims=True)
            dc = ((dn - m1 - norm * m2) * inv[out, :]).astype(BF16)
            wide = dc.astype(F32)
            s_dwb = s_dwb + fold(wide)
            wide = wide.reshape(8, 8, C)
            j0 = n * (CH // 8) + m * 8
            dcw[pl.ds(j0, 8)] = wide
            for o in range(8):
                dconv_out[:, pl.ds(pl.multiple_of((j0 + o) * C, C), C)] = wide[o].astype(BF16)
            return s_gain, s_lnb, s_dwb

        s_gain, s_lnb, s_dwb = lax.fori_loop(0, CH // 64, back, (s_gain, s_lnb, s_dwb), unroll=4)
        return s_gain, s_lnb, s_dwb

    for n in range(PIX // CH):
        lnout_t[n, C:, :] = jnp.ones((16, CH), BF16)
    zero = jnp.zeros((8, C), F32)
    s_gain, s_lnb, s_dwb = lax.fori_loop(0, PIX // CH, mlp, (zero, zero, zero))

    small[...] = jnp.zeros_like(small)
    down = lambda v: jnp.sum(v, axis=0, keepdims=True)
    sum_g = down(sum_g8[...])
    small[49:50, :] = down(s_dwb)
    small[50:51, :] = down(s_gain)
    small[51:52, :] = down(s_lnb)
    small[52:53, :] = sum_g * scale[...]

    s_scale = jnp.zeros((C, 1), F32)
    for q in range(4):
        lanes = slice(q * 256, q * 256 + 256)
        total = jnp.zeros((C + 16, 256), F32)
        for n in range(PIX // CH):
            part = slice(n * CH, (n + 1) * CH)
            total = total + jnp.dot(lnout_t[n], dpre[part, lanes], preferred_element_type=F32)
        small[54 + q : 55 + q, :] = total[C : C + 1]
        pay[0, q * 4 : q * 4 + 4] = total[0:C].reshape(4, 64, C)
    for q in range(4):
        lanes = slice(q * 256, q * 256 + 256)
        total = jnp.zeros((C, 256), F32)
        for n in range(PIX // CH):
            part = slice(n * CH, (n + 1) * CH)
            total = total + jnp.dot(grad_t[n], act[part, lanes], preferred_element_type=F32)
        s_scale = s_scale + jnp.sum(total * w_out_t[:, lanes].astype(F32), axis=1, keepdims=True)
        pay[1, q * 4 : q * 4 + 4] = (total.T * scale[...]).reshape(4, 64, C)
    wide_scale = jnp.broadcast_to(s_scale, (C, 128)).T
    small[53:54, :] = wide_scale[0:1, :] + b_out[...] * sum_g

    for lane in range(2):
        lanes = slice(lane * 128, lane * 128 + 128)
        for group in ((0, 1, 2), (3, 4), (5, 6)):

            def taps(n, acc, group=group, lanes=lanes):
                first = n * JB
                d = [dcw[first + o, :, lanes] for o in range(JB)]
                acc = list(acc)
                for p, a in enumerate(group):
                    for t in range(JB + 6):
                        x = shifted[a, first + t, :, lanes]
                        for b in range(7):
                            o = t - b
                            if 0 <= o < JB:
                                acc[p * 7 + b] = acc[p * 7 + b] + d[o] * x
                return tuple(acc)

            none = jnp.zeros((8, 128), F32)
            acc = lax.fori_loop(0, COLS // JB, taps, (none,) * (7 * len(group)))
            for p, a in enumerate(group):
                for b in range(7):
                    k = a * 7 + b
                    small[k : k + 1, lanes] = down(acc[p * 7 + b])

    even = core[0] == 0
    for k in range(16):
        rest = small[k * 8 : k * 8 + 8, :] if k < 8 else jnp.zeros((8, C), F32)
        none = jnp.zeros((8, C), F32)
        for out, half, first in ((keep, core[0], even), (send, 1 - core[0], jnp.logical_not(even))):
            extra = jnp.where(first, rest, none)
            out[k] = jnp.concatenate([pay[half, k], extra], axis=0).astype(BF16)


def prepare_kernel(grad, w_out_t, scale, grad_t, dact, sum_g8, flat):
    def step(n, total):
        for o in range(32):
            at = pl.multiple_of((n * 32 + o) * C, C)
            flat[o * 8 : o * 8 + 8, :] = grad[:, pl.ds(at, C)].astype(F32)
        g = flat[...]
        grad_t[n] = g.T.astype(BF16)
        branch = (g * scale[...]).astype(BF16)
        rows = pl.ds(pl.multiple_of(n * 256, 256), 256)
        dact[rows, :] = jnp.dot(branch, w_out_t[...], preferred_element_type=F32)
        return total + fold(g)

    sum_g8[...] = lax.fori_loop(0, PIX // 256, step, jnp.zeros((8, C), F32))


def transposed_kernel(
    core, own, left, right, rows, grad, dww, out, tall, shifted, spread
):
    shift_rows(core, own, left, right, rows, tall, shifted)
    spread_weights(dww, spread)

    def step(n, carry):
        first = n * JB
        for lane in range(2):
            for o, acc in enumerate(conv_block(shifted, spread, first, lane)):
                at = pl.ds(pl.multiple_of((first + o) * C + lane * 128, 128), 128)
                out[:, at] = (acc + grad[:, at].astype(F32)).astype(BF16)
        return carry

    lax.fori_loop(0, COLS // JB, step, 0)


def finish_kernel(
    core, mine, other, o_dw, o_dwb, o_gain, o_lnb, o_win, o_bin, o_wout, o_bout, o_scale, small, win, wout
):
    even = core[0] == 0
    total = jnp.zeros((8, 256), F32)
    for k in range(16):
        a, b = mine[k].astype(F32), other[k].astype(F32)
        first, second = jnp.where(even, a, b), jnp.where(even, b, a)
        squares = first[0:64] * first[0:64] + second[0:64] * second[0:64]
        total = total + jnp.sum(squares.reshape(8, 8, C), axis=0)
        q, part = k // 4, k % 4
        win[part * 64 : part * 64 + 64, q * 256 : q * 256 + 256] = first[0:64]
        wout[k * 64 : k * 64 + 64, :] = second[0:64]
        if k < 8:
            small[k * 8 : k * 8 + 8, :] = first[64:72]
    rest = small[...]
    total = total + jnp.sum((rest * rest).reshape(8, 8, C), axis=0)
    squares = jnp.sum(jnp.sum(total, axis=1, keepdims=True), axis=0, keepdims=True)
    factor = jnp.minimum(1.0, clip_bound / jnp.sqrt(squares))
    o_win[...] = win[...] * factor
    o_wout[...] = wout[...] * factor
    o_dw[...] = small[0:49, :] * factor
    o_dwb[...] = small[49:50, :] * factor
    o_gain[...] = small[50:51, :] * factor
    o_lnb[...] = small[51:52, :] * factor
    o_bout[...] = small[52:53, :] * factor
    o_scale[...] = small[53:54, :] * factor
    for q in range(4):
        o_bin[:, q * 256 : q * 256 + 256] = small[54 + q : 55 + q, :] * factor


CONV_SCRATCH = (
    pltpu.VMEM((WIDE, 24, C), F32),
    pltpu.VMEM((7, WIDE, 8, C), F32),
    pltpu.VMEM((49, 8, C), F32),
)


def run_main(*operands):
    return pl.pallas_call(
        main_kernel,
        out_shape=(
            jax.ShapeDtypeStruct((ROWS, COLS * C), BF16),
            jax.ShapeDtypeStruct((16, 72, C), BF16),
            jax.ShapeDtypeStruct((16, 72, C), BF16),
        ),
        in_specs=[pl.BlockSpec(memory_space=pltpu.SMEM)]
        + [pl.BlockSpec(memory_space=pltpu.VMEM)] * (len(operands) - 1),
        scratch_shapes=CONV_SCRATCH
        + (
            pltpu.VMEM((COLS, 8, C), F32),
            pltpu.VMEM((PIX, C), F32),
            pltpu.VMEM((PIX, 1), F32),
            pltpu.VMEM((PIX, C), BF16),
            pltpu.VMEM((4, C + 16, 256), BF16),
            pltpu.VMEM((256, HID), F32),
            pltpu.VMEM((256, C), F32),
            pltpu.VMEM((PIX, HID), BF16),
            pltpu.VMEM((PIX, HID), BF16),
            pltpu.VMEM((COLS, 8, C), F32),
            pltpu.VMEM((64, C), F32),
            pltpu.VMEM((2, 16, 64, C), F32),
        ),
        compiler_params=pltpu.CompilerParams(vmem_limit_bytes=30 * MIB),
        name="block_backward",
    )(*operands)


def run_prepare(*operands):
    return pl.pallas_call(
        prepare_kernel,
        out_shape=(
            jax.ShapeDtypeStruct((PIX // 256, C, 256), BF16),
            jax.ShapeDtypeStruct((PIX, HID), F32),
            jax.ShapeDtypeStruct((8, C), F32),
        ),
        scratch_shapes=(pltpu.VMEM((256, C), F32),),
        compiler_params=pltpu.CompilerParams(vmem_limit_bytes=10 * MIB),
        cost_estimate=pl.CostEstimate(flops=600_000_000, bytes_accessed=8 * MIB, transcendentals=0),
        name="prepare",
    )(*operands)


def run_transposed(*operands):
    return pl.pallas_call(
        transposed_kernel,
        out_shape=jax.ShapeDtypeStruct((ROWS, COLS * C), BF16),
        in_specs=[pl.BlockSpec(memory_space=pltpu.SMEM)]
        + [pl.BlockSpec(memory_space=pltpu.VMEM)] * (len(operands) - 1),
        scratch_shapes=CONV_SCRATCH,
        compiler_params=pltpu.CompilerParams(vmem_limit_bytes=20 * MIB),
        cost_estimate=pl.CostEstimate(flops=200_000_000, bytes_accessed=40 * MIB, transcendentals=0),
        name="transposed_conv",
    )(*operands)


def run_finish(core, mine, other):
    vec = jax.ShapeDtypeStruct((1, C), F32)
    vmem = pl.BlockSpec(memory_space=pltpu.VMEM)
    return pl.pallas_call(
        finish_kernel,
        in_specs=[pl.BlockSpec(memory_space=pltpu.SMEM), vmem, vmem],
        out_shape=(
            jax.ShapeDtypeStruct((49, C), F32), vec, vec, vec, jax.ShapeDtypeStruct((C, HID), F32),
            jax.ShapeDtypeStruct((1, HID), F32), jax.ShapeDtypeStruct((HID, C), F32), vec, vec,
        ),
        scratch_shapes=(
            pltpu.VMEM((64, C), F32), pltpu.VMEM((C, HID), F32), pltpu.VMEM((HID, C), F32),
        ),
        compiler_params=pltpu.CompilerParams(vmem_limit_bytes=16 * MIB),
        name="clip",
    )(core, mine, other)


def pair_swaps(n):
    inner = [(i, i ^ 1) for i in range(n)]
    outer = [(i, i + 1 if i % 2 else i - 1) for i in range(1, n - 1)]
    return inner, outer


def halo(x, core, beside_columns=None, beside_rows=None):
    inner, outer = pair_swaps(lax.axis_size("wa"))
    even = lax.rem(lax.axis_index("wa"), 2) == 0
    first, last = x[:, : 3 * C], x[:, -3 * C :]
    near = lax.ppermute(jnp.where(even, last, first), "wa", inner)
    far = lax.ppermute(jnp.where(even, first, last), "wa", outer)
    if beside_columns is not None:
        near, far, _ = lax.optimization_barrier((near, far, beside_columns))
    left, right = jnp.where(even, far, near), jnp.where(even, near, far)
    inner, outer = pair_swaps(lax.axis_size("ha"))
    even = core[0] == 0
    last = jnp.concatenate([left[5:], x[5:], right[5:]], axis=1)
    lead = jnp.concatenate([left[:3], x[:3], right[:3]], axis=1)
    crossed = lax.ppermute(jnp.where(even, lead, last), "ha", outer)
    swapped = lax.ppermute(jnp.where(even, last, lead), "ha", inner)
    if beside_rows is not None:
        crossed, swapped, _ = lax.optimization_barrier((crossed, swapped, beside_rows))
    return left, right, jnp.concatenate([crossed, swapped], axis=0)


def plane_and_line():
    wide, pairs = lax.axis_size("wa"), lax.axis_size("ha") // 2
    depth = pairs // 2
    at = lambda x, z, c, w: ((x * depth + z) * 2 + c) * wide + w
    plane = [
        [at(x, z, c, w) for x in range(2) for w in range(wide)]
        for z in range(depth)
        for c in range(2)
    ]
    line = [
        [at(x, z, c, w) for z in range(depth)]
        for x in range(2)
        for w in range(wide)
        for c in range(2)
    ]
    return plane, line


def on_device(
    features, grad_out, dw_weight, dw_bias, ln_gain, ln_bias, w_in, b_in, w_out, b_out, scale
):
    row = lambda v: v.reshape(1, -1)
    core = lax.rem(lax.axis_index("ha"), 2).reshape(1).astype(jnp.int32)
    swap, _ = pair_swaps(lax.axis_size("ha"))
    plane, line = plane_and_line()

    def exchange(x, groups):
        return lax.all_to_all(x, ("ha", "wa"), 0, 0, axis_index_groups=groups, tiled=True)

    prepared = run_prepare(grad_out, w_out.T, row(scale))
    dconv, keep, send = run_main(
        core, features, *halo(features, core), *prepared, dw_weight, row(dw_bias), row(ln_gain),
        row(ln_bias), w_in, w_in.T, row(b_in), w_out.T, row(b_out), row(scale),
    )
    half = (keep.astype(F32) + lax.ppermute(send, "ha", swap).astype(F32)).astype(BF16)
    half, dconv = lax.optimization_barrier((half, dconv))
    add_up = lambda v: jnp.sum(v.astype(F32), axis=0).astype(BF16)
    repeat = lambda v, n: jnp.broadcast_to(v[None], (n,) + v.shape)
    terms = exchange(half, plane)
    sums = exchange(repeat(add_up(terms), len(line[0])), line)
    edges = halo(dconv, core, terms, sums)
    total = add_up(sums)
    total, edges = lax.optimization_barrier((total, edges))
    mine = exchange(repeat(total, len(plane[0])), plane)
    grad_features = run_transposed(core, dconv, *edges, grad_out, dw_weight[::-1])
    mine, grad_features = lax.optimization_barrier((mine, grad_features))
    other = lax.ppermute(mine, "ha", swap)
    o_dw, o_dwb, o_gain, o_lnb, o_win, o_bin, o_wout, o_bout, o_scale = run_finish(
        core, mine, other
    )
    flat = lambda v: v.reshape(-1)
    return (
        grad_features, o_dw, flat(o_dwb), flat(o_gain), flat(o_lnb), o_win, flat(o_bin), o_wout,
        flat(o_bout), flat(o_scale),
    )


def solution(mesh):
    return jax.shard_map(
        on_device,
        mesh=mesh,
        in_specs=(P("ha", "wa"), P("ha", "wa"), P(), P(), P(), P(), P(), P(), P(), P(), P()),
        out_specs=(P("ha", "wa"), P(), P(), P(), P(), P(), P(), P(), P(), P()),
        check_vma=False,
    )
```

```python
import math

import jax
import jax.numpy as jnp
from jax import lax
from jax.experimental import pallas as pl
from jax.experimental.pallas import tpu as pltpu
from jax.sharding import PartitionSpec as P

eps_norm = 1e-06
clip_bound = 500.0
F32, BF16 = jnp.float32, jnp.bfloat16
ROWS, COLS, C, HID = 8, 128, 256, 1024
PIX = ROWS * COLS
WIDE = COLS + 6
JB = 8
MIB = 1024 * 1024


def shift_rows(core, own, left, right, rows, tall, shifted):
    even = core[0] == 0

    def place(j, mid, at):
        edge = rows[:, pl.ds(at, C)].astype(F32)
        crossed, swapped = edge[0:3], edge[3:6]
        tall[j, 8:16, :] = mid.astype(F32)
        tall[j, 5:8, :] = jnp.where(even, crossed, swapped)
        tall[j, 16:19, :] = jnp.where(even, swapped, crossed)
        for a in range(7):
            shifted[a, j] = tall[j, 5 + a : 13 + a, :]

    for k in range(3):
        place(k, left[:, k * C : (k + 1) * C], k * C)
        place(COLS + 3 + k, right[:, k * C : (k + 1) * C], (COLS + 3 + k) * C)

    def step(j, carry):
        mid = own[:, pl.ds(pl.multiple_of(j * C, C), C)]
        place(j + 3, mid, pl.multiple_of((j + 3) * C, C))
        return carry

    lax.fori_loop(0, COLS, step, 0, unroll=4)


def spread_weights(w_ref, spread):
    for k in range(49):
        spread[k] = jnp.broadcast_to(w_ref[k : k + 1, :], (8, C))


def conv_block(shifted, spread, first, lane):
    lanes = slice(lane * 128, lane * 128 + 128)
    acc = [None] * JB
    for a in range(7):
        taps = [spread[a * 7 + b, :, lanes] for b in range(7)]
        for t in range(JB + 6):
            x = shifted[a, first + t, :, lanes]
            for b in range(7):
                o = t - b
                if 0 <= o < JB:
                    term = x * taps[b]
                    acc[o] = term if acc[o] is None else acc[o] + term
    return acc


def fold(x):
    return jnp.sum(x.reshape(-1, 8, C), axis=0)


def main_kernel(
    core, own, left, right, rows, grad, dww, dwb, gain, lnb, w_in, w_in_t, b_in, w_out_t, b_out, scale,
    dconv_out, keep, send,
    tall, shifted, spread, conv, normed, inv, lnout, lnout_t, grad_flat, grad_t, pre, dact, act, dpre, dcw, small,
    pay,
):
    shift_rows(core, own, left, right, rows, tall, shifted)
    spread_weights(dww, spread)

    def normalize(n):
        first = n * JB
        block = conv[pl.ds(first, JB)].reshape(JB * 8, C) + dwb[...]
        center = block - jnp.mean(block, axis=-1, keepdims=True)
        inverse = lax.rsqrt(jnp.mean(center * center, axis=-1, keepdims=True) + eps_norm)
        norm = center * inverse
        at = pl.ds(pl.multiple_of(first * 8, 64), JB * 8)
        normed[at, :] = norm
        inv[at, :] = inverse
        lnout[at, :] = (norm * gain[...] + lnb[...]).astype(BF16)

    def convolve(n):
        first = n * JB
        for lane in range(2):
            lanes = slice(lane * 128, lane * 128 + 128)
            for o, acc in enumerate(conv_block(shifted, spread, first, lane)):
                conv[first + o, :, lanes] = acc
        for o in range(JB):
            at = pl.multiple_of((first + o) * C, C)
            g = grad[:, pl.ds(at, C)].astype(F32)
            grad_flat[pl.ds(pl.multiple_of((first + o) * 8, 8), 8), :] = g

    def forward(n, carry):
        normalize(n - 1)
        convolve(n)
        return carry

    convolve(0)
    lax.fori_loop(1, COLS // JB, forward, 0, unroll=5)
    normalize(COLS // JB - 1)

    CH = 256

    def mlp(n, carry):
        s_gain, s_lnb, s_g, s_dwb = carry
        rows = pl.ds(pl.multiple_of(n * CH, CH), CH)
        ln = lnout[rows, :]
        lnout_t[n, 0:C, :] = ln.astype(F32).T.astype(BF16)
        g = grad_flat[rows, :]
        grad_t[n] = g.T.astype(BF16)
        pre[...] = jnp.dot(ln, w_in[...], preferred_element_type=F32) + b_in[...]
        dbr = (g * scale[...]).astype(BF16)
        dact[...] = jnp.dot(dbr, w_out_t[...], preferred_element_type=F32)
        s_g = s_g + fold(g)

        def gelu(m, c):
            sub = pl.ds(pl.multiple_of(m * 16, 16), 16)
            out = pl.ds(pl.multiple_of(n * CH + m * 16, 16), 16)
            for q in range(4):
                lanes = slice(q * 256, q * 256 + 256)
                v = pre[sub, lanes]
                e = jnp.exp2(v * v * (-0.5 / math.log(2.0)))
                d = 1.0 + (0.3275911 / math.sqrt(2.0)) * jnp.abs(v)
                t = pl.reciprocal(d, approx=True)
                t = t * (2.0 - d * t)
                poly = 0.5 * 1.061405429 * t - 0.5 * 1.453152027
                poly = poly * t + 0.5 * 1.421413741
                poly = poly * t - 0.5 * 0.284496736
                poly = poly * t + 0.5 * 0.254829592
                tail = poly * t * e
                cdf = jnp.where(v < 0.0, tail, 1.0 - tail)
                act[out, lanes] = (v * cdf).astype(BF16)
                slope = cdf + v * (e * (1.0 / math.sqrt(2.0 * math.pi)))
                dpre[out, lanes] = (dact[sub, lanes] * slope).astype(BF16)
            return c

        lax.fori_loop(0, CH // 16, gelu, 0, unroll=16)
        dact[:, 0:C] = jnp.dot(dpre[rows, :], w_in_t[...], preferred_element_type=F32)

        def back(m, c):
            s_gain, s_lnb, s_dwb = c
            sub = pl.ds(pl.multiple_of(m * 64, 64), 64)
            out = pl.ds(pl.multiple_of(n * CH + m * 64, 64), 64)
            dln = dact[sub, 0:C]
            norm = normed[out, :]
            prod = dln * norm
            s_gain = s_gain + fold(prod)
            s_lnb = s_lnb + fold(dln)
            dn = dln * gain[...]
            m1 = jnp.mean(dn, axis=-1, keepdims=True)
            m2 = jnp.mean(dn * norm, axis=-1, keepdims=True)
            dc = ((dn - m1 - norm * m2) * inv[out, :]).astype(BF16)
            wide = dc.astype(F32)
            s_dwb = s_dwb + fold(wide)
            wide = wide.reshape(8, 8, C)
            j0 = n * (CH // 8) + m * 8
            dcw[pl.ds(j0, 8)] = wide
            for o in range(8):
                dconv_out[:, pl.ds(pl.multiple_of((j0 + o) * C, C), C)] = wide[o].astype(BF16)
            return s_gain, s_lnb, s_dwb

        s_gain, s_lnb, s_dwb = lax.fori_loop(0, CH // 64, back, (s_gain, s_lnb, s_dwb), unroll=4)
        return s_gain, s_lnb, s_g, s_dwb

    for n in range(PIX // CH):
        lnout_t[n, C:, :] = jnp.ones((16, CH), BF16)
    zero = jnp.zeros((8, C), F32)
    s_gain, s_lnb, s_g, s_dwb = lax.fori_loop(0, PIX // CH, mlp, (zero, zero, zero, zero), unroll=2)

    small[...] = jnp.zeros_like(small)
    down = lambda v: jnp.sum(v, axis=0, keepdims=True)
    sum_g = down(s_g)
    small[49:50, :] = down(s_dwb)
    small[50:51, :] = down(s_gain)
    small[51:52, :] = down(s_lnb)
    small[52:53, :] = sum_g * scale[...]

    s_scale = jnp.zeros((C, 1), F32)
    for q in range(4):
        lanes = slice(q * 256, q * 256 + 256)
        total = jnp.zeros((C + 16, 256), F32)
        for n in range(PIX // CH):
            part = slice(n * CH, (n + 1) * CH)
            total = total + jnp.dot(lnout_t[n], dpre[part, lanes], preferred_element_type=F32)
        small[54 + q : 55 + q, :] = total[C : C + 1]
        pay[0, q * 4 : q * 4 + 4] = total[0:C].reshape(4, 64, C)
    for q in range(4):
        lanes = slice(q * 256, q * 256 + 256)
        total = jnp.zeros((C, 256), F32)
        for n in range(PIX // CH):
            part = slice(n * CH, (n + 1) * CH)
            total = total + jnp.dot(grad_t[n], act[part, lanes], preferred_element_type=F32)
        s_scale = s_scale + jnp.sum(total * w_out_t[:, lanes].astype(F32), axis=1, keepdims=True)
        pay[1, q * 4 : q * 4 + 4] = (total.T * scale[...]).reshape(4, 64, C)
    wide_scale = jnp.broadcast_to(s_scale, (C, 128)).T
    small[53:54, :] = wide_scale[0:1, :] + b_out[...] * sum_g

    for lane in range(2):
        lanes = slice(lane * 128, lane * 128 + 128)
        for group in ((0, 1, 2), (3, 4), (5, 6)):

            def taps(n, acc, group=group, lanes=lanes):
                first = n * JB
                d = [dcw[first + o, :, lanes] for o in range(JB)]
                acc = list(acc)
                for p, a in enumerate(group):
                    for t in range(JB + 6):
                        x = shifted[a, first + t, :, lanes]
                        for b in range(7):
                            o = t - b
                            if 0 <= o < JB:
                                acc[p * 7 + b] = acc[p * 7 + b] + d[o] * x
                return tuple(acc)

            none = jnp.zeros((8, 128), F32)
            acc = lax.fori_loop(0, COLS // JB, taps, (none,) * (7 * len(group)), unroll=4)
            for p, a in enumerate(group):
                for b in range(7):
                    k = a * 7 + b
                    small[k : k + 1, lanes] = down(acc[p * 7 + b])

    even = core[0] == 0
    for k in range(16):
        rest = small[k * 8 : k * 8 + 8, :] if k < 8 else jnp.zeros((8, C), F32)
        none = jnp.zeros((8, C), F32)
        for out, half, first in ((keep, core[0], even), (send, 1 - core[0], jnp.logical_not(even))):
            extra = jnp.where(first, rest, none)
            out[k] = jnp.concatenate([pay[half, k], extra], axis=0).astype(BF16)


def transposed_kernel(
    core, own, left, right, rows, grad, dww, out, tall, shifted, spread
):
    shift_rows(core, own, left, right, rows, tall, shifted)
    spread_weights(dww, spread)

    def step(n, carry):
        first = n * JB
        for lane in range(2):
            for o, acc in enumerate(conv_block(shifted, spread, first, lane)):
                at = pl.ds(pl.multiple_of((first + o) * C + lane * 128, 128), 128)
                out[:, at] = (acc + grad[:, at].astype(F32)).astype(BF16)
        return carry

    lax.fori_loop(0, COLS // JB, step, 0)


def finish_kernel(
    core, mine, other, o_dw, o_dwb, o_gain, o_lnb, o_win, o_bin, o_wout, o_bout, o_scale, small, win, wout
):
    even = core[0] == 0
    total = jnp.zeros((8, 256), F32)
    for k in range(16):
        a, b = mine[k].astype(F32), other[k].astype(F32)
        first, second = jnp.where(even, a, b), jnp.where(even, b, a)
        squares = first[0:64] * first[0:64] + second[0:64] * second[0:64]
        total = total + jnp.sum(squares.reshape(8, 8, C), axis=0)
        q, part = k // 4, k % 4
        win[part * 64 : part * 64 + 64, q * 256 : q * 256 + 256] = first[0:64]
        wout[k * 64 : k * 64 + 64, :] = second[0:64]
        if k < 8:
            small[k * 8 : k * 8 + 8, :] = first[64:72]
    rest = small[...]
    total = total + jnp.sum((rest * rest).reshape(8, 8, C), axis=0)
    squares = jnp.sum(jnp.sum(total, axis=1, keepdims=True), axis=0, keepdims=True)
    factor = jnp.minimum(1.0, clip_bound / jnp.sqrt(squares))
    o_win[...] = win[...] * factor
    o_wout[...] = wout[...] * factor
    o_dw[...] = small[0:49, :] * factor
    o_dwb[...] = small[49:50, :] * factor
    o_gain[...] = small[50:51, :] * factor
    o_lnb[...] = small[51:52, :] * factor
    o_bout[...] = small[52:53, :] * factor
    o_scale[...] = small[53:54, :] * factor
    for q in range(4):
        o_bin[:, q * 256 : q * 256 + 256] = small[54 + q : 55 + q, :] * factor


CONV_SCRATCH = (
    pltpu.VMEM((WIDE, 24, C), F32),
    pltpu.VMEM((7, WIDE, 8, C), F32),
    pltpu.VMEM((49, 8, C), F32),
)


def run_main(*operands):
    return pl.pallas_call(
        main_kernel,
        out_shape=(
            jax.ShapeDtypeStruct((ROWS, COLS * C), BF16),
            jax.ShapeDtypeStruct((16, 72, C), BF16),
            jax.ShapeDtypeStruct((16, 72, C), BF16),
        ),
        in_specs=[pl.BlockSpec(memory_space=pltpu.SMEM)]
        + [pl.BlockSpec(memory_space=pltpu.VMEM)] * (len(operands) - 1),
        scratch_shapes=CONV_SCRATCH
        + (
            pltpu.VMEM((COLS, 8, C), F32),
            pltpu.VMEM((PIX, C), F32),
            pltpu.VMEM((PIX, 1), F32),
            pltpu.VMEM((PIX, C), BF16),
            pltpu.VMEM((4, C + 16, 256), BF16),
            pltpu.VMEM((PIX, C), F32),
            pltpu.VMEM((4, C, 256), BF16),
            pltpu.VMEM((256, HID), F32),
            pltpu.VMEM((256, HID), F32),
            pltpu.VMEM((PIX, HID), BF16),
            pltpu.VMEM((PIX, HID), BF16),
            pltpu.VMEM((COLS, 8, C), F32),
            pltpu.VMEM((64, C), F32),
            pltpu.VMEM((2, 16, 64, C), F32),
        ),
        compiler_params=pltpu.CompilerParams(vmem_limit_bytes=40 * MIB),
        name="block_backward",
    )(*operands)


def run_transposed(*operands):
    return pl.pallas_call(
        transposed_kernel,
        out_shape=jax.ShapeDtypeStruct((ROWS, COLS * C), BF16),
        in_specs=[pl.BlockSpec(memory_space=pltpu.SMEM)]
        + [pl.BlockSpec(memory_space=pltpu.VMEM)] * (len(operands) - 1),
        scratch_shapes=CONV_SCRATCH,
        compiler_params=pltpu.CompilerParams(vmem_limit_bytes=20 * MIB),
        cost_estimate=pl.CostEstimate(flops=200_000_000, bytes_accessed=40 * MIB, transcendentals=0),
        name="transposed_conv",
    )(*operands)


def run_finish(core, mine, other):
    vec = jax.ShapeDtypeStruct((1, C), F32)
    vmem = pl.BlockSpec(memory_space=pltpu.VMEM)
    return pl.pallas_call(
        finish_kernel,
        in_specs=[pl.BlockSpec(memory_space=pltpu.SMEM), vmem, vmem],
        out_shape=(
            jax.ShapeDtypeStruct((49, C), F32), vec, vec, vec, jax.ShapeDtypeStruct((C, HID), F32),
            jax.ShapeDtypeStruct((1, HID), F32), jax.ShapeDtypeStruct((HID, C), F32), vec, vec,
        ),
        scratch_shapes=(
            pltpu.VMEM((64, C), F32), pltpu.VMEM((C, HID), F32), pltpu.VMEM((HID, C), F32),
        ),
        compiler_params=pltpu.CompilerParams(vmem_limit_bytes=16 * MIB),
        name="clip",
    )(core, mine, other)


def pair_swaps(n):
    inner = [(i, i ^ 1) for i in range(n)]
    outer = [(i, i + 1 if i % 2 else i - 1) for i in range(1, n - 1)]
    return inner, outer


def halo(x, core, beside_columns=None, beside_rows=None):
    inner, outer = pair_swaps(lax.axis_size("wa"))
    even = lax.rem(lax.axis_index("wa"), 2) == 0
    first, last = x[:, : 3 * C], x[:, -3 * C :]
    near = lax.ppermute(jnp.where(even, last, first), "wa", inner)
    far = lax.ppermute(jnp.where(even, first, last), "wa", outer)
    if beside_columns is not None:
        near, far, _ = lax.optimization_barrier((near, far, beside_columns))
    left, right = jnp.where(even, far, near), jnp.where(even, near, far)
    inner, outer = pair_swaps(lax.axis_size("ha"))
    even = core[0] == 0
    last = jnp.concatenate([left[5:], x[5:], right[5:]], axis=1)
    lead = jnp.concatenate([left[:3], x[:3], right[:3]], axis=1)
    crossed = lax.ppermute(jnp.where(even, lead, last), "ha", outer)
    swapped = lax.ppermute(jnp.where(even, last, lead), "ha", inner)
    if beside_rows is not None:
        crossed, swapped, _ = lax.optimization_barrier((crossed, swapped, beside_rows))
    return left, right, jnp.concatenate([crossed, swapped], axis=0)


def plane_and_line():
    wide, pairs = lax.axis_size("wa"), lax.axis_size("ha") // 2
    depth = pairs // 2
    at = lambda x, z, c, w: ((x * depth + z) * 2 + c) * wide + w
    plane = [
        [at(x, z, c, w) for x in range(2) for w in range(wide)]
        for z in range(depth)
        for c in range(2)
    ]
    line = [
        [at(x, z, c, w) for z in range(depth)]
        for x in range(2)
        for w in range(wide)
        for c in range(2)
    ]
    return plane, line


def on_device(
    features, grad_out, dw_weight, dw_bias, ln_gain, ln_bias, w_in, b_in, w_out, b_out, scale
):
    row = lambda v: v.reshape(1, -1)
    core = lax.rem(lax.axis_index("ha"), 2).reshape(1).astype(jnp.int32)
    swap, _ = pair_swaps(lax.axis_size("ha"))
    plane, line = plane_and_line()

    def exchange(x, groups):
        return lax.all_to_all(x, ("ha", "wa"), 0, 0, axis_index_groups=groups, tiled=True)

    dconv, keep, send = run_main(
        core, features, *halo(features, core), grad_out, dw_weight, row(dw_bias), row(ln_gain),
        row(ln_bias), w_in, w_in.T, row(b_in), w_out.T, row(b_out), row(scale),
    )
    half = (keep.astype(F32) + lax.ppermute(send, "ha", swap).astype(F32)).astype(BF16)
    half, dconv = lax.optimization_barrier((half, dconv))
    add_up = lambda v: jnp.sum(v.astype(F32), axis=0).astype(BF16)
    repeat = lambda v, n: jnp.broadcast_to(v[None], (n,) + v.shape)
    terms = exchange(half, plane)
    sums = exchange(repeat(add_up(terms), len(line[0])), line)
    edges = halo(dconv, core, terms, sums)
    total = add_up(sums)
    total, edges = lax.optimization_barrier((total, edges))
    mine = exchange(repeat(total, len(plane[0])), plane)
    grad_features = run_transposed(core, dconv, *edges, grad_out, dw_weight[::-1])
    mine, grad_features = lax.optimization_barrier((mine, grad_features))
    other = lax.ppermute(mine, "ha", swap)
    o_dw, o_dwb, o_gain, o_lnb, o_win, o_bin, o_wout, o_bout, o_scale = run_finish(
        core, mine, other
    )
    flat = lambda v: v.reshape(-1)
    return (
        grad_features, o_dw, flat(o_dwb), flat(o_gain), flat(o_lnb), o_win, flat(o_bin), o_wout,
        flat(o_bout), flat(o_scale),
    )


def solution(mesh):
    return jax.shard_map(
        on_device,
        mesh=mesh,
        in_specs=(P("ha", "wa"), P("ha", "wa"), P(), P(), P(), P(), P(), P(), P(), P(), P()),
        out_specs=(P("ha", "wa"), P(), P(), P(), P(), P(), P(), P(), P(), P()),
        check_vma=False,
    )
```
